32 devices in a mesh: seq: 4 (over y, core), ctx: 8 (over z, x).
Axes of the slice: x: 2, y: 2, z: 4, core: 2. Of those that a mesh axis runs over, the one named last changes fastest.
Arguments:
- tokens: bfloat16 [4, 2048, 1152], P('seq', 'ctx'), may hold values from -6 to 6
- cotangent: bfloat16 [4, 2048, 1152], P('seq', 'ctx'), may hold values from -6 to 6
- segments: int32 [4, 2048], P('seq'), may hold values from 0 to 256, as said below
- positions: int32 [4, 2048], P('seq', 'ctx'), may hold values from 0 to 4094, as said below
- attn_w: float32 [2949120], P(('seq', 'ctx'))
- attn_m: float32 [2949120], P(('seq', 'ctx')), may hold values from -256 to 256
- attn_v: float32 [2949120], P(('seq', 'ctx')), may hold values from 1024 to 16384
- mlp_w: float32 [6912, 3456], P('ctx', 'seq')
- mlp_m: float32 [6912, 3456], P('ctx', 'seq'), may hold values from -256 to 256
- mlp_v: float32 [6912, 3456], P('ctx', 'seq'), may hold values from 1024 to 16384
- gains: float32 [5120], P(('seq', 'ctx')), may hold values from 0.6 to 2
- gain_m: float32 [5120], P(('seq', 'ctx')), may hold values from -512 to 512
- gain_v: float32 [5120], P(('seq', 'ctx')), may hold values from 4096 to 65536
Outputs:
- mixed: bfloat16 [4, 2048, 1152], P('seq', 'ctx')
- input_grad: bfloat16 [4, 2048, 1152], P('seq', 'ctx')
- attn_grad: float32 [2949120], P(('seq', 'ctx'))
- attn_m_new: float32 [2949120], P(('seq', 'ctx'))
- attn_v_new: float32 [2949120], P(('seq', 'ctx'))
- attn_new: float32 [2949120], P(('seq', 'ctx'))
- mlp_grad: float32 [6912, 3456], P('ctx', 'seq')
- mlp_m_new: float32 [6912, 3456], P('ctx', 'seq')
- mlp_v_new: float32 [6912, 3456], P('ctx', 'seq')
- mlp_new: float32 [6912, 3456], P('ctx', 'seq')
- gain_grad: float32 [5120], P(('seq', 'ctx'))
- gain_m_new: float32 [5120], P(('seq', 'ctx'))
- gain_v_new: float32 [5120], P(('seq', 'ctx'))
- gain_new: float32 [5120], P(('seq', 'ctx'))
The draws below stay inside these ranges and needn't reach their ends.
Inputs may be any that keep to these rules, and one draw needn't show every extreme that they name: `segments`: in each sequence document numbers start at 0 and never fall; one document covers at least the positions 128 to 1919. Within a document positions start at 0 and rise by 1 or 2 from one token to the next.
All inputs are finite; a program needn't handle non-finite values.
Results may differ from the reference program's by a relative error of at most 0.03.
The reference program's roundings to bfloat16 on the way count: a program that leaves them out, or rounds other values in their place, can miss the bound.
Values may be sent and summed in bfloat16 or wider, within the bound.
No kernel may reach another device: no remote copies, remote signals or barrier semaphores. Data moves between devices by JAX's collectives and lax.ppermute only.
A program may use at most 320 MiB of HBM per device.

```python
import math
import jax
import jax.numpy as jnp
from jax import lax

D = 1152
H = 4
HD = 256
FF = 6912
TOK_DEV = 256
STEP = 5
LEN = 2048
SEQS = 4
PA = 2949120
G = 5120


def layout(key):
    subkeys = jax.random.split(key, 5)
    half_tok = max(TOK_DEV // 2, 1)
    chosen = jax.random.randint(subkeys[4], (), 0, SEQS)
    seq_index = jnp.arange(SEQS, dtype=jnp.int32)[:, None]
    many_docs = seq_index == chosen
    single_doc = seq_index == (chosen + 1) % SEQS
    leading = jax.random.randint(subkeys[0], (SEQS, 1), 1, half_tok + 1)
    trailing = jax.random.randint(subkeys[1], (SEQS, 1), 1, half_tok + 1)
    leading = jnp.where(many_docs, half_tok, leading)
    trailing = jnp.where(many_docs, half_tok, trailing)
    token_index = jnp.arange(LEN, dtype=jnp.int32)[None, :]
    coin_flip = (jax.random.randint(subkeys[2], (SEQS, LEN), 0, 8) == 0) | many_docs
    border = (token_index < leading) | (token_index >= LEN - trailing)
    begins = (coin_flip & border | (token_index == leading) | (token_index == LEN - trailing)) & (token_index > 0)
    begins = begins & jnp.logical_not(single_doc)
    documents = jnp.cumsum(begins.astype(jnp.int32), axis=1)
    stride = jax.random.randint(subkeys[3], (SEQS, LEN), 1, 3)
    stride = jnp.where(single_doc, 2, stride)
    return (documents, begins | (token_index == 0), stride)


def draw_segments(key, part):
    documents, begins, stride = layout(key)
    return documents


def draw_positions(key, part):
    documents, begins, stride = layout(key)
    running = jnp.cumsum(stride, axis=1) - stride
    anchor = lax.cummax(jnp.where(begins, running, 0), axis=1)
    return running - anchor


def region_scale(total, split_at, first_fan, second_fan):
    entry_index = jnp.arange(total)
    return jnp.where(entry_index < split_at, first_fan ** (-0.5), second_fan ** (-0.5)).astype(jnp.float32)


def draw_attn_w(key, part):
    key = jax.random.fold_in(key, 11)
    base = jax.random.normal(key, (PA,), jnp.float32)
    return base * region_scale(PA, D * (H + 2) * HD, D, H * HD // 32)


def draw_mlp_w(key, part):
    key = jax.random.fold_in(key, 12)
    base = jax.random.normal(key, (FF, 3 * D), jnp.float32)
    return base * region_scale(3 * D, 2 * D, D, FF)[None, :]


def draw_gains(key, part):
    key = jax.random.fold_in(key, 13)
    spread = jax.random.uniform(key, (G,), jnp.float32)
    entry_index = jnp.arange(G)
    rotary_part = (entry_index >= D) & (entry_index < D + 2 * HD)
    drawn = 0.6 + 0.8 * spread
    rotary = jnp.exp(jnp.log(2.0) * spread)
    return jnp.where(rotary_part, rotary, drawn)


def steps_of(stream_key, extent, shards, least, top_value):
    def one(axis_at, shards_of):
        draws = jax.random.uniform(jax.random.fold_in(jax.random.fold_in(stream_key, 6), axis_at), (shards_of,), jnp.float32, least / len(shards), top_value / len(shards))
        return jnp.repeat(jnp.exp(draws), extent[axis_at] // shards_of).reshape((-1,) + (1,) * (len(extent) - axis_at - 1))

    loudness = one(*shards[0])
    for cut in shards[1:]:
        loudness = loudness * one(*cut)
    return loudness


def centred(stream_key, extent, width, bound, cuts=(), kind=jnp.bfloat16):
    drawn = width * jax.random.normal(stream_key, extent, jnp.float32)
    if cuts:
        drawn = drawn * steps_of(stream_key, extent, cuts, -0.22, 0.18)
    return jnp.clip(drawn, -bound, bound).astype(kind)


def setup_inputs(seed: int = 0) -> dict:
    key_list = jax.random.split(jax.random.key(seed), 14)
    tokens = centred(key_list[0], (SEQS, LEN, D), 1.0, 6.0, ((0, 4), (1, 8)))
    cotangent = centred(key_list[1], (SEQS, LEN, D), 1.0, 6.0, ((0, 4), (1, 8)))
    segments = draw_segments(jax.random.fold_in(key_list[13], 71), 0)
    positions = draw_positions(jax.random.fold_in(key_list[13], 71), 0)
    attn_w = draw_attn_w(jax.random.fold_in(key_list[13], 71), 0)
    attn_m = centred(key_list[5], (PA,), (0.5 * (SEQS * LEN) ** 0.5), 256.0, ((0, 32),), jnp.float32)
    attn_v = jnp.clip(jnp.exp(math.log(16384.0) - 2.7725887 * jax.random.uniform(key_list[6], (PA,), jnp.float32) ** steps_of(key_list[6], (PA,), ((0, 32),), -0.2, 0.2)), 1024.0, 16384.0)
    mlp_w = draw_mlp_w(jax.random.fold_in(key_list[13], 71), 0)
    mlp_m = centred(key_list[8], (FF, 3 * D), (0.5 * (SEQS * LEN) ** 0.5), 256.0, ((0, 8), (1, 4)), jnp.float32)
    mlp_v = jnp.clip(jnp.exp(math.log(16384.0) - 2.7725887 * jax.random.uniform(key_list[9], (FF, 3 * D), jnp.float32) ** steps_of(key_list[9], (FF, 3 * D), ((0, 8), (1, 4)), -0.2, 0.2)), 1024.0, 16384.0)
    gains = draw_gains(jax.random.fold_in(key_list[13], 71), 0)
    gain_m = centred(key_list[11], (G,), ((SEQS * LEN) ** 0.5), 512.0, ((0, 32),), jnp.float32)
    gain_v = jnp.clip(jnp.exp(math.log(65536.0) - 2.7725887 * jax.random.uniform(key_list[12], (G,), jnp.float32) ** steps_of(key_list[12], (G,), ((0, 32),), -0.2, 0.2)), 4096.0, 65536.0)
    return {"tokens": tokens, "cotangent": cotangent, "segments": segments, "positions": positions, "attn_w": attn_w, "attn_m": attn_m, "attn_v": attn_v, "mlp_w": mlp_w, "mlp_m": mlp_m, "mlp_v": mlp_v, "gains": gains, "gain_m": gain_m, "gain_v": gain_v}


NORM_EPS = 1e-06
SCORE_FLOOR = -1e+30
ROPE_BASE = 1000000.0
BETA_MOMENT = 0.5
ADAM_EPS = 1e-08
RATE_MATRIX = 0.03
RATE_GAIN = 0.5
DECAY_MATRIX = 0.1
HIGHEST = lax.Precision.HIGHEST

@jax.custom_vjp
def low(v):
    return lax.optimization_barrier(v.astype(jnp.bfloat16)).astype(jnp.float32)

@jax.custom_vjp
def low_back(v):
    return v

def low_keep(v):
    return (low(v), None)

def low_pass(kept, grad):
    return (grad,)

def back_keep(v):
    return (v, None)

def back_low(kept, grad):
    return (low(grad),)
low.defvjp(low_keep, low_pass)
low_back.defvjp(back_keep, back_low)

def normed_ref(value):
    return value * lax.rsqrt(lax.optimization_barrier(jnp.mean(value * value, axis=-1, keepdims=True)) + NORM_EPS)

def angles(position):
    half_index = jnp.arange(HD // 2, dtype=jnp.float32)
    frequency = jnp.exp(half_index * (-2.0 * jnp.log(ROPE_BASE) / HD))
    angle = position.astype(jnp.float32)[:, None] * frequency[None, :]
    return (jnp.cos(angle), jnp.sin(angle))

def rotate(value, cosine, sine):
    half_width = value.shape[-1] // 2
    first_half = value[..., :half_width]
    second_half = value[..., half_width:]
    return jnp.concatenate([first_half * cosine - second_half * sine, second_half * cosine + first_half * sine], axis=-1)

def attend(query, key_rows, value_rows, documents):
    length = documents.shape[0]
    block_rows = min(512, length)
    block_count = length // block_rows
    token_index = jnp.arange(length, dtype=jnp.int32)

    def query_block(pieces):
        query_part, doc_part, index_part = pieces
        scores = jnp.einsum('qhd,kd->qhk', query_part, key_rows, precision=HIGHEST) * HD ** (-0.5)
        scores = low_back(scores)
        allowed = (doc_part[:, None] == documents[None, :]) & (index_part[:, None] >= token_index[None, :])
        allowed = allowed[:, None, :]
        masked = jnp.where(allowed, scores, SCORE_FLOOR)
        row_max = lax.optimization_barrier(jnp.max(masked, axis=-1, keepdims=True))
        exponent = jnp.where(allowed, jnp.exp(masked - row_max), 0.0)
        probs = low(exponent / lax.optimization_barrier(jnp.sum(exponent, axis=-1, keepdims=True)))
        return jnp.einsum('qhk,kd->qhd', probs, value_rows, precision=HIGHEST)
    blocks = lax.map(jax.checkpoint(query_block), (query.reshape(block_count, block_rows, H, HD), documents.reshape(block_count, block_rows), token_index.reshape(block_count, block_rows)))
    return blocks.reshape(length, H, HD)

def layer_forward(hidden_in, flat_attn, mlp_rows, gain_all, documents, position):
    qkv_width = (H + 2) * HD
    w_qkv = flat_attn[:D * qkv_width].reshape(D, qkv_width)
    w_out = flat_attn[D * qkv_width:].reshape(H * HD, D)
    w_gate = mlp_rows[:, :D].T
    w_up = mlp_rows[:, D:2 * D].T
    w_down = mlp_rows[:, 2 * D:]
    gain_pre = gain_all[:D]
    gain_q = gain_all[D:D + HD]
    gain_k = gain_all[D + HD:D + 2 * HD]
    gain_post = gain_all[D + 2 * HD:2 * D + 2 * HD]
    gain_fpre = gain_all[2 * D + 2 * HD:3 * D + 2 * HD]
    gain_fpost = gain_all[3 * D + 2 * HD:]
    length = hidden_in.shape[0]
    normed_in = low(normed_ref(hidden_in) * gain_pre)
    qkv = low_back(jnp.dot(normed_in, w_qkv, precision=HIGHEST, preferred_element_type=jnp.float32))
    cosine, sine = angles(position)
    query = low(rotate(normed_ref(qkv[:, :H * HD].reshape(length, H, HD)) * gain_q, cosine[:, None, :], sine[:, None, :]))
    key_rows = low(rotate(normed_ref(qkv[:, H * HD:(H + 1) * HD]) * gain_k, cosine, sine))
    value_rows = low(qkv[:, (H + 1) * HD:])
    heads_out = attend(query, key_rows, value_rows, documents).reshape(length, H * HD)
    heads_out = low_back(low(heads_out))
    attn_out = low_back(jnp.dot(heads_out, w_out, precision=HIGHEST, preferred_element_type=jnp.float32))
    middle = hidden_in + normed_ref(attn_out) * gain_post
    ffn_in = low(normed_ref(middle) * gain_fpre)
    gate = low_back(jnp.dot(ffn_in, w_gate, precision=HIGHEST, preferred_element_type=jnp.float32))
    up_part = low_back(jnp.dot(ffn_in, w_up, precision=HIGHEST, preferred_element_type=jnp.float32))
    activated = low(jax.nn.gelu(gate, approximate=True) * up_part)
    mlp_out = low_back(jnp.dot(activated, w_down, precision=HIGHEST, preferred_element_type=jnp.float32))
    return middle + normed_ref(mlp_out) * gain_fpost

def adam_update(weight, moment_one, second, gradient, learn_rate, decay_rate):
    moment_new = BETA_MOMENT * moment_one + (1.0 - BETA_MOMENT) * gradient
    second_new = BETA_MOMENT * second + (1.0 - BETA_MOMENT) * gradient * gradient
    correction = 1.0 - BETA_MOMENT ** STEP
    update = moment_new / correction / (jnp.sqrt(second_new / correction) + ADAM_EPS)
    return (moment_new, second_new, weight - learn_rate * (update + decay_rate * weight))

def reference(tokens, cotangent, segments, positions, attn_w, attn_m, attn_v, mlp_w, mlp_m, mlp_v, gains, gain_m, gain_v):
    low_attn = low(attn_w)
    low_mlp = low(mlp_w)
    low_gain = low(gains)

    def per_sequence(totals, inputs):
        seq_tokens, seq_cot, seq_docs, seq_pos = inputs

        def closed(hidden_in, flat_attn, mlp_rows, gain_all):
            return layer_forward(hidden_in, flat_attn, mlp_rows, gain_all, seq_docs, seq_pos)
        output, pullback = jax.vjp(closed, seq_tokens.astype(jnp.float32), low_attn, low_mlp, low_gain)
        d_input, d_attn, d_mlp, d_gain = pullback(seq_cot.astype(jnp.float32))
        summed = (totals[0] + d_attn, totals[1] + d_mlp, totals[2] + d_gain)
        return (summed, (output.astype(jnp.bfloat16), d_input.astype(jnp.bfloat16)))
    start_totals = (jnp.zeros(attn_w.shape, jnp.float32), jnp.zeros(mlp_w.shape, jnp.float32), jnp.zeros(gains.shape, jnp.float32))
    (attn_grad, mlp_grad, gain_grad), (mixed, input_grad) = lax.scan(per_sequence, start_totals, (tokens, cotangent, segments, positions))
    attn_m_new, attn_v_new, attn_new = adam_update(attn_w, attn_m, attn_v, attn_grad, RATE_MATRIX, DECAY_MATRIX)
    mlp_m_new, mlp_v_new, mlp_new = adam_update(mlp_w, mlp_m, mlp_v, mlp_grad, RATE_MATRIX, DECAY_MATRIX)
    gain_m_new, gain_v_new, gain_new = adam_update(gains, gain_m, gain_v, gain_grad, RATE_GAIN, 0.0)
    return (mixed, input_grad, attn_grad, attn_m_new, attn_v_new, attn_new, mlp_grad, mlp_m_new, mlp_v_new, mlp_new, gain_grad, gain_m_new, gain_v_new, gain_new)
```

```python
import jax
import jax.numpy as jnp
import numpy as np
from jax import lax
from jax.experimental import pallas as pl
from jax.experimental.pallas import tpu as pltpu
from jax.sharding import Mesh, PartitionSpec as P

D = 1152
H = 4
HD = 256
STEP = 5

NORM_EPS = 1e-06
SCORE_FLOOR = -1e30
ROPE_BASE = 1000000.0
BETA_MOMENT = 0.5
ADAM_EPS = 1e-08
RATE_MATRIX = 0.03
RATE_GAIN = 0.5
DECAY_MATRIX = 0.1

bf16 = jnp.bfloat16
f32 = jnp.float32
LANES = 128


def normed(value):
    factor = lax.rsqrt(jnp.mean(value * value, axis=-1, keepdims=True) + NORM_EPS)
    return (value * factor, factor)


def norm_back(unit, factor, d_unit):
    return factor * (d_unit - unit * jnp.mean(d_unit * unit, axis=-1, keepdims=True))


def angles(position):
    half_index = jnp.arange(HD // 2, dtype=f32)
    frequency = jnp.exp(half_index * (-2.0 * jnp.log(ROPE_BASE) / HD))
    angle = position.astype(f32)[:, None] * frequency[None, :]
    return (jnp.cos(angle), jnp.sin(angle))


def rotate(value, cosine, sine):
    half_width = value.shape[-1] // 2
    first_half = value[..., :half_width]
    second_half = value[..., half_width:]
    return jnp.concatenate(
        [first_half * cosine - second_half * sine, second_half * cosine + first_half * sine],
        axis=-1,
    )


def contract(left, right, left_dim, right_dim):
    return lax.dot_general(
        left, right, (((left_dim,), (right_dim,)), ((), ())), preferred_element_type=f32
    )


def adam_update(weight, moment_one, second, gradient, learn_rate, decay_rate):
    moment_new = BETA_MOMENT * moment_one + (1.0 - BETA_MOMENT) * gradient
    second_new = BETA_MOMENT * second + (1.0 - BETA_MOMENT) * gradient * gradient
    correction = 1.0 - BETA_MOMENT**STEP
    update = moment_new / correction / (jnp.sqrt(second_new / correction) + ADAM_EPS)
    return (moment_new, second_new, weight - learn_rate * (update + decay_rate * weight))


def add_low(*parts):
    total = parts[0].astype(f32)
    for part in parts[1:]:
        total = total + part.astype(f32)
    return total.astype(bf16)


def after(value, *earlier):
    return lax.optimization_barrier((value,) + earlier)[0]


def halfway(rows):
    return rows // 32 * 16 if rows >= 32 else rows // 2


VMEM_LIMIT = 56 * 1024 * 1024


def spread_rows(parts, order, lines, q_rows, q_width, o_rows, o_width):
    count = sum(part.shape[0] for part in parts)
    padded = parts[0].shape[1]
    gain_at = -(-lines // 16) * 16
    q_across, o_across = q_width // LANES, o_width // LANES
    total = count * lines

    def body(order_ref, *refs):
        sources = refs[: len(parts)]
        q_ref, o_ref, gain_ref, held, flat, sems = refs[len(parts) :]
        copies = []
        for part, source in zip(parts, sources):
            for i in range(part.shape[0]):
                k = len(copies)
                copies.append(
                    pltpu.make_async_copy(source.at[i], held.at[order_ref[k]], sems.at[k])
                )
        for copy in copies:
            copy.start()
        for copy in copies:
            copy.wait()
        for i in range(count):
            flat[i * lines : (i + 1) * lines, :] = held[i, :gain_at, :].astype(f32)[:lines]
            gain_ref[i] = held[i, gain_at:, :].astype(f32)
        for j in range(q_across):
            q_ref[:, j * LANES : (j + 1) * LANES] = flat[
                pl.ds(j, q_rows, stride=q_across), :
            ].astype(bf16)
        for j in range(o_across):
            o_ref[:, j * LANES : (j + 1) * LANES] = flat[
                pl.ds(q_rows * q_across + j, o_rows, stride=o_across), :
            ].astype(bf16)

    return pl.pallas_call(
        body,
        out_shape=(
            jax.ShapeDtypeStruct((q_rows, q_width), bf16),
            jax.ShapeDtypeStruct((o_rows, o_width), bf16),
            jax.ShapeDtypeStruct((count, padded - gain_at, LANES), f32),
        ),
        in_specs=[pl.BlockSpec(memory_space=pltpu.SMEM)]
        + [pl.BlockSpec(memory_space=pl.ANY)] * len(parts),
        out_specs=[pl.BlockSpec(memory_space=pltpu.VMEM)] * 3,
        scratch_shapes=[
            pltpu.VMEM((count, padded, LANES), bf16),
            pltpu.VMEM((total, LANES), f32),
            pltpu.SemaphoreType.DMA((count,)),
        ],
        compiler_params=pltpu.CompilerParams(vmem_limit_bytes=VMEM_LIMIT),
        cost_estimate=pl.CostEstimate(flops=0, bytes_accessed=24 * total * LANES, transcendentals=0),
        name="spread_rows",
    )(order, *parts)


def pack_rows(d_wqkv, d_wout, gain_lines, place, lines):
    count, gain_rows, _ = gain_lines.shape
    q_rows, q_width = d_wqkv.shape
    o_rows, o_width = d_wout.shape
    gain_at = -(-lines // 16) * 16
    q_across, o_across = q_width // LANES, o_width // LANES
    total = count * lines

    def body(place_ref, q_ref, o_ref, gain_ref, out_ref, flat):
        flat[total:, :] = jnp.zeros((flat.shape[0] - total, LANES), f32)
        for j in range(q_across):
            flat[pl.ds(j, q_rows, stride=q_across), :] = q_ref[:, j * LANES : (j + 1) * LANES]
        for j in range(o_across):
            flat[pl.ds(q_rows * q_across + j, o_rows, stride=o_across), :] = o_ref[
                :, j * LANES : (j + 1) * LANES
            ]
        for i in range(count):
            out_ref[place_ref[i], :gain_at, :] = flat[i * lines : i * lines + gain_at, :].astype(bf16)
            out_ref[place_ref[i], gain_at:, :] = gain_ref[i].astype(bf16)

    return pl.pallas_call(
        body,
        out_shape=jax.ShapeDtypeStruct((count, gain_at + gain_rows, LANES), bf16),
        in_specs=[pl.BlockSpec(memory_space=pltpu.SMEM)]
        + [pl.BlockSpec(memory_space=pltpu.VMEM)] * 3,
        out_specs=pl.BlockSpec(memory_space=pltpu.VMEM),
        scratch_shapes=[pltpu.VMEM((total + 16, LANES), f32)],
        compiler_params=pltpu.CompilerParams(vmem_limit_bytes=VMEM_LIMIT),
        cost_estimate=pl.CostEstimate(flops=0, bytes_accessed=24 * total * LANES, transcendentals=0),
        name="pack_rows",
    )(place, d_wqkv, d_wout, gain_lines)


DEAD, WHOLE, MASKED = 0, 1, 2


def allowed_of(kdoc_ref, qdoc_ref, shift):
    keys, queries = kdoc_ref.shape[0], qdoc_ref.shape[1]
    key_at = lax.broadcasted_iota(jnp.int32, (keys, queries), 0) + shift
    query_at = lax.broadcasted_iota(jnp.int32, (keys, queries), 1)
    return (kdoc_ref[...] == qdoc_ref[...]) & (key_at <= query_at)


def attend(info, query, kv, key_docs, query_docs):
    blocks, rows, _ = kv.shape

    def body(info_ref, q_ref, kv_ref, kdoc_ref, qdoc_ref, o_ref, lse_ref, peak, total, acc):
        step = pl.program_id(0)

        @pl.when(step == 0)
        def _():
            peak[...] = jnp.full_like(peak, SCORE_FLOOR)
            total[...] = jnp.zeros_like(total)
            acc[...] = jnp.zeros_like(acc)

        def visit(masked):
            key = kv_ref[0, :, :HD]
            value_t = kv_ref[0, :, HD:].T
            if masked:
                allowed = allowed_of(
                    kdoc_ref, qdoc_ref, (info_ref[0, step] - info_ref[0, 0]) * rows
                )
            for h in range(H):
                score = contract(key, q_ref[:, h * HD : (h + 1) * HD], 1, 1)
                if masked:
                    score = jnp.where(allowed, score, SCORE_FLOOR)
                old = peak[h : h + 1, :]
                new = jnp.maximum(old, jnp.max(score, axis=0, keepdims=True))
                weight = jnp.exp(score - new)
                shrink = jnp.exp(old - new)
                peak[h : h + 1, :] = new
                total[h : h + 1, :] = total[h : h + 1, :] * shrink + jnp.sum(
                    weight, axis=0, keepdims=True
                )
                acc[h] = acc[h] * shrink + contract(value_t, weight.astype(bf16), 1, 0)

        pl.when(info_ref[1, step] == WHOLE)(lambda: visit(False))
        pl.when(info_ref[1, step] == MASKED)(lambda: visit(True))

        @pl.when(step == blocks - 1)
        def _():
            lse_ref[...] = jnp.zeros_like(lse_ref)
            for h in range(H):
                lse_ref[h : h + 1, :] = peak[h : h + 1, :] + jnp.log(total[h : h + 1, :])
                o_ref[:, h * HD : (h + 1) * HD] = (acc[h] / total[h : h + 1, :]).T.astype(bf16)

    return pl.pallas_call(
        body,
        grid_spec=pltpu.PrefetchScalarGridSpec(
            num_scalar_prefetch=1,
            grid=(blocks,),
            in_specs=[
                pl.BlockSpec((rows, H * HD), lambda i, info: (0, 0)),
                pl.BlockSpec((1, rows, 2 * HD), lambda i, info: (i, 0, 0)),
                pl.BlockSpec((rows, 1), lambda i, info: (info[0, i], 0)),
                pl.BlockSpec((1, rows), lambda i, info: (0, 0)),
            ],
            out_specs=[
                pl.BlockSpec((rows, H * HD), lambda i, info: (0, 0)),
                pl.BlockSpec((8, rows), lambda i, info: (0, 0)),
            ],
            scratch_shapes=[
                pltpu.VMEM((8, rows), f32),
                pltpu.VMEM((8, rows), f32),
                pltpu.VMEM((H, HD, rows), f32),
            ],
        ),
        out_shape=(
            jax.ShapeDtypeStruct((rows, H * HD), bf16),
            jax.ShapeDtypeStruct((8, rows), f32),
        ),
        compiler_params=pltpu.CompilerParams(vmem_limit_bytes=VMEM_LIMIT),
        cost_estimate=pl.CostEstimate(
            flops=4 * blocks * rows * rows * H * HD,
            bytes_accessed=2 * kv.size,
            transcendentals=blocks * rows * rows * H,
        ),
        name="attend",
    )(info, query, kv, key_docs, query_docs)


def attend_back(info, query, kv, key_docs, query_docs, d_heads, log_total, delta):
    blocks, rows, _ = kv.shape

    def body(
        info_ref, q_ref, kv_ref, kdoc_ref, qdoc_ref, do_ref, lse_ref, delta_ref, dq_ref, dkv_ref
    ):
        step = pl.program_id(0)

        @pl.when(step == 0)
        def _():
            dq_ref[...] = jnp.zeros_like(dq_ref)

        def visit(masked):
            key, value = kv_ref[0, :, :HD], kv_ref[0, :, HD:]
            if masked:
                allowed = allowed_of(
                    kdoc_ref, qdoc_ref, (info_ref[0, step] - info_ref[0, 0]) * rows
                )
            d_key = jnp.zeros((rows, HD), f32)
            d_value = jnp.zeros((rows, HD), f32)
            for h in range(H):
                cols = slice(h * HD, (h + 1) * HD)
                q, d_o = q_ref[:, cols], do_ref[:, cols]
                prob = jnp.exp(contract(key, q, 1, 1) - lse_ref[h : h + 1, :])
                if masked:
                    prob = jnp.where(allowed, prob, 0.0)
                d_value = d_value + contract(prob.astype(bf16), d_o, 1, 0)
                d_prob = contract(value, d_o, 1, 1)
                d_score = (prob * (d_prob - delta_ref[h : h + 1, :])).astype(bf16)
                d_key = d_key + contract(d_score, q, 1, 0)
                dq_ref[:, cols] = dq_ref[:, cols] + contract(d_score, key, 0, 0)
            dkv_ref[0, :, :HD] = d_key.astype(bf16)
            dkv_ref[0, :, HD:] = d_value.astype(bf16)

        pl.when(info_ref[1, step] == WHOLE)(lambda: visit(False))
        pl.when(info_ref[1, step] == MASKED)(lambda: visit(True))

        @pl.when(info_ref[1, step] == DEAD)
        def _():
            dkv_ref[...] = jnp.zeros_like(dkv_ref)

        @pl.when(step == blocks - 1)
        def _():
            dq_ref[...] = dq_ref[...] * HD ** (-0.5)

    whole = pl.BlockSpec((rows, H * HD), lambda i, info: (0, 0))
    stats = pl.BlockSpec((8, rows), lambda i, info: (0, 0))
    block = pl.BlockSpec((1, rows, 2 * HD), lambda i, info: (i, 0, 0))
    return pl.pallas_call(
        body,
        grid_spec=pltpu.PrefetchScalarGridSpec(
            num_scalar_prefetch=1,
            grid=(blocks,),
            in_specs=[
                whole,
                block,
                pl.BlockSpec((rows, 1), lambda i, info: (info[0, i], 0)),
                pl.BlockSpec((1, rows), lambda i, info: (0, 0)),
                whole,
                stats,
                stats,
            ],
            out_specs=[whole, block],
        ),
        out_shape=(
            jax.ShapeDtypeStruct((rows, H * HD), f32),
            jax.ShapeDtypeStruct(kv.shape, bf16),
        ),
        compiler_params=pltpu.CompilerParams(vmem_limit_bytes=VMEM_LIMIT),
        cost_estimate=pl.CostEstimate(
            flops=10 * blocks * rows * rows * H * HD,
            bytes_accessed=4 * kv.size,
            transcendentals=blocks * rows * rows * H,
        ),
        name="attend_back",
    )(info, query, kv, key_docs, query_docs, d_heads, log_total, delta)


class Ways:
    def __init__(self, sizes):
        self.sizes = sizes

    def size(self, axis):
        if isinstance(axis, str):
            return self.sizes[axis]
        n = 1
        for a in axis:
            n *= self.sizes[a]
        return n

    def fro(self, value, axis, offset):
        n = self.size(axis)
        if offset % n == 0:
            return value
        return lax.ppermute(value, axis, [((i + offset) % n, i) for i in range(n)])

    def places(self):
        nx, ny = self.sizes["x"], self.sizes["y"]
        return [(ox, oy) for ox in range(nx) for oy in range(ny)]

    def outers(self):
        return [(ou, ov) for ou in range(self.sizes["u"]) for ov in range(self.sizes["v"])]

    def plane_gather(self, value):
        nx, ny = self.sizes["x"], self.sizes["y"]
        half = halfway(value.shape[0])
        found = {(0, 0): value}
        for ox in range(1, nx):
            found[ox, 0] = self.fro(value, "x", ox)
        for oy in range(1, ny):
            found[0, oy] = self.fro(value, "y", oy)
        for ox in range(1, nx):
            for oy in range(1, ny):
                first = self.fro(found[ox, 0][:half], "y", oy)
                second = self.fro(found[0, oy][half:], "x", ox)
                found[ox, oy] = jnp.concatenate([first, second], axis=0)
        return {at: [block, self.fro(block, "c", 1)] for at, block in found.items()}

    def plane_scatter(self, parts):
        nx, ny = self.sizes["x"], self.sizes["y"]
        low = {
            at: add_low(parts[at][0], self.fro(parts[at][1], "c", 1))
            for at in sorted(parts, reverse=True)
        }
        half = halfway(low[0, 0].shape[0])
        along_x = {ox: [low[ox, 0][:half]] for ox in range(1, nx)}
        along_y = {oy: [low[0, oy][half:]] for oy in range(1, ny)}
        for ox in range(1, nx):
            for oy in range(1, ny):
                along_x[ox].append(self.fro(low[ox, oy][:half], "y", -oy))
                along_y[oy].append(self.fro(low[ox, oy][half:], "x", -ox))
        total = low[0, 0].astype(f32)
        for ox in range(1, nx):
            whole = jnp.concatenate([add_low(*along_x[ox]), low[ox, 0][half:]], axis=0)
            total = total + self.fro(whole, "x", -ox).astype(f32)
        for oy in range(1, ny):
            whole = jnp.concatenate([low[0, oy][:half], add_low(*along_y[oy])], axis=0)
            total = total + self.fro(whole, "y", -oy).astype(f32)
        return total

    def z_gather(self, value, cut=None, later=()):
        n = self.sizes["z"]
        if n != 4:
            return [self.fro(value, "z", oz) for oz in range(n)]
        above, below = self.fro(value, "z", 1), self.fro(value, "z", -1)
        if cut is None:
            half = halfway(value.shape[0])
            near = above[:half], below[half:]
        else:
            near = above[:, :cut], below[:, cut:]
        if later:
            near = lax.optimization_barrier(near + tuple(later))[:2]
        first, second = self.fro(near[0], "z", 1), self.fro(near[1], "z", -1)
        return [value, above, jnp.concatenate([first, second], axis=0 if cut is None else 1), below]

    def z_scatter_begin(self, parts):
        if self.sizes["z"] != 4:
            return ()
        half = halfway(parts[0].shape[0])
        return self.fro(parts[2][:half], "z", -1), self.fro(parts[2][half:], "z", 1)

    def z_scatter_go(self, parts, begun):
        n = self.sizes["z"]
        if n != 4:
            return [self.fro(parts[oz], "z", -oz) for oz in range(1, n)]
        half = halfway(parts[0].shape[0])
        above = jnp.concatenate([add_low(parts[1][:half], begun[0]), parts[1][half:]], axis=0)
        below = jnp.concatenate([parts[3][:half], add_low(parts[3][half:], begun[1])], axis=0)
        return [self.fro(above, "z", -1), self.fro(below, "z", 1)]

    def z_scatter(self, parts):
        total = parts[0].astype(f32)
        for heard in self.z_scatter_go(parts, self.z_scatter_begin(parts)):
            total = total + heard.astype(f32)
        return total


def gelu_parts(gate):
    scale = 0.7978845608028654
    square = gate * gate
    inner = jnp.tanh(scale * gate * (1.0 + 0.044715 * square))
    half_up = 0.5 * (1.0 + inner)
    slope = half_up + 0.5 * gate * (1.0 - inner * inner) * scale * (1.0 + 3 * 0.044715 * square)
    return gate * half_up, slope


SEQ = ("u", "y", "c")
CTX = ("z", "v", "x")
ACROSS = ("v", "x")


def make_shards(sizes):
    ways = Ways(sizes)
    ns, nctx, nx = ways.size(SEQ), ways.size(CTX), ways.size(ACROSS)
    nz = sizes["z"]
    devices = ns * nctx
    places, outers = ways.places(), ways.outers()

    def shards(
        tokens, cotangent, segments, positions, attn_w, attn_m, attn_v,
        mlp_w, mlp_m, mlp_v, gains, gain_m, gain_v,
    ):
        at = {a: lax.axis_index(a) for a in sizes}
        seq_place = lax.axis_index(SEQ)
        across_place = lax.axis_index(ACROSS)
        ctx_place = at["z"] * nx + across_place
        piece, gain_piece = attn_w.shape[0], gains.shape[0]
        lines = piece // LANES
        gain_at = -(-lines // 16) * 16
        gain_rows = -(-gain_piece // (16 * LANES)) * 16
        qkv_width = (H + 2) * HD

        sides = [sizes[a] for a in ("x", "y", "c", "u", "v", "z")]
        here = [at[a] for a in ("x", "y", "c", "u", "v", "z")]
        ox, oy, oc, ou, ov, oz = (
            (jnp.asarray(o, jnp.int32) + h) % n
            for o, h, n in zip(np.unravel_index(np.arange(devices), sides), here, sides)
        )
        order = ((ou * sizes["y"] + oy) * sizes["c"] + oc) * nz + oz
        order = (order * sizes["v"] + ov) * sizes["x"] + ox
        by_axis = dict(zip(SEQ + CTX, np.unravel_index(np.arange(devices), [sizes[a] for a in SEQ + CTX])))
        place_of = jnp.zeros((devices,), jnp.int32)
        for a, h, n in zip(("x", "y", "c", "u", "v", "z"), here, sides):
            place_of = place_of * n + (jnp.asarray(by_axis[a], jnp.int32) + (n - h)) % n

        def gain_lines_of(value):
            value = value.reshape(-1, gain_piece)
            value = jnp.pad(value, ((0, 0), (0, gain_rows * LANES - gain_piece)))
            return value.reshape(-1, gain_rows, LANES)

        low_piece = jnp.concatenate(
            [
                jnp.pad(attn_w.reshape(lines, LANES), ((0, gain_at - lines), (0, 0))),
                gain_lines_of(gains)[0],
            ],
            axis=0,
        ).astype(bf16)
        line_z = jnp.concatenate(ways.z_gather(low_piece), axis=0)
        line_z = jnp.concatenate(
            [ways.fro(ways.fro(line_z, "u", ou), "v", ov) for ou, ov in outers], axis=0
        )
        gathered = ways.plane_gather(line_z)
        line_parts = [part for p in places for part in gathered[p]]
        w_qkv, w_out, gain_lines = spread_rows(
            [part.reshape(-1, gain_at + gain_rows, LANES) for part in line_parts],
            order, lines, D, qkv_width, H * HD, D,
        )
        gain_all = gain_lines.reshape(devices, -1)[:, :gain_piece].reshape(-1)
        gain_pre = gain_all[:D]
        gain_q = gain_all[D : D + HD]
        gain_k = gain_all[D + HD : D + 2 * HD]
        gain_post = gain_all[D + 2 * HD : 2 * D + 2 * HD]
        gain_fpre = gain_all[2 * D + 2 * HD : 3 * D + 2 * HD]
        gain_fpost = gain_all[3 * D + 2 * HD :]

        units, width = mlp_w.shape
        share = units // ns
        held = -(-share // 32) * 32

        def seq_exchange(by_place):
            kept = jnp.zeros_like(by_place)
            for offset in range(ns):
                sent = lax.dynamic_index_in_dim(by_place, (seq_place - offset) % ns, 0, keepdims=False)
                heard = ways.fro(sent, SEQ, offset)
                kept = lax.dynamic_update_index_in_dim(kept, heard, (seq_place + offset) % ns, 0)
            return kept

        by_cols = seq_exchange(mlp_w.astype(bf16).reshape(ns, share, width))
        rows_own = jnp.concatenate([by_cols[i] for i in range(ns)], axis=1)
        rows_own = jnp.pad(rows_own, ((0, held - share), (0, 0)))

        tok_rows = tokens.shape[1]
        hidden_in = tokens[0].astype(f32)
        unit_in, scale_in = normed(hidden_in)
        normed_in = (unit_in * gain_pre).astype(bf16)
        qkv = jnp.dot(normed_in, w_qkv, preferred_element_type=f32)
        head_cols = [slice(h * HD, (h + 1) * HD) for h in range(H)]
        normed_q = [normed(qkv[:, cols]) for cols in head_cols]
        unit_k, scale_k = normed(qkv[:, H * HD : (H + 1) * HD])
        cosine, sine = angles(positions[0])
        query = jnp.concatenate(
            [rotate(unit * gain_q, cosine, sine).astype(bf16) for unit, _ in normed_q], axis=1
        ) * jnp.asarray(HD ** (-0.5), bf16)
        key_local = rotate(unit_k * gain_k, cosine, sine).astype(bf16)
        value_local = qkv[:, (H + 1) * HD :].astype(bf16)
        kv_local = jnp.concatenate([key_local, value_local], axis=1)
        kv_all = jnp.stack(
            [ways.fro(block, ACROSS, oa) for block in ways.z_gather(kv_local) for oa in range(nx)]
        )

        def all_units(blocks):
            whole = jnp.concatenate(blocks, axis=0)
            return jnp.concatenate(
                [ways.fro(ways.fro(whole, "u", ou), "v", ov) for ou, ov in outers], axis=0
            )

        gate_up = ways.z_gather(rows_own[:, : 2 * D], cut=D, later=(kv_all,))
        w_gate = all_units([block[:, :D] for block in gate_up])
        w_up = all_units([block[:, D:] for block in gate_up])

        doc_all = segments[0]
        first_docs, last_docs = doc_all[::tok_rows], doc_all[tok_rows - 1 :: tok_rows]
        key_at = np.arange(nctx)
        key_place = (at["z"] + jnp.asarray(key_at // nx, jnp.int32)) % nz * nx
        key_place = key_place + (across_place + jnp.asarray(key_at % nx, jnp.int32)) % nx
        is_place = key_place[:, None] == jnp.arange(nctx, dtype=jnp.int32)[None, :]
        key_first = jnp.sum(jnp.where(is_place, first_docs[None, :], 0), axis=1)
        key_last = jnp.sum(jnp.where(is_place, last_docs[None, :], 0), axis=1)
        live = (key_place < ctx_place) & (key_last >= key_first[0])
        same = key_first == key_last[0]
        task = jnp.where(live, jnp.where(same, WHOLE, MASKED), DEAD)
        task = jnp.where(key_place == ctx_place, MASKED, task)
        info = jnp.stack([key_place, task]).astype(jnp.int32)
        key_docs = doc_all[:, None]
        query_docs = lax.dynamic_slice_in_dim(doc_all, ctx_place * tok_rows, tok_rows)[None]

        heads_flat, log_total = attend(info, query, kv_all, key_docs, query_docs)
        w_down = all_units(ways.z_gather(after(rows_own[:, 2 * D :], heads_flat)))
        attn_out = jnp.dot(heads_flat, w_out, preferred_element_type=f32)
        unit_post, scale_post = normed(attn_out)
        middle = hidden_in + unit_post * gain_post
        unit_mid, scale_mid = normed(middle)
        ffn_in = (unit_mid * gain_fpre).astype(bf16)

        ffn_rows = {p: jnp.concatenate(b, axis=0) for p, b in ways.plane_gather(ffn_in).items()}
        act_low, gelu_low, slope_low, partial = {}, {}, {}, {}
        for p in places:
            gate = contract(ffn_rows[p], w_gate, 1, 1)
            up_part = contract(ffn_rows[p], w_up, 1, 1)
            gelu, slope = gelu_parts(gate)
            act_low[p] = (gelu * up_part).astype(bf16)
            gelu_low[p] = gelu.astype(bf16)
            slope_low[p] = (slope * up_part).astype(bf16)
            low = contract(act_low[p], w_down, 1, 0).astype(bf16)
            partial[p] = [low[:tok_rows], low[tok_rows:]]
        out_rows = ways.plane_scatter(partial)
        unit_out, scale_out = normed(out_rows)
        mixed = (middle + unit_out * gain_fpost).astype(bf16)[None]

        upstream = cotangent[0].astype(f32)
        d_gfpost = jnp.sum(upstream * unit_out, axis=0)
        d_mlp_out = norm_back(unit_out, scale_out, upstream * gain_fpost).astype(bf16)
        d_out_rows = {p: jnp.concatenate(b, axis=0) for p, b in ways.plane_gather(d_mlp_out).items()}
        d_gate_low, d_up_low, partial = {}, {}, {}
        for p in places:
            d_act = contract(d_out_rows[p], w_down, 1, 1)
            d_gate_low[p] = (d_act * slope_low[p].astype(f32)).astype(bf16)
            d_up_low[p] = (d_act * gelu_low[p].astype(f32)).astype(bf16)
            low = (
                contract(d_gate_low[p], w_gate, 1, 0) + contract(d_up_low[p], w_up, 1, 0)
            ).astype(bf16)
            partial[p] = [low[:tok_rows], low[tok_rows:]]
        d_rows_in = ways.plane_scatter(partial)

        def together(by_place):
            return jnp.concatenate([by_place[p] for p in places], axis=0)

        ffn_all = after(together(ffn_rows), *[partial[p][0] for p in places])
        grads = [
            contract(together(act_low), after(together(d_out_rows), ffn_all), 0, 0).astype(bf16),
            contract(together(d_gate_low), ffn_all, 0, 0).astype(bf16),
            contract(together(d_up_low), ffn_all, 0, 0).astype(bf16),
        ]

        def own_plane(grad):
            per = nz * held
            total = add_low(
                *[
                    ways.fro(ways.fro(grad[i * per : (i + 1) * per], "u", -ou), "v", -ov)
                    for i, (ou, ov) in enumerate(outers)
                ]
            )
            return [total[oz * held : (oz + 1) * held] for oz in range(nz)]

        grad_parts = [own_plane(g) for g in grads]
        begun = [ways.z_scatter_begin(parts) for parts in grad_parts]

        d_gfpre = jnp.sum(d_rows_in * unit_mid, axis=0)
        d_middle = upstream + norm_back(unit_mid, scale_mid, d_rows_in * gain_fpre)
        d_gpost = jnp.sum(d_middle * unit_post, axis=0)
        d_attn_out = norm_back(unit_post, scale_post, d_middle * gain_post).astype(bf16)
        d_wout = contract(heads_flat, d_attn_out, 0, 0)
        d_heads = contract(d_attn_out, w_out, 1, 1).astype(bf16)
        going = []
        for parts, sent in zip(grad_parts, begun):
            sent = tuple(after(s, d_heads) for s in sent)
            going.append(ways.z_scatter_go(parts, sent))
        delta = jnp.stack(
            [
                jnp.sum(d_heads[:, cols].astype(f32) * heads_flat[:, cols].astype(f32), axis=1)
                for cols in head_cols
            ]
        )
        delta = jnp.pad(delta, ((0, 8 - H), (0, 0)))
        d_query, d_kv = attend_back(
            info, query, kv_all, key_docs, query_docs, d_heads, log_total, delta
        )
        d_kv = d_kv.reshape(nz, nx, tok_rows, 2 * HD)
        kv_parts = {}
        for oz in sorted(range(nz), key=lambda o: abs(o - nz // 2)):
            kv_parts[oz] = add_low(*[ways.fro(d_kv[oz, oa], ACROSS, -oa) for oa in range(nx)])
        kv_mine = ways.z_scatter([kv_parts[oz] for oz in range(nz)])

        d_gq = jnp.zeros((HD,), f32)
        d_raw = []
        for (unit, scale), cols in zip(normed_q, head_cols):
            rotated = rotate(d_query[:, cols], cosine, -sine)
            d_gq = d_gq + jnp.sum(rotated * unit, axis=0)
            d_raw.append(norm_back(unit, scale, rotated * gain_q).astype(bf16))
        rotated_k = rotate(kv_mine[:, :HD], cosine, -sine)
        d_gk = jnp.sum(rotated_k * unit_k, axis=0)
        d_raw.append(norm_back(unit_k, scale_k, rotated_k * gain_k).astype(bf16))
        d_raw.append(kv_mine[:, HD:].astype(bf16))
        d_qkv = jnp.concatenate(d_raw, axis=1)
        d_wqkv = contract(normed_in, d_qkv, 0, 0)
        d_normed_in = contract(d_qkv, w_qkv, 1, 1)
        d_gpre = jnp.sum(d_normed_in * unit_in, axis=0)
        input_grad = (d_middle + norm_back(unit_in, scale_in, d_normed_in * gain_pre)).astype(bf16)[None]

        gain_grad = jnp.concatenate([d_gpre, d_gq, d_gk, d_gpost, d_gfpre, d_gfpost])
        packed = pack_rows(d_wqkv, d_wout, gain_lines_of(gain_grad), place_of, lines)
        rows = gain_at + gain_rows
        packed = packed.reshape(len(places), sizes["c"], len(outers) * nz * rows, LANES)
        plane_sum = ways.plane_scatter(
            {p: [packed[i, oc] for oc in range(sizes["c"])] for i, p in enumerate(places)}
        ).astype(bf16)
        plane_sum = plane_sum.reshape(len(outers), nz * rows, LANES)
        plane_sum = add_low(
            *[
                ways.fro(ways.fro(plane_sum[i], "u", -ou), "v", -ov)
                for i, (ou, ov) in enumerate(outers)
            ]
        )
        red = ways.z_scatter([plane_sum[oz * rows : (oz + 1) * rows] for oz in range(nz)])
        attn_red = red[:lines].reshape(-1)
        gain_red = red[gain_at:].reshape(-1)[:gain_piece]

        owned = []
        for parts, heard in zip(grad_parts, going):
            total = after(parts[0], d_kv).astype(f32)
            for value in heard:
                total = total + value.astype(f32)
            owned.append(total.astype(bf16)[:share])
        own_rows = jnp.concatenate([owned[1], owned[2], owned[0]], axis=1)
        by_cols = jnp.stack([own_rows[:, i * width : (i + 1) * width] for i in range(ns)])
        mlp_red = seq_exchange(by_cols).astype(f32).reshape(units, width)

        attn_m_new, attn_v_new, attn_new = adam_update(
            attn_w, attn_m, attn_v, attn_red, RATE_MATRIX, DECAY_MATRIX
        )
        mlp_m_new, mlp_v_new, mlp_new = adam_update(
            mlp_w, mlp_m, mlp_v, mlp_red, RATE_MATRIX, DECAY_MATRIX
        )
        gain_m_new, gain_v_new, gain_new = adam_update(
            gains, gain_m, gain_v, gain_red, RATE_GAIN, 0.0
        )
        return (
            mixed, input_grad,
            attn_red, attn_m_new, attn_v_new, attn_new,
            mlp_red, mlp_m_new, mlp_v_new, mlp_new,
            gain_red, gain_m_new, gain_v_new, gain_new,
        )

    return shards


def solution(mesh):
    seq, ctx = mesh.shape["seq"], mesh.shape["ctx"]
    nz = 4 if ctx % 4 == 0 else 1
    chips_y, chips_x = seq // 2, ctx // nz
    y, x = 2 - chips_y % 2, 2 - chips_x % 2
    sizes = {"u": chips_y // y, "y": y, "c": 2, "z": nz, "v": chips_x // x, "x": x}
    fine = Mesh(mesh.devices.reshape(*sizes.values()), tuple(sizes))
    s, x = SEQ, CTX
    both = s + x
    in_specs = (
        P(s, x, None), P(s, x, None), P(s, None), P(s, x),
        P(both), P(both), P(both),
        P(x, s), P(x, s), P(x, s),
        P(both), P(both), P(both),
    )
    out_specs = (
        P(s, x, None), P(s, x, None),
        P(both), P(both), P(both), P(both),
        P(x, s), P(x, s), P(x, s), P(x, s),
        P(both), P(both), P(both), P(both),
    )
    return jax.shard_map(
        make_shards(sizes), mesh=fine, in_specs=in_specs, out_specs=out_specs, check_vma=False
    )
```

```python
import jax
import jax.numpy as jnp
import numpy as np
from jax import lax
from jax.experimental import pallas as pl
from jax.experimental.pallas import tpu as pltpu
from jax.sharding import Mesh, PartitionSpec as P

D = 1152
H = 4
HD = 256
STEP = 5

NORM_EPS = 1e-06
SCORE_FLOOR = -1e30
ROPE_BASE = 1000000.0
BETA_MOMENT = 0.5
ADAM_EPS = 1e-08
RATE_MATRIX = 0.03
RATE_GAIN = 0.5
DECAY_MATRIX = 0.1

bf16 = jnp.bfloat16
f32 = jnp.float32
LANES = 128


def normed(value):
    factor = lax.rsqrt(jnp.mean(value * value, axis=-1, keepdims=True) + NORM_EPS)
    return (value * factor, factor)


def norm_back(unit, factor, d_unit):
    return factor * (d_unit - unit * jnp.mean(d_unit * unit, axis=-1, keepdims=True))


def angles(position):
    half_index = jnp.arange(HD // 2, dtype=f32)
    frequency = jnp.exp(half_index * (-2.0 * jnp.log(ROPE_BASE) / HD))
    angle = position.astype(f32)[:, None] * frequency[None, :]
    return (jnp.cos(angle), jnp.sin(angle))


def rotate(value, cosine, sine):
    half_width = value.shape[-1] // 2
    first_half = value[..., :half_width]
    second_half = value[..., half_width:]
    return jnp.concatenate(
        [first_half * cosine - second_half * sine, second_half * cosine + first_half * sine],
        axis=-1,
    )


def contract(left, right, left_dim, right_dim):
    return lax.dot_general(
        left, right, (((left_dim,), (right_dim,)), ((), ())), preferred_element_type=f32
    )


def adam_update(weight, moment_one, second, gradient, learn_rate, decay_rate):
    moment_new = BETA_MOMENT * moment_one + (1.0 - BETA_MOMENT) * gradient
    second_new = BETA_MOMENT * second + (1.0 - BETA_MOMENT) * gradient * gradient
    correction = 1.0 - BETA_MOMENT**STEP
    update = moment_new / correction / (jnp.sqrt(second_new / correction) + ADAM_EPS)
    return (moment_new, second_new, weight - learn_rate * (update + decay_rate * weight))


def add_low(*parts):
    total = parts[0].astype(f32)
    for part in parts[1:]:
        total = total + part.astype(f32)
    return total.astype(bf16)


def after(value, *earlier):
    return lax.optimization_barrier((value,) + earlier)[0]


def halfway(rows):
    return rows // 32 * 16 if rows >= 32 else rows // 2


VMEM_LIMIT = 56 * 1024 * 1024
SCORE_SCALE = HD ** (-0.5)
SPACES = {"v": pltpu.VMEM, "h": pl.ANY, "s": pltpu.SMEM}


def run(name, body, operands, spaces, out_shape, scratch=(), out_spaces=None):
    return pl.pallas_call(
        body,
        out_shape=tuple(jax.ShapeDtypeStruct(s, d) for s, d in out_shape),
        in_specs=[pl.BlockSpec(memory_space=SPACES[s]) for s in spaces],
        out_specs=tuple(
            pl.BlockSpec(memory_space=SPACES[s]) for s in out_spaces or "v" * len(out_shape)
        ),
        scratch_shapes=list(scratch),
        compiler_params=pltpu.CompilerParams(vmem_limit_bytes=VMEM_LIMIT),
        cost_estimate=pl.CostEstimate(flops=0, bytes_accessed=0, transcendentals=0),
        name=name,
    )(*operands)


class Flat:
    def __init__(self, piece, gain_piece, devices):
        self.devices = devices
        self.lines = piece // LANES
        self.gain_at = -(-self.lines // 16) * 16
        self.gain_piece = gain_piece
        self.rows = self.gain_at + 16
        self.q_across, self.o_across = (H + 2) * HD // LANES, D // LANES
        self.q_lines, self.o_lines = D * self.q_across, H * HD * self.o_across
        widths = [D, HD, HD, D, D, D]
        self.gain_rows = [w // LANES for w in widths]
        self.gain_lines = sum(self.gain_rows)

    def gain_line(self, device):
        return self.gain_piece * device // LANES


def fetch(order_ref, sources, held, sems):
    copies = []
    for source in sources:
        for i in range(source.shape[0]):
            k = len(copies)
            copies.append(pltpu.make_async_copy(source.at[i], held.at[order_ref[k]], sems.at[k]))
    for copy in copies:
        copy.start()
    return copies


def first_part(flat, parts, order, tokens, cosine, sine):
    tok_rows = tokens.shape[0]
    wide = (H + 2) * HD
    blocks = -(-flat.q_lines // flat.lines)

    def body(order_ref, *refs):
        sources = refs[: len(parts)]
        (
            tok_ref, cos_ref, sin_ref, w_ref, g_pre, g_q, g_k, g_post, g_fpre, g_fpost,
            a_ref, q_ref, kv_ref, raw_ref, held, lines, gains, sems,
        ) = refs[len(parts) :]
        copies = fetch(order_ref, sources, held, sems)
        unit, _ = normed(tok_ref[...].astype(f32))
        gains[...] = jnp.zeros_like(gains)
        for copy in copies:
            copy.wait()
        for i in range(flat.devices):
            at = flat.gain_line(i)
            gains[at : at + 3, :] += held[i, flat.gain_at :, :].astype(f32)[:3]
        at = 0
        for ref, rows in zip((g_pre, g_q, g_k, g_post, g_fpre, g_fpost), flat.gain_rows):
            for i in range(rows):
                ref[:, i * LANES : (i + 1) * LANES] = gains[at + i : at + i + 1, :]
            at += rows
        a_ref[...] = (unit * g_pre[...]).astype(bf16)
        for i in range(blocks):
            lines[i * flat.lines : (i + 1) * flat.lines, :] = held[i, : flat.gain_at, :].astype(f32)[
                : flat.lines
            ]
        for j in range(flat.q_across):
            w_ref[:, j * LANES : (j + 1) * LANES] = lines[
                pl.ds(j, D, stride=flat.q_across), :
            ].astype(bf16)
        qkv = contract(a_ref[...], w_ref[...], 1, 0)
        raw_ref[...] = qkv[:, : (H + 1) * HD]
        cos, sin = cos_ref[...], sin_ref[...]
        for h in range(H):
            head = normed(qkv[:, h * HD : (h + 1) * HD])[0] * g_q[...]
            low = rotate(head, cos, sin).astype(bf16)
            q_ref[:, h * HD : (h + 1) * HD] = (low.astype(f32) * SCORE_SCALE).astype(bf16)
        key = normed(qkv[:, H * HD : (H + 1) * HD])[0] * g_k[...]
        kv_ref[:, :HD] = rotate(key, cos, sin).astype(bf16)
        kv_ref[:, HD:] = qkv[:, (H + 1) * HD :].astype(bf16)

    row = [((1, w * LANES), f32) for w in flat.gain_rows]
    return run(
        "first_part",
        body,
        [order, *parts, tokens, cosine, sine],
        "s" + "h" * len(parts) + "vvv",
        [((D, wide), bf16), *row]
        + [((tok_rows, D), bf16), ((tok_rows, H * HD), bf16), ((tok_rows, 2 * HD), bf16)]
        + [((tok_rows, (H + 1) * HD), f32)],
        [
            pltpu.VMEM((flat.devices, flat.rows, LANES), bf16),
            pltpu.VMEM((blocks * flat.lines, LANES), f32),
            pltpu.VMEM((-(-(flat.gain_lines + 3) // 8) * 8, LANES), f32),
            pltpu.SemaphoreType.DMA((flat.devices,)),
        ],
    )


def spread_out(flat, parts, order):
    start = flat.q_lines // flat.lines

    def body(order_ref, *refs):
        sources = refs[: len(parts)]
        w_ref, held, lines, sems = refs[len(parts) :]
        for copy in fetch(order_ref, sources, held, sems):
            copy.wait()
        for i in range(start, flat.devices):
            at = (i - start) * flat.lines
            lines[at : at + flat.lines, :] = held[i, : flat.gain_at, :].astype(f32)[: flat.lines]
        for j in range(flat.o_across):
            w_ref[:, j * LANES : (j + 1) * LANES] = lines[
                pl.ds(flat.q_lines - start * flat.lines + j, H * HD, stride=flat.o_across), :
            ].astype(bf16)

    return run(
        "spread_out",
        body,
        [order, *parts],
        "s" + "h" * len(parts),
        [((H * HD, D), bf16)],
        [
            pltpu.VMEM((flat.devices, flat.rows, LANES), bf16),
            pltpu.VMEM(((flat.devices - start) * flat.lines, LANES), f32),
            pltpu.SemaphoreType.DMA((flat.devices,)),
        ],
    )[0]


DEAD, WHOLE, MASKED = 0, 1, 2


def allowed_of(kdoc_ref, qdoc_ref, shift):
    keys, queries = kdoc_ref.shape[0], qdoc_ref.shape[1]
    key_at = lax.broadcasted_iota(jnp.int32, (keys, queries), 0) + shift
    query_at = lax.broadcasted_iota(jnp.int32, (keys, queries), 1)
    return (kdoc_ref[...] == qdoc_ref[...]) & (key_at <= query_at)


def same(shape):
    return pl.BlockSpec(shape, lambda i, info: (0,) * len(shape))


def attend(info, query, kv, key_docs, query_docs, w_out, tokens, g_post, g_fpre):
    blocks, rows, _ = kv.shape

    def body(
        info_ref, q_ref, kv_ref, kdoc_ref, qdoc_ref, w_ref, tok_ref, g_post_ref, g_fpre_ref,
        o_ref, lse_ref, out_ref, mid_ref, in_ref, peak, total, acc,
    ):
        step = pl.program_id(0)

        @pl.when(step == 0)
        def _():
            peak[...] = jnp.full_like(peak, SCORE_FLOOR)
            total[...] = jnp.zeros_like(total)
            acc[...] = jnp.zeros_like(acc)

        def visit(masked):
            key = kv_ref[0, :, :HD]
            value_t = kv_ref[0, :, HD:].T
            if masked:
                allowed = allowed_of(
                    kdoc_ref, qdoc_ref, (info_ref[0, step] - info_ref[0, 0]) * rows
                )
            for h in range(H):
                score = contract(key, q_ref[:, h * HD : (h + 1) * HD], 1, 1)
                if masked:
                    score = jnp.where(allowed, score, SCORE_FLOOR)
                old = peak[h : h + 1, :]
                new = jnp.maximum(old, jnp.max(score, axis=0, keepdims=True))
                weight = jnp.exp(score - new)
                shrink = jnp.exp(old - new)
                peak[h : h + 1, :] = new
                total[h : h + 1, :] = total[h : h + 1, :] * shrink + jnp.sum(
                    weight, axis=0, keepdims=True
                )
                acc[h] = acc[h] * shrink + contract(value_t, weight.astype(bf16), 1, 0)

        pl.when(info_ref[1, step] == WHOLE)(lambda: visit(False))
        pl.when(info_ref[1, step] == MASKED)(lambda: visit(True))

        @pl.when(step == blocks - 1)
        def _():
            lse_ref[...] = jnp.zeros_like(lse_ref)
            for h in range(H):
                lse_ref[h : h + 1, :] = peak[h : h + 1, :] + jnp.log(total[h : h + 1, :])
                o_ref[:, h * HD : (h + 1) * HD] = (acc[h] / total[h : h + 1, :]).T.astype(bf16)
            attn_out = contract(o_ref[...], w_ref[...], 1, 0)
            out_ref[...] = attn_out
            middle = tok_ref[...].astype(f32) + normed(attn_out)[0] * g_post_ref[...]
            mid_ref[...] = middle
            in_ref[...] = (normed(middle)[0] * g_fpre_ref[...]).astype(bf16)

    return pl.pallas_call(
        body,
        grid_spec=pltpu.PrefetchScalarGridSpec(
            num_scalar_prefetch=1,
            grid=(blocks,),
            in_specs=[
                same((rows, H * HD)),
                pl.BlockSpec((1, rows, 2 * HD), lambda i, info: (i, 0, 0)),
                pl.BlockSpec((rows, 1), lambda i, info: (info[0, i], 0)),
                same((1, rows)),
                same((H * HD, D)),
                same((rows, D)),
                same((1, D)),
                same((1, D)),
            ],
            out_specs=[
                same((rows, H * HD)),
                same((8, rows)),
                same((rows, D)),
                same((rows, D)),
                same((rows, D)),
            ],
            scratch_shapes=[
                pltpu.VMEM((8, rows), f32),
                pltpu.VMEM((8, rows), f32),
                pltpu.VMEM((H, HD, rows), f32),
            ],
        ),
        out_shape=(
            jax.ShapeDtypeStruct((rows, H * HD), bf16),
            jax.ShapeDtypeStruct((8, rows), f32),
            jax.ShapeDtypeStruct((rows, D), f32),
            jax.ShapeDtypeStruct((rows, D), f32),
            jax.ShapeDtypeStruct((rows, D), bf16),
        ),
        compiler_params=pltpu.CompilerParams(vmem_limit_bytes=VMEM_LIMIT),
        cost_estimate=pl.CostEstimate(flops=0, bytes_accessed=0, transcendentals=0),
        name="attend",
    )(info, query, kv, key_docs, query_docs, w_out, tokens, g_post, g_fpre)


def attend_back(
    info, query, kv, key_docs, query_docs, heads, log_total, d_in, middle, attn_out, cotangent,
    w_out, g_post, g_fpre,
):
    blocks, rows, _ = kv.shape
    terms = len(d_in)

    def body(info_ref, q_ref, kv_ref, kdoc_ref, qdoc_ref, o_ref, lse_ref, *refs):
        terms_ref = refs[:terms]
        (
            mid_ref, out_ref, cot_ref, w_ref, g_post_ref, g_fpre_ref,
            dq_ref, dkv_ref, dout_ref, dmid_ref, dg_fpre_ref, dg_post_ref, do_ref, delta_ref,
        ) = refs[terms:]
        step = pl.program_id(0)

        @pl.when(step == 0)
        def _():
            d_rows = sum(ref[...].astype(f32) for ref in terms_ref)
            unit, scale = normed(mid_ref[...])
            dg_fpre_ref[...] = jnp.sum(d_rows * unit, axis=0, keepdims=True)
            d_middle = cot_ref[...].astype(f32) + norm_back(unit, scale, d_rows * g_fpre_ref[...])
            dmid_ref[...] = d_middle
            unit, scale = normed(out_ref[...])
            dg_post_ref[...] = jnp.sum(d_middle * unit, axis=0, keepdims=True)
            d_out = norm_back(unit, scale, d_middle * g_post_ref[...]).astype(bf16)
            dout_ref[...] = d_out
            delta_ref[...] = jnp.zeros_like(delta_ref)
            for h in range(H):
                cols = slice(h * HD, (h + 1) * HD)
                d_o = contract(d_out, w_ref[cols, :], 1, 1).astype(bf16)
                do_ref[:, cols] = d_o
                each = (d_o.astype(f32) * o_ref[:, cols].astype(f32)).T
                delta_ref[h : h + 1, :] = jnp.sum(each, axis=0, keepdims=True)
            dq_ref[...] = jnp.zeros_like(dq_ref)

        def visit(masked):
            key, value = kv_ref[0, :, :HD], kv_ref[0, :, HD:]
            if masked:
                allowed = allowed_of(
                    kdoc_ref, qdoc_ref, (info_ref[0, step] - info_ref[0, 0]) * rows
                )
            d_key = jnp.zeros((rows, HD), f32)
            d_value = jnp.zeros((rows, HD), f32)
            for h in range(H):
                cols = slice(h * HD, (h + 1) * HD)
                q, d_o = q_ref[:, cols], do_ref[:, cols]
                prob = jnp.exp(contract(key, q, 1, 1) - lse_ref[h : h + 1, :])
                if masked:
                    prob = jnp.where(allowed, prob, 0.0)
                d_value = d_value + contract(prob.astype(bf16), d_o, 1, 0)
                d_prob = contract(value, d_o, 1, 1)
                d_score = (prob * (d_prob - delta_ref[h : h + 1, :])).astype(bf16)
                d_key = d_key + contract(d_score, q, 1, 0)
                dq_ref[:, cols] = dq_ref[:, cols] + contract(d_score, key, 0, 0)
            dkv_ref[0, :, :HD] = d_key.astype(bf16)
            dkv_ref[0, :, HD:] = d_value.astype(bf16)

        pl.when(info_ref[1, step] == WHOLE)(lambda: visit(False))
        pl.when(info_ref[1, step] == MASKED)(lambda: visit(True))

        @pl.when(info_ref[1, step] == DEAD)
        def _():
            dkv_ref[...] = jnp.zeros_like(dkv_ref)

        @pl.when(step == blocks - 1)
        def _():
            dq_ref[...] = dq_ref[...] * SCORE_SCALE

    block = pl.BlockSpec((1, rows, 2 * HD), lambda i, info: (i, 0, 0))
    return pl.pallas_call(
        body,
        grid_spec=pltpu.PrefetchScalarGridSpec(
            num_scalar_prefetch=1,
            grid=(blocks,),
            in_specs=[
                same((rows, H * HD)),
                block,
                pl.BlockSpec((rows, 1), lambda i, info: (info[0, i], 0)),
                same((1, rows)),
                same((rows, H * HD)),
                same((8, rows)),
                *[same((rows, D))] * (terms + 3),
                same((H * HD, D)),
                same((1, D)),
                same((1, D)),
            ],
            out_specs=[
                same((rows, H * HD)),
                block,
                same((rows, D)),
                same((rows, D)),
                same((1, D)),
                same((1, D)),
            ],
            scratch_shapes=[pltpu.VMEM((rows, H * HD), bf16), pltpu.VMEM((8, rows), f32)],
        ),
        out_shape=(
            jax.ShapeDtypeStruct((rows, H * HD), f32),
            jax.ShapeDtypeStruct(kv.shape, bf16),
            jax.ShapeDtypeStruct((rows, D), bf16),
            jax.ShapeDtypeStruct((rows, D), f32),
            jax.ShapeDtypeStruct((1, D), f32),
            jax.ShapeDtypeStruct((1, D), f32),
        ),
        compiler_params=pltpu.CompilerParams(vmem_limit_bytes=VMEM_LIMIT),
        cost_estimate=pl.CostEstimate(flops=0, bytes_accessed=0, transcendentals=0),
        name="attend_back",
    )(
        info, query, kv, key_docs, query_docs, heads, log_total, *d_in, middle, attn_out, cotangent,
        w_out, g_post, g_fpre,
    )


def gelu_parts(gate):
    scale = 0.7978845608028654
    square = gate * gate
    inner = jnp.tanh(scale * gate * (1.0 + 0.044715 * square))
    half_up = 0.5 * (1.0 + inner)
    slope = half_up + 0.5 * gate * (1.0 - inner * inner) * scale * (1.0 + 3 * 0.044715 * square)
    return gate * half_up, slope


def gather_rows(refs, held, sems):
    tok = refs[0].shape[0]
    return [
        pltpu.make_async_copy(ref, held.at[k * tok : (k + 1) * tok], sems.at[k])
        for k, ref in enumerate(refs)
    ]


def scatter_rows(held, refs, sems):
    tok = refs[0].shape[0]
    return [
        pltpu.make_async_copy(held.at[k * tok : (k + 1) * tok], ref, sems.at[k])
        for k, ref in enumerate(refs)
    ]


def by_chunk(step, chunks, copies, do):
    per = len(copies) // chunks
    for k in range(chunks):

        @pl.when(step == k)
        def _(k=k):
            for copy in copies[k * per : (k + 1) * per]:
                do(copy)


def ffn_call(name, body, rows, streams, weights, outs):
    count, (tok, wide) = len(rows), rows[0].shape
    chunks = -(-count * tok // 512)
    both = count * tok // chunks
    per = weights.shape[0]

    def kernel(*refs):
        row_refs, refs = refs[:count], refs[count:]
        stream_refs, refs = refs[: len(streams)], refs[len(streams) :]
        w_refs, refs = refs[:3], refs[3:]
        out_refs, refs = refs[: len(outs)], refs[len(outs) :]
        sum_refs, (held, given, sems_in, sems_out) = refs[:count], refs[count:]
        step = pl.program_id(0)
        coming = gather_rows(row_refs, held, sems_in)
        going = scatter_rows(given, sum_refs, sems_out)

        @pl.when(step == 0)
        def _():
            for copy in coming:
                copy.start()

        by_chunk(step, chunks, coming, lambda copy: copy.wait())
        here = pl.ds(pl.multiple_of(step * both, both), both)
        given[here, :] = body(held[here, :], stream_refs, w_refs, out_refs)
        by_chunk(step, chunks, going, lambda copy: copy.start())

        @pl.when(step == chunks - 1)
        def _():
            for copy in going:
                copy.wait()

    def chunk(width):
        return pl.BlockSpec((both, width), lambda i: (i, 0))

    anywhere = pl.BlockSpec(memory_space=pl.ANY)
    return pl.pallas_call(
        kernel,
        grid=(chunks,),
        in_specs=[anywhere] * count
        + [chunk(s.shape[1]) for s in streams]
        + [pl.BlockSpec((per, D), lambda i, k=k: (0, k)) for k in range(3)],
        out_specs=tuple([chunk(w) for w in outs] + [anywhere] * count),
        out_shape=tuple(
            [jax.ShapeDtypeStruct((count * tok, w), bf16) for w in outs]
            + [jax.ShapeDtypeStruct((tok, wide), bf16)] * count
        ),
        scratch_shapes=[
            pltpu.VMEM((count * tok, wide), bf16),
            pltpu.VMEM((count * tok, wide), bf16),
            pltpu.SemaphoreType.DMA((count,)),
            pltpu.SemaphoreType.DMA((count,)),
        ],
        compiler_params=pltpu.CompilerParams(vmem_limit_bytes=VMEM_LIMIT),
        cost_estimate=pl.CostEstimate(
            flops=6 * count * tok * per * D, bytes_accessed=0, transcendentals=0
        ),
        name=name,
    )(*rows, *streams, weights, weights, weights)


def ffn_forward(rows, weights):
    def body(x, _, w_refs, out_refs):
        act_ref, gelu_ref, slope_ref = out_refs
        gate = contract(x, w_refs[0][...], 1, 1)
        up = contract(x, w_refs[1][...], 1, 1)
        gelu, slope = gelu_parts(gate)
        act = (gelu * up).astype(bf16)
        act_ref[...] = act
        gelu_ref[...] = gelu.astype(bf16)
        slope_ref[...] = (slope * up).astype(bf16)
        return contract(act, w_refs[2][...], 1, 0).astype(bf16)

    per = weights.shape[0]
    act, gelu, slope, *parts = ffn_call("ffn_forward", body, rows, [], weights, [per] * 3)
    return act, gelu, slope, parts


def ffn_backward(rows, gelu, slope, weights):
    per = weights.shape[0]

    def body(x, stream_refs, w_refs, out_refs):
        gelu_ref, slope_ref = stream_refs
        d_act = contract(x, w_refs[2][...], 1, 1)
        d_gate = (d_act * slope_ref[...].astype(f32)).astype(bf16)
        d_up = (d_act * gelu_ref[...].astype(f32)).astype(bf16)
        out_refs[0][:, :per] = d_gate
        out_refs[0][:, per:] = d_up
        return (contract(d_gate, w_refs[0][...], 1, 0) + contract(d_up, w_refs[1][...], 1, 0)).astype(bf16)

    d_both, *parts = ffn_call("ffn_backward", body, rows, [gelu, slope], weights, [2 * per])
    return d_both, parts


def unit_grads(units, per, rows):
    parts, count = len(units), len(rows)
    tokens, wide = sum(u.shape[0] for u in units), units[0].shape[1]
    n = wide // per

    def body(*refs):
        unit_refs, row_refs = refs[:parts], refs[parts : parts + count]
        out_ref, held, sems = refs[parts + count :]
        copies = gather_rows(row_refs, held, sems)

        @pl.when(pl.program_id(0) == 0)
        def _():
            for copy in copies:
                copy.start()
            for copy in copies:
                copy.wait()

        total, at = None, 0
        for ref in unit_refs:
            part = contract(ref[...], held[at : at + ref.shape[0], :], 0, 0)
            total = part if total is None else total + part
            at += ref.shape[0]
        out_ref[...] = total.astype(bf16)

    return pl.pallas_call(
        body,
        grid=(n,),
        in_specs=[pl.BlockSpec((u.shape[0], per), lambda i: (0, i)) for u in units]
        + [pl.BlockSpec(memory_space=pl.ANY)] * count,
        out_specs=pl.BlockSpec((per, D), lambda i: (0, i)),
        out_shape=jax.ShapeDtypeStruct((per, n * D), bf16),
        scratch_shapes=[pltpu.VMEM((tokens, D), bf16), pltpu.SemaphoreType.DMA((count,))],
        compiler_params=pltpu.CompilerParams(vmem_limit_bytes=VMEM_LIMIT),
        cost_estimate=pl.CostEstimate(
            flops=2 * tokens * wide * D, bytes_accessed=0, transcendentals=0
        ),
        name="unit_grads",
    )(*units, *rows)


def after_ffn(out_parts, middle, cotangent, g_fpost):
    terms = len(out_parts)

    def body(*refs):
        mid_ref, cot_ref, g_ref, mixed_ref, d_ref, dg_ref = refs[terms:]
        total = refs[0][...].astype(f32)
        for ref in refs[1:terms]:
            total = total + ref[...].astype(f32)
        unit, scale = normed(total)
        mixed_ref[...] = (mid_ref[...] + unit * g_ref[...]).astype(bf16)
        upstream = cot_ref[...].astype(f32)
        dg_ref[...] = jnp.sum(upstream * unit, axis=0, keepdims=True)
        d_ref[...] = norm_back(unit, scale, upstream * g_ref[...]).astype(bf16)

    shape = out_parts[0].shape
    return run(
        "after_ffn",
        body,
        [*out_parts, middle, cotangent, g_fpost],
        "v" * (terms + 3),
        [(shape, bf16), (shape, bf16), ((1, D), f32)],
    )


def query_side(flat, d_query, raw, cosine, sine, g_q, a, w_qkv, heads, d_attn_out):
    tok = a.shape[0]
    wide = H * HD

    def body(
        dq_ref, raw_ref, cos_ref, sin_ref, g_ref, a_ref, w_ref, o_ref, dout_ref,
        lines, da_ref, dg_ref, low, grad, grad_o,
    ):
        cos, sin = cos_ref[...], sin_ref[...]
        dg = jnp.zeros((1, HD), f32)
        for h in range(H):
            cols = slice(h * HD, (h + 1) * HD)
            unit, scale = normed(raw_ref[:, cols])
            turned = rotate(dq_ref[:, cols], cos, -sin)
            dg = dg + jnp.sum(turned * unit, axis=0, keepdims=True)
            low[:, cols] = norm_back(unit, scale, turned * g_ref[...]).astype(bf16)
        dg_ref[...] = dg
        da_ref[...] = contract(low[...], w_ref[:, :wide], 1, 1)
        grad[...] = contract(a_ref[...], low[...], 0, 0)
        for j in range(wide // LANES):
            lines[pl.ds(j, D, stride=flat.q_across), :] = grad[:, j * LANES : (j + 1) * LANES]
        grad_o[...] = contract(o_ref[...], dout_ref[...], 0, 0)
        for j in range(flat.o_across):
            lines[pl.ds(flat.q_lines + j, wide, stride=flat.o_across), :] = grad_o[
                :, j * LANES : (j + 1) * LANES
            ]
        lines[flat.q_lines + flat.o_lines :, :] = jnp.zeros((16, LANES), f32)

    return run(
        "query_side",
        body,
        [d_query, raw, cosine, sine, g_q, a, w_qkv, heads, d_attn_out],
        "v" * 9,
        [((flat.q_lines + flat.o_lines + 16, LANES), f32), ((tok, D), f32), ((1, HD), f32)],
        [pltpu.VMEM((tok, wide), bf16), pltpu.VMEM((D, wide), f32), pltpu.VMEM((wide, D), f32)],
    )


def last_part(
    flat, order, groups, lines, kv_parts, raw, cosine, sine, g_k, a, w_qkv, tokens, g_pre, d_middle,
    da_query, gain_grads,
):
    tok = a.shape[0]
    terms = len(kv_parts)
    wide = H * HD
    each = flat.devices // groups

    def body(order_ref, lines_ref, *refs):
        kv_refs = refs[:terms]
        (
            raw_ref, cos_ref, sin_ref, gk_ref, a_ref, w_ref, tok_ref, gpre_ref, dmid_ref, da_ref,
            dgq, dgpost, dgfpre, dgfpost, in_ref, *outs, held, grad, gains, blocks, sems,
        ) = refs[terms:]
        q_copy = pltpu.make_async_copy(
            lines_ref.at[: flat.q_lines], held.at[: flat.q_lines], sems.at[0]
        )
        o_copy = pltpu.make_async_copy(
            lines_ref.at[flat.q_lines :], held.at[flat.q_lines :], sems.at[1]
        )
        q_copy.start()
        o_copy.start()
        d_kv = kv_refs[0][...].astype(f32)
        for ref in kv_refs[1:]:
            d_kv = d_kv + ref[...].astype(f32)
        unit, scale = normed(raw_ref[:, wide:])
        turned = rotate(d_kv[:, :HD], cos_ref[...], -sin_ref[...])
        dgk = jnp.sum(turned * unit, axis=0, keepdims=True)
        low = jnp.concatenate(
            [norm_back(unit, scale, turned * gk_ref[...]).astype(bf16), d_kv[:, HD:].astype(bf16)],
            axis=1,
        )
        grad[...] = contract(a_ref[...], low, 0, 0)
        d_a = da_ref[...] + contract(low, w_ref[:, wide:], 1, 1)
        unit, scale = normed(tok_ref[...].astype(f32))
        dgpre = jnp.sum(d_a * unit, axis=0, keepdims=True)
        in_ref[...] = (dmid_ref[...] + norm_back(unit, scale, d_a * gpre_ref[...])).astype(bf16)
        gains[...] = jnp.zeros_like(gains)
        at = 0
        for value in (dgpre, dgq[...], dgk, dgpost[...], dgfpre[...], dgfpost[...]):
            for i in range(value.shape[1] // LANES):
                gains[at : at + 1, :] = value[:, i * LANES : (i + 1) * LANES]
                at += 1
        q_copy.wait()
        for j in range(2 * HD // LANES):
            held[pl.ds(wide // LANES + j, D, stride=flat.q_across), :] = grad[
                :, j * LANES : (j + 1) * LANES
            ]
        o_copy.wait()
        for i in range(flat.devices):
            at = i * flat.lines
            blocks[i, : flat.gain_at, :] = held[at : at + flat.gain_at, :].astype(bf16)
            at = flat.gain_line(i)
            blocks[i, flat.gain_at :, :] = gains[at : at + 16, :].astype(bf16)
        copies = [
            pltpu.make_async_copy(
                blocks.at[order_ref[k]], outs[k // each].at[k % each], sems.at[2 + k]
            )
            for k in range(flat.devices)
        ]
        for copy in copies:
            copy.start()
        for copy in copies:
            copy.wait()

    return run(
        "last_part",
        body,
        [order, lines, *kv_parts, raw, cosine, sine, g_k, a, w_qkv, tokens, g_pre, d_middle]
        + [da_query, *gain_grads],
        "sh" + "v" * (terms + 14),
        [((tok, D), bf16)] + [((each, flat.rows, LANES), bf16)] * groups,
        [
            pltpu.VMEM(lines.shape, f32),
            pltpu.VMEM((D, 2 * HD), f32),
            pltpu.VMEM((-(-(flat.gain_lines + 16) // 8) * 8, LANES), f32),
            pltpu.VMEM((flat.devices, flat.rows, LANES), bf16),
            pltpu.SemaphoreType.DMA((2 + flat.devices,)),
        ],
        "v" + "h" * groups,
    )


class Ways:
    def __init__(self, sizes):
        self.sizes = sizes
        self.what = ""

    def size(self, axis):
        if isinstance(axis, str):
            return self.sizes[axis]
        n = 1
        for a in axis:
            n *= self.sizes[a]
        return n

    def fro(self, value, axis, offset):
        n = self.size(axis)
        if offset % n == 0:
            return value
        with jax.named_scope(self.what + "_" + "".join(axis) + str(offset)):
            return lax.ppermute(value, axis, [((i + offset) % n, i) for i in range(n)])

    def places(self):
        nx, ny = self.sizes["x"], self.sizes["y"]
        return [(ox, oy) for ox in range(nx) for oy in range(ny)]

    def outers(self):
        return [(ou, ov) for ou in range(self.sizes["u"]) for ov in range(self.sizes["v"])]

    def plane_gather(self, value, beside=None):
        nx, ny = self.sizes["x"], self.sizes["y"]
        half = halfway(value.shape[0])
        found = {(0, 0): value}
        for ox in range(1, nx):
            found[ox, 0] = self.fro(value, "x", ox)
        for oy in range(1, ny):
            found[0, oy] = self.fro(value, "y", oy)
        if beside is not None:
            found, beside = lax.optimization_barrier((found, beside))
        for ox in range(1, nx):
            for oy in range(1, ny):
                first = self.fro(found[ox, 0][:half], "y", oy)
                second = self.fro(found[0, oy][half:], "x", ox)
                found[ox, oy] = jnp.concatenate([first, second], axis=0)
        found = {at: [block, self.fro(block, "c", 1)] for at, block in found.items()}
        return found if beside is None else (found, beside)

    def plane_scatter(self, parts, beside=None):
        nx, ny = self.sizes["x"], self.sizes["y"]
        low = {
            at: add_low(parts[at][0], self.fro(parts[at][1], "c", 1))
            for at in sorted(parts, reverse=True)
        }
        half = halfway(low[0, 0].shape[0])
        along_x = {ox: [low[ox, 0][:half]] for ox in range(1, nx)}
        along_y = {oy: [low[0, oy][half:]] for oy in range(1, ny)}
        for ox in range(1, nx):
            for oy in range(1, ny):
                along_x[ox].append(self.fro(low[ox, oy][:half], "y", -oy))
                along_y[oy].append(self.fro(low[ox, oy][half:], "x", -ox))
        if beside is not None:
            along_x, along_y, beside = lax.optimization_barrier((along_x, along_y, beside))
        terms = [low[0, 0]]
        for ox in range(1, nx):
            whole = jnp.concatenate([add_low(*along_x[ox]), low[ox, 0][half:]], axis=0)
            terms.append(self.fro(whole, "x", -ox))
        for oy in range(1, ny):
            whole = jnp.concatenate([low[0, oy][:half], add_low(*along_y[oy])], axis=0)
            terms.append(self.fro(whole, "y", -oy))
        return terms if beside is None else (terms, beside)

    def z_begin(self, value):
        n = self.sizes["z"]
        if n != 4:
            return ()
        return self.fro(value, "z", 1), self.fro(value, "z", -1)

    def z_end(self, value, begun, halves=None):
        n = self.sizes["z"]
        if n != 4:
            return [self.fro(value, "z", oz) for oz in range(n)]
        above, below = begun
        half = halfway(value.shape[0])
        first, second = self.fro(above[:half], "z", 1), self.fro(below[half:], "z", -1)
        return [value, above, jnp.concatenate([first, second], axis=0), below]

    def z_gather(self, value):
        return self.z_end(value, self.z_begin(value))

    def z_pair(self, one, other, begun_one, begun_other):
        if self.sizes["z"] != 4:
            return self.z_end(one, ()), self.z_end(other, ())
        far_one = self.fro(begun_one[0], "z", 1)
        far_other = self.fro(begun_other[1], "z", -1)
        return [one, begun_one[0], far_one, begun_one[1]], [
            other, begun_other[0], far_other, begun_other[1]
        ]

    def z_scatter_begin(self, parts):
        if self.sizes["z"] != 4:
            return ()
        half = halfway(parts[0].shape[0])
        return self.fro(parts[2][:half], "z", -1), self.fro(parts[2][half:], "z", 1)

    def z_scatter_go(self, parts, begun):
        n = self.sizes["z"]
        if n != 4:
            return [self.fro(parts[oz], "z", -oz) for oz in range(1, n)]
        half = halfway(parts[0].shape[0])
        above = jnp.concatenate([add_low(parts[1][:half], begun[0]), parts[1][half:]], axis=0)
        below = jnp.concatenate([parts[3][:half], add_low(parts[3][half:], begun[1])], axis=0)
        return [self.fro(above, "z", -1), self.fro(below, "z", 1)]

    def z_scatter(self, parts):
        return [parts[0], *self.z_scatter_go(parts, self.z_scatter_begin(parts))]


SEQ = ("u", "y", "c")
CTX = ("z", "v", "x")
ACROSS = ("v", "x")


def make_shards(sizes):
    ways = Ways(sizes)
    ns, nctx, nx = ways.size(SEQ), ways.size(CTX), ways.size(ACROSS)
    nz, nc = sizes["z"], sizes["c"]
    devices = ns * nctx
    places, outers = ways.places(), ways.outers()

    def from_outers(value):
        if len(outers) == 1:
            return value
        return jnp.concatenate(
            [ways.fro(ways.fro(value, "u", ou), "v", ov) for ou, ov in outers], axis=0
        )

    def to_outers(value):
        if len(outers) == 1:
            return value
        rows = value.shape[0] // len(outers)
        return add_low(
            *[
                ways.fro(ways.fro(value[i * rows : (i + 1) * rows], "u", -ou), "v", -ov)
                for i, (ou, ov) in enumerate(outers)
            ]
        )

    def plane_rows(value):
        found = ways.plane_gather(value)
        return [block for p in places for block in found[p]]

    def by_device(parts):
        return {p: parts[i * nc : (i + 1) * nc] for i, p in enumerate(places)}

    def own_units(grad):
        return lax.psum_scatter(to_outers(grad), "z", scatter_dimension=0, tiled=True)

    def shards(
        tokens, cotangent, segments, positions, attn_w, attn_m, attn_v,
        mlp_w, mlp_m, mlp_v, gains, gain_m, gain_v,
    ):
        at = {a: lax.axis_index(a) for a in sizes}
        seq_place = lax.axis_index(SEQ)
        across_place = lax.axis_index(ACROSS)
        ctx_place = at["z"] * nx + across_place
        device = seq_place * nctx + ctx_place
        piece, gain_piece = attn_w.shape[0], gains.shape[0]
        flat = Flat(piece, gain_piece, devices)

        sides = [sizes[a] for a in ("x", "y", "c", "u", "v", "z")]
        here = [at[a] for a in ("x", "y", "c", "u", "v", "z")]
        ox, oy, oc, ou, ov, oz = (
            (jnp.asarray(o, jnp.int32) + h) % n
            for o, h, n in zip(np.unravel_index(np.arange(devices), sides), here, sides)
        )
        order = ((ou * sizes["y"] + oy) * sizes["c"] + oc) * nz + oz
        order = (order * sizes["v"] + ov) * sizes["x"] + ox

        ways.what = "attn_gather"
        gain_offset = gain_piece * device % LANES
        gain_window = lax.dynamic_update_slice(
            jnp.zeros((16 * LANES,), bf16), gains.astype(bf16), (gain_offset,)
        )
        low_piece = jnp.concatenate(
            [
                jnp.pad(
                    attn_w.astype(bf16).reshape(flat.lines, LANES),
                    ((0, flat.gain_at - flat.lines), (0, 0)),
                ),
                gain_window.reshape(16, LANES),
            ],
            axis=0,
        )
        line_blocks = ways.z_gather(low_piece)

        ways.what = "unit_exchange"
        units, width = mlp_w.shape
        share = units // ns
        held = -(-share // 32) * 32

        def seq_send(by_place):
            return [
                ways.fro(
                    lax.dynamic_index_in_dim(by_place, (seq_place - offset) % ns, 0, keepdims=False),
                    SEQ,
                    offset,
                )
                for offset in range(ns)
            ]

        def seq_place_all(heard):
            kept = jnp.zeros((ns,) + heard[0].shape, heard[0].dtype)
            for offset, value in enumerate(heard):
                kept = lax.dynamic_update_index_in_dim(kept, value, (seq_place + offset) % ns, 0)
            return kept

        heard = seq_send(mlp_w.astype(bf16).reshape(ns, share, width))
        line_blocks, heard = lax.optimization_barrier((line_blocks, heard))
        by_cols = seq_place_all(heard)
        rows_own = jnp.concatenate([by_cols[i] for i in range(ns)], axis=1)
        rows_own = jnp.pad(rows_own, ((0, held - share), (0, 0)))
        ways.what = "attn_gather"
        line_z = from_outers(jnp.concatenate(line_blocks, axis=0))
        gathered = ways.plane_gather(line_z)
        line_parts = [part.reshape(-1, flat.rows, LANES) for p in places for part in gathered[p]]
        units_here = from_outers(lax.all_gather(rows_own, "z", axis=0, tiled=True))

        tok_rows = tokens.shape[1]
        cosine, sine = angles(positions[0])
        (
            w_qkv, g_pre, g_q, g_k, g_post, g_fpre, g_fpost, normed_in, query, kv_local, raw,
        ) = first_part(flat, line_parts, order, tokens[0], cosine, sine)
        w_out = spread_out(flat, [after(part, kv_local) for part in line_parts], order)
        ways.what = "kv_gather"
        kv_all = jnp.stack(
            [ways.fro(block, ACROSS, oa) for block in ways.z_gather(kv_local) for oa in range(nx)]
        )

        doc_all = segments[0]
        first_docs, last_docs = doc_all[::tok_rows], doc_all[tok_rows - 1 :: tok_rows]
        key_at = np.arange(nctx)
        key_place = (at["z"] + jnp.asarray(key_at // nx, jnp.int32)) % nz * nx
        key_place = key_place + (across_place + jnp.asarray(key_at % nx, jnp.int32)) % nx
        is_place = key_place[:, None] == jnp.arange(nctx, dtype=jnp.int32)[None, :]
        key_first = jnp.sum(jnp.where(is_place, first_docs[None, :], 0), axis=1)
        key_last = jnp.sum(jnp.where(is_place, last_docs[None, :], 0), axis=1)
        live = (key_place < ctx_place) & (key_last >= key_first[0])
        one_doc = key_first == key_last[0]
        task = jnp.where(live, jnp.where(one_doc, WHOLE, MASKED), DEAD)
        task = jnp.where(key_place == ctx_place, MASKED, task)
        info = jnp.stack([key_place, task]).astype(jnp.int32)
        key_docs = doc_all[:, None]
        query_docs = lax.dynamic_slice_in_dim(doc_all, ctx_place * tok_rows, tok_rows)[None]

        heads, log_total, attn_out, middle, ffn_in = attend(
            info, query, kv_all, key_docs, query_docs, w_out, tokens[0], g_post, g_fpre
        )

        ways.what = "ffn_in_gather"
        ffn_rows = plane_rows(ffn_in)
        act, gelu, slope, parts = ffn_forward(ffn_rows, units_here)
        ways.what = "ffn_out_sum"
        out_parts = ways.plane_scatter(by_device(parts))
        mixed, d_mlp_out, d_gfpost = after_ffn(out_parts, middle, cotangent[0], g_fpost)

        ways.what = "d_out_gather"
        d_out_rows = plane_rows(d_mlp_out)
        held_here = units_here.shape[0]
        d_w_down = unit_grads([act], held_here, d_out_rows)
        ways.what = "ffn_grad_sum"
        owned_down = own_units(d_w_down)
        d_out_rows[0] = after(d_out_rows[0], d_w_down)
        d_both, parts = ffn_backward(d_out_rows, gelu, slope, units_here)
        ways.what = "d_in_sum"
        d_in_parts, d_both = ways.plane_scatter(by_device(parts), d_both)

        d_w_gate_up = unit_grads([d_both], held_here, ffn_rows)
        owned_gate_up = own_units(d_w_gate_up)
        d_in_parts = lax.optimization_barrier((d_in_parts, d_w_gate_up))[0]

        d_query, d_kv, d_attn_out, d_middle, d_gfpre, d_gpost = attend_back(
            info, query, kv_all, key_docs, query_docs, heads, log_total, d_in_parts, middle, attn_out,
            cotangent[0], w_out, g_post, g_fpre,
        )
        ways.what = "kv_sum"
        d_kv = d_kv.reshape(nz, nx, tok_rows, 2 * HD)
        kv_parts = {}
        for oz in sorted(range(nz), key=lambda o: abs(o - nz // 2)):
            kv_parts[oz] = add_low(*[ways.fro(d_kv[oz, oa], ACROSS, -oa) for oa in range(nx)])
        kv_parts[0], owned_down = lax.optimization_barrier((kv_parts[0], owned_down))
        kv_parts = ways.z_scatter([kv_parts[oz] for oz in range(nz)])
        lines, da_query, d_gq = query_side(
            flat, d_query, raw, cosine, sine, g_q, normed_in, w_qkv, heads, d_attn_out
        )
        input_grad, *packed = last_part(
            flat, order, len(places) * nc, lines, kv_parts, raw, cosine, sine, g_k, normed_in, w_qkv, tokens[0],
            g_pre, d_middle, da_query, [d_gq, d_gpost, d_gfpre, d_gfpost],
        )

        ways.what = "attn_grad_sum"
        packed[0], owned_gate_up = lax.optimization_barrier((packed[0], owned_gate_up))
        packed = [part.reshape(-1, LANES) for part in packed]
        plane_sum = add_low(
            *ways.plane_scatter(
                {p: packed[i * nc : (i + 1) * nc] for i, p in enumerate(places)}
            )
        )
        plane_sum = to_outers(plane_sum)
        red = sum(
            part.astype(f32)
            for part in ways.z_scatter(
                [plane_sum[oz * flat.rows : (oz + 1) * flat.rows] for oz in range(nz)]
            )
        )
        attn_red = red[: flat.lines].reshape(-1)
        gain_red = lax.dynamic_slice(red[flat.gain_at :].reshape(-1), (gain_offset,), (gain_piece,))

        ways.what = "grad_exchange"
        own_rows = jnp.concatenate([owned_gate_up[:share], owned_down[:share]], axis=1)
        by_cols = jnp.stack([own_rows[:, i * width : (i + 1) * width] for i in range(ns)])
        mlp_red = seq_place_all(seq_send(by_cols)).astype(f32).reshape(units, width)

        attn_m_new, attn_v_new, attn_new = adam_update(
            attn_w, attn_m, attn_v, attn_red, RATE_MATRIX, DECAY_MATRIX
        )
        mlp_m_new, mlp_v_new, mlp_new = adam_update(
            mlp_w, mlp_m, mlp_v, mlp_red, RATE_MATRIX, DECAY_MATRIX
        )
        gain_m_new, gain_v_new, gain_new = adam_update(
            gains, gain_m, gain_v, gain_red, RATE_GAIN, 0.0
        )
        return (
            mixed[None], input_grad[None],
            attn_red, attn_m_new, attn_v_new, attn_new,
            mlp_red, mlp_m_new, mlp_v_new, mlp_new,
            gain_red, gain_m_new, gain_v_new, gain_new,
        )

    return shards


def solution(mesh):
    seq, ctx = mesh.shape["seq"], mesh.shape["ctx"]
    nz = 4 if ctx % 4 == 0 else 1
    chips_y, chips_x = seq // 2, ctx // nz
    y, x = 2 - chips_y % 2, 2 - chips_x % 2
    sizes = {"u": chips_y // y, "y": y, "c": 2, "z": nz, "v": chips_x // x, "x": x}
    fine = Mesh(mesh.devices.reshape(*sizes.values()), tuple(sizes))
    s, x = SEQ, CTX
    both = s + x
    in_specs = (
        P(s, x, None), P(s, x, None), P(s, None), P(s, x),
        P(both), P(both), P(both),
        P(x, s), P(x, s), P(x, s),
        P(both), P(both), P(both),
    )
    out_specs = (
        P(s, x, None), P(s, x, None),
        P(both), P(both), P(both), P(both),
        P(x, s), P(x, s), P(x, s), P(x, s),
        P(both), P(both), P(both), P(both),
    )
    return jax.shard_map(
        make_shards(sizes), mesh=fine, in_specs=in_specs, out_specs=out_specs, check_vma=False
    )
```

```python
import jax
import jax.numpy as jnp
import numpy as np
from jax import lax
from jax.experimental import pallas as pl
from jax.experimental.pallas import tpu as pltpu
from jax.sharding import Mesh, PartitionSpec as P

D = 1152
H = 4
HD = 256
STEP = 5

NORM_EPS = 1e-06
SCORE_FLOOR = -1e30
ROPE_BASE = 1000000.0
BETA_MOMENT = 0.5
ADAM_EPS = 1e-08
RATE_MATRIX = 0.03
RATE_GAIN = 0.5
DECAY_MATRIX = 0.1

bf16 = jnp.bfloat16
f32 = jnp.float32
LANES = 128


def normed(value):
    factor = lax.rsqrt(jnp.mean(value * value, axis=-1, keepdims=True) + NORM_EPS)
    return (value * factor, factor)


def norm_back(unit, factor, d_unit):
    return factor * (d_unit - unit * jnp.mean(d_unit * unit, axis=-1, keepdims=True))


def angles(position):
    half_index = jnp.arange(HD // 2, dtype=f32)
    frequency = jnp.exp(half_index * (-2.0 * jnp.log(ROPE_BASE) / HD))
    angle = position.astype(f32)[:, None] * frequency[None, :]
    return (jnp.cos(angle), jnp.sin(angle))


def rotate(value, cosine, sine):
    half_width = value.shape[-1] // 2
    first_half = value[..., :half_width]
    second_half = value[..., half_width:]
    return jnp.concatenate(
        [first_half * cosine - second_half * sine, second_half * cosine + first_half * sine],
        axis=-1,
    )


def contract(left, right, left_dim, right_dim):
    return lax.dot_general(
        left, right, (((left_dim,), (right_dim,)), ((), ())), preferred_element_type=f32
    )


def adam_update(weight, moment_one, second, gradient, learn_rate, decay_rate):
    moment_new = BETA_MOMENT * moment_one + (1.0 - BETA_MOMENT) * gradient
    second_new = BETA_MOMENT * second + (1.0 - BETA_MOMENT) * gradient * gradient
    correction = 1.0 - BETA_MOMENT**STEP
    update = moment_new / correction / (jnp.sqrt(second_new / correction) + ADAM_EPS)
    return (moment_new, second_new, weight - learn_rate * (update + decay_rate * weight))


def add_low(*parts):
    total = parts[0].astype(f32)
    for part in parts[1:]:
        total = total + part.astype(f32)
    return total.astype(bf16)


def after(value, *earlier):
    return lax.optimization_barrier((value,) + earlier)[0]


def halfway(rows):
    return rows // 32 * 16 if rows >= 32 else rows // 2


VMEM_LIMIT = 56 * 1024 * 1024
SCORE_SCALE = HD ** (-0.5)
SPACES = {"v": pltpu.VMEM, "h": pl.ANY, "s": pltpu.SMEM}


def run(name, body, operands, spaces, out_shape, scratch=(), out_spaces=None):
    return pl.pallas_call(
        body,
        out_shape=tuple(jax.ShapeDtypeStruct(s, d) for s, d in out_shape),
        in_specs=[pl.BlockSpec(memory_space=SPACES[s]) for s in spaces],
        out_specs=tuple(
            pl.BlockSpec(memory_space=SPACES[s]) for s in out_spaces or "v" * len(out_shape)
        ),
        scratch_shapes=list(scratch),
        compiler_params=pltpu.CompilerParams(vmem_limit_bytes=VMEM_LIMIT),
        cost_estimate=pl.CostEstimate(flops=0, bytes_accessed=0, transcendentals=0),
        name=name,
    )(*operands)


class Flat:
    def __init__(self, piece, gain_piece, devices):
        self.devices = devices
        self.lines = piece // LANES
        self.gain_at = -(-self.lines // 16) * 16
        self.gain_piece = gain_piece
        self.rows = self.gain_at + 16
        self.q_across, self.o_across = (H + 2) * HD // LANES, D // LANES
        self.q_lines, self.o_lines = D * self.q_across, H * HD * self.o_across
        widths = [D, HD, HD, D, D, D]
        self.gain_rows = [w // LANES for w in widths]
        self.gain_lines = sum(self.gain_rows)

    def gain_line(self, device):
        return self.gain_piece * device // LANES


def fetch(order_ref, sources, held, sems):
    copies = []
    for source in sources:
        for i in range(source.shape[0]):
            k = len(copies)
            copies.append(pltpu.make_async_copy(source.at[i], held.at[order_ref[k]], sems.at[k]))
    for copy in copies:
        copy.start()
    return copies


def first_part(flat, parts, order, tokens, cosine, sine):
    tok_rows = tokens.shape[0]
    wide = (H + 2) * HD
    blocks = -(-flat.q_lines // flat.lines)

    def body(order_ref, *refs):
        sources = refs[: len(parts)]
        (
            tok_ref, cos_ref, sin_ref, w_ref, g_pre, g_q, g_k, g_post, g_fpre, g_fpost,
            a_ref, q_ref, kv_ref, raw_ref, held, lines, gains, sems,
        ) = refs[len(parts) :]
        copies = fetch(order_ref, sources, held, sems)
        unit, _ = normed(tok_ref[...].astype(f32))
        gains[...] = jnp.zeros_like(gains)
        for copy in copies:
            copy.wait()
        for i in range(flat.devices):
            at = flat.gain_line(i)
            gains[at : at + 3, :] += held[i, flat.gain_at :, :].astype(f32)[:3]
        at = 0
        for ref, rows in zip((g_pre, g_q, g_k, g_post, g_fpre, g_fpost), flat.gain_rows):
            for i in range(rows):
                ref[:, i * LANES : (i + 1) * LANES] = gains[at + i : at + i + 1, :]
            at += rows
        a_ref[...] = (unit * g_pre[...]).astype(bf16)
        for i in range(blocks):
            lines[i * flat.lines : (i + 1) * flat.lines, :] = held[i, : flat.gain_at, :].astype(f32)[
                : flat.lines
            ]
        for j in range(flat.q_across):
            w_ref[:, j * LANES : (j + 1) * LANES] = lines[
                pl.ds(j, D, stride=flat.q_across), :
            ].astype(bf16)
        qkv = contract(a_ref[...], w_ref[...], 1, 0)
        raw_ref[...] = qkv[:, : (H + 1) * HD]
        cos, sin = cos_ref[...], sin_ref[...]
        for h in range(H):
            head = normed(qkv[:, h * HD : (h + 1) * HD])[0] * g_q[...]
            low = rotate(head, cos, sin).astype(bf16)
            q_ref[:, h * HD : (h + 1) * HD] = (low.astype(f32) * SCORE_SCALE).astype(bf16)
        key = normed(qkv[:, H * HD : (H + 1) * HD])[0] * g_k[...]
        kv_ref[:, :HD] = rotate(key, cos, sin).astype(bf16)
        kv_ref[:, HD:] = qkv[:, (H + 1) * HD :].astype(bf16)

    row = [((1, w * LANES), f32) for w in flat.gain_rows]
    return run(
        "first_part",
        body,
        [order, *parts, tokens, cosine, sine],
        "s" + "h" * len(parts) + "vvv",
        [((D, wide), bf16), *row]
        + [((tok_rows, D), bf16), ((tok_rows, H * HD), bf16), ((tok_rows, 2 * HD), bf16)]
        + [((tok_rows, (H + 1) * HD), f32)],
        [
            pltpu.VMEM((flat.devices, flat.rows, LANES), bf16),
            pltpu.VMEM((blocks * flat.lines, LANES), f32),
            pltpu.VMEM((-(-(flat.gain_lines + 3) // 8) * 8, LANES), f32),
            pltpu.SemaphoreType.DMA((flat.devices,)),
        ],
    )


def spread_out(flat, parts, order):
    start = flat.q_lines // flat.lines

    def body(order_ref, *refs):
        sources = refs[: len(parts)]
        w_ref, held, lines, sems = refs[len(parts) :]
        for copy in fetch(order_ref, sources, held, sems):
            copy.wait()
        for i in range(start, flat.devices):
            at = (i - start) * flat.lines
            lines[at : at + flat.lines, :] = held[i, : flat.gain_at, :].astype(f32)[: flat.lines]
        for j in range(flat.o_across):
            w_ref[:, j * LANES : (j + 1) * LANES] = lines[
                pl.ds(flat.q_lines - start * flat.lines + j, H * HD, stride=flat.o_across), :
            ].astype(bf16)

    return run(
        "spread_out",
        body,
        [order, *parts],
        "s" + "h" * len(parts),
        [((H * HD, D), bf16)],
        [
            pltpu.VMEM((flat.devices, flat.rows, LANES), bf16),
            pltpu.VMEM(((flat.devices - start) * flat.lines, LANES), f32),
            pltpu.SemaphoreType.DMA((flat.devices,)),
        ],
    )[0]


DEAD, WHOLE, MASKED = 0, 1, 2


def allowed_of(kdoc_ref, qdoc_ref, shift):
    keys, queries = kdoc_ref.shape[0], qdoc_ref.shape[1]
    key_at = lax.broadcasted_iota(jnp.int32, (keys, queries), 0) + shift
    query_at = lax.broadcasted_iota(jnp.int32, (keys, queries), 1)
    return (kdoc_ref[...] == qdoc_ref[...]) & (key_at <= query_at)


def same(shape):
    return pl.BlockSpec(shape, lambda i, info: (0,) * len(shape))


def attend(info, query, kv, key_docs, query_docs, w_out, tokens, g_post, g_fpre):
    blocks, rows, _ = kv.shape

    def body(
        info_ref, q_ref, kv_ref, kdoc_ref, qdoc_ref, w_ref, tok_ref, g_post_ref, g_fpre_ref,
        o_ref, lse_ref, out_ref, mid_ref, in_ref, peak, total, acc,
    ):
        step = pl.program_id(0)

        @pl.when(step == 0)
        def _():
            peak[...] = jnp.full_like(peak, SCORE_FLOOR)
            total[...] = jnp.zeros_like(total)
            acc[...] = jnp.zeros_like(acc)

        def visit(masked):
            key = kv_ref[0, :, :HD]
            value_t = kv_ref[0, :, HD:].T
            if masked:
                allowed = allowed_of(
                    kdoc_ref, qdoc_ref, (info_ref[0, step] - info_ref[0, 0]) * rows
                )
            for h in range(H):
                score = contract(key, q_ref[:, h * HD : (h + 1) * HD], 1, 1)
                if masked:
                    score = jnp.where(allowed, score, SCORE_FLOOR)
                old = peak[h : h + 1, :]
                new = jnp.maximum(old, jnp.max(score, axis=0, keepdims=True))
                weight = jnp.exp(score - new)
                shrink = jnp.exp(old - new)
                peak[h : h + 1, :] = new
                total[h : h + 1, :] = total[h : h + 1, :] * shrink + jnp.sum(
                    weight, axis=0, keepdims=True
                )
                acc[h] = acc[h] * shrink + contract(value_t, weight.astype(bf16), 1, 0)

        pl.when(info_ref[1, step] == WHOLE)(lambda: visit(False))
        pl.when(info_ref[1, step] == MASKED)(lambda: visit(True))

        @pl.when(step == blocks - 1)
        def _():
            lse_ref[...] = jnp.zeros_like(lse_ref)
            for h in range(H):
                lse_ref[h : h + 1, :] = peak[h : h + 1, :] + jnp.log(total[h : h + 1, :])
                o_ref[:, h * HD : (h + 1) * HD] = (acc[h] / total[h : h + 1, :]).T.astype(bf16)
            attn_out = contract(o_ref[...], w_ref[...], 1, 0)
            out_ref[...] = attn_out
            middle = tok_ref[...].astype(f32) + normed(attn_out)[0] * g_post_ref[...]
            mid_ref[...] = middle
            in_ref[...] = (normed(middle)[0] * g_fpre_ref[...]).astype(bf16)

    return pl.pallas_call(
        body,
        grid_spec=pltpu.PrefetchScalarGridSpec(
            num_scalar_prefetch=1,
            grid=(blocks,),
            in_specs=[
                same((rows, H * HD)),
                pl.BlockSpec((1, rows, 2 * HD), lambda i, info: (i, 0, 0)),
                pl.BlockSpec((rows, 1), lambda i, info: (info[0, i], 0)),
                same((1, rows)),
                same((H * HD, D)),
                same((rows, D)),
                same((1, D)),
                same((1, D)),
            ],
            out_specs=[
                same((rows, H * HD)),
                same((8, rows)),
                same((rows, D)),
                same((rows, D)),
                same((rows, D)),
            ],
            scratch_shapes=[
                pltpu.VMEM((8, rows), f32),
                pltpu.VMEM((8, rows), f32),
                pltpu.VMEM((H, HD, rows), f32),
            ],
        ),
        out_shape=(
            jax.ShapeDtypeStruct((rows, H * HD), bf16),
            jax.ShapeDtypeStruct((8, rows), f32),
            jax.ShapeDtypeStruct((rows, D), f32),
            jax.ShapeDtypeStruct((rows, D), f32),
            jax.ShapeDtypeStruct((rows, D), bf16),
        ),
        compiler_params=pltpu.CompilerParams(vmem_limit_bytes=VMEM_LIMIT),
        cost_estimate=pl.CostEstimate(flops=0, bytes_accessed=0, transcendentals=0),
        name="attend",
    )(info, query, kv, key_docs, query_docs, w_out, tokens, g_post, g_fpre)


def attend_back(
    info, query, kv, key_docs, query_docs, heads, log_total, d_in, middle, attn_out, cotangent,
    w_out, g_post, g_fpre,
):
    blocks, rows, _ = kv.shape
    terms = len(d_in)

    def body(info_ref, q_ref, kv_ref, kdoc_ref, qdoc_ref, o_ref, lse_ref, *refs):
        terms_ref = refs[:terms]
        (
            mid_ref, out_ref, cot_ref, w_ref, g_post_ref, g_fpre_ref,
            dq_ref, dkv_ref, dout_ref, dmid_ref, dg_fpre_ref, dg_post_ref, do_ref, delta_ref,
        ) = refs[terms:]
        step = pl.program_id(0)

        @pl.when(step == 0)
        def _():
            d_rows = sum(ref[...].astype(f32) for ref in terms_ref)
            unit, scale = normed(mid_ref[...])
            dg_fpre_ref[...] = jnp.sum(d_rows * unit, axis=0, keepdims=True)
            d_middle = cot_ref[...].astype(f32) + norm_back(unit, scale, d_rows * g_fpre_ref[...])
            dmid_ref[...] = d_middle
            unit, scale = normed(out_ref[...])
            dg_post_ref[...] = jnp.sum(d_middle * unit, axis=0, keepdims=True)
            d_out = norm_back(unit, scale, d_middle * g_post_ref[...]).astype(bf16)
            dout_ref[...] = d_out
            delta_ref[...] = jnp.zeros_like(delta_ref)
            for h in range(H):
                cols = slice(h * HD, (h + 1) * HD)
                d_o = contract(d_out, w_ref[cols, :], 1, 1).astype(bf16)
                do_ref[:, cols] = d_o
                each = (d_o.astype(f32) * o_ref[:, cols].astype(f32)).T
                delta_ref[h : h + 1, :] = jnp.sum(each, axis=0, keepdims=True)
            dq_ref[...] = jnp.zeros_like(dq_ref)

        def visit(masked):
            key, value = kv_ref[0, :, :HD], kv_ref[0, :, HD:]
            if masked:
                allowed = allowed_of(
                    kdoc_ref, qdoc_ref, (info_ref[0, step] - info_ref[0, 0]) * rows
                )
            d_key = jnp.zeros((rows, HD), f32)
            d_value = jnp.zeros((rows, HD), f32)
            for h in range(H):
                cols = slice(h * HD, (h + 1) * HD)
                q, d_o = q_ref[:, cols], do_ref[:, cols]
                prob = jnp.exp(contract(key, q, 1, 1) - lse_ref[h : h + 1, :])
                if masked:
                    prob = jnp.where(allowed, prob, 0.0)
                d_value = d_value + contract(prob.astype(bf16), d_o, 1, 0)
                d_prob = contract(value, d_o, 1, 1)
                d_score = (prob * (d_prob - delta_ref[h : h + 1, :])).astype(bf16)
                d_key = d_key + contract(d_score, q, 1, 0)
                dq_ref[:, cols] = dq_ref[:, cols] + contract(d_score, key, 0, 0)
            dkv_ref[0, :, :HD] = d_key.astype(bf16)
            dkv_ref[0, :, HD:] = d_value.astype(bf16)

        pl.when(info_ref[1, step] == WHOLE)(lambda: visit(False))
        pl.when(info_ref[1, step] == MASKED)(lambda: visit(True))

        @pl.when(info_ref[1, step] == DEAD)
        def _():
            dkv_ref[...] = jnp.zeros_like(dkv_ref)

        @pl.when(step == blocks - 1)
        def _():
            dq_ref[...] = dq_ref[...] * SCORE_SCALE

    block = pl.BlockSpec((1, rows, 2 * HD), lambda i, info: (i, 0, 0))
    return pl.pallas_call(
        body,
        grid_spec=pltpu.PrefetchScalarGridSpec(
            num_scalar_prefetch=1,
            grid=(blocks,),
            in_specs=[
                same((rows, H * HD)),
                block,
                pl.BlockSpec((rows, 1), lambda i, info: (info[0, i], 0)),
                same((1, rows)),
                same((rows, H * HD)),
                same((8, rows)),
                *[same((rows, D))] * (terms + 3),
                same((H * HD, D)),
                same((1, D)),
                same((1, D)),
            ],
            out_specs=[
                same((rows, H * HD)),
                block,
                same((rows, D)),
                same((rows, D)),
                same((1, D)),
                same((1, D)),
            ],
            scratch_shapes=[pltpu.VMEM((rows, H * HD), bf16), pltpu.VMEM((8, rows), f32)],
        ),
        out_shape=(
            jax.ShapeDtypeStruct((rows, H * HD), f32),
            jax.ShapeDtypeStruct(kv.shape, bf16),
            jax.ShapeDtypeStruct((rows, D), bf16),
            jax.ShapeDtypeStruct((rows, D), f32),
            jax.ShapeDtypeStruct((1, D), f32),
            jax.ShapeDtypeStruct((1, D), f32),
        ),
        compiler_params=pltpu.CompilerParams(vmem_limit_bytes=VMEM_LIMIT),
        cost_estimate=pl.CostEstimate(flops=0, bytes_accessed=0, transcendentals=0),
        name="attend_back",
    )(
        info, query, kv, key_docs, query_docs, heads, log_total, *d_in, middle, attn_out, cotangent,
        w_out, g_post, g_fpre,
    )


def gelu_parts(gate):
    scale = 0.7978845608028654
    square = gate * gate
    inner = jnp.tanh(scale * gate * (1.0 + 0.044715 * square))
    half_up = 0.5 * (1.0 + inner)
    slope = half_up + 0.5 * gate * (1.0 - inner * inner) * scale * (1.0 + 3 * 0.044715 * square)
    return gate * half_up, slope


def gather_rows(refs, held, sems):
    tok = refs[0].shape[0]
    return [
        pltpu.make_async_copy(ref, held.at[k * tok : (k + 1) * tok], sems.at[k])
        for k, ref in enumerate(refs)
    ]


def scatter_rows(held, refs, sems):
    tok = refs[0].shape[0]
    return [
        pltpu.make_async_copy(held.at[k * tok : (k + 1) * tok], ref, sems.at[k])
        for k, ref in enumerate(refs)
    ]


def by_chunk(step, chunks, copies, do):
    per = len(copies) // chunks
    for k in range(chunks):

        @pl.when(step == k)
        def _(k=k):
            for copy in copies[k * per : (k + 1) * per]:
                do(copy)


def ffn_call(name, body, rows, streams, weights, outs):
    count, (tok, wide) = len(rows), rows[0].shape
    chunks = -(-count * tok // 512)
    both = count * tok // chunks
    per = weights.shape[0]

    def kernel(*refs):
        row_refs, refs = refs[:count], refs[count:]
        stream_refs, refs = refs[: len(streams)], refs[len(streams) :]
        w_refs, refs = refs[:3], refs[3:]
        out_refs, refs = refs[: len(outs)], refs[len(outs) :]
        sum_refs, (held, given, sems_in, sems_out) = refs[:count], refs[count:]
        step = pl.program_id(0)
        coming = gather_rows(row_refs, held, sems_in)
        going = scatter_rows(given, sum_refs, sems_out)

        @pl.when(step == 0)
        def _():
            for copy in coming:
                copy.start()

        by_chunk(step, chunks, coming, lambda copy: copy.wait())
        here = pl.ds(pl.multiple_of(step * both, both), both)
        given[here, :] = body(held[here, :], stream_refs, w_refs, out_refs)
        by_chunk(step, chunks, going, lambda copy: copy.start())

        @pl.when(step == chunks - 1)
        def _():
            for copy in going:
                copy.wait()

    def chunk(width):
        return pl.BlockSpec((both, width), lambda i: (i, 0))

    anywhere = pl.BlockSpec(memory_space=pl.ANY)
    return pl.pallas_call(
        kernel,
        grid=(chunks,),
        in_specs=[anywhere] * count
        + [chunk(s.shape[1]) for s in streams]
        + [pl.BlockSpec((per, D), lambda i, k=k: (0, k)) for k in range(3)],
        out_specs=tuple([chunk(w) for w in outs] + [anywhere] * count),
        out_shape=tuple(
            [jax.ShapeDtypeStruct((count * tok, w), bf16) for w in outs]
            + [jax.ShapeDtypeStruct((tok, wide), bf16)] * count
        ),
        scratch_shapes=[
            pltpu.VMEM((count * tok, wide), bf16),
            pltpu.VMEM((count * tok, wide), bf16),
            pltpu.SemaphoreType.DMA((count,)),
            pltpu.SemaphoreType.DMA((count,)),
        ],
        compiler_params=pltpu.CompilerParams(vmem_limit_bytes=VMEM_LIMIT),
        cost_estimate=pl.CostEstimate(
            flops=6 * count * tok * per * D, bytes_accessed=0, transcendentals=0
        ),
        name=name,
    )(*rows, *streams, weights, weights, weights)


def ffn_forward(rows, weights):
    def body(x, _, w_refs, out_refs):
        act_ref, gelu_ref, slope_ref = out_refs
        gate = contract(x, w_refs[0][...], 1, 1)
        up = contract(x, w_refs[1][...], 1, 1)
        gelu, slope = gelu_parts(gate)
        act = (gelu * up).astype(bf16)
        act_ref[...] = act
        gelu_ref[...] = gelu.astype(bf16)
        slope_ref[...] = (slope * up).astype(bf16)
        return contract(act, w_refs[2][...], 1, 0).astype(bf16)

    per = weights.shape[0]
    act, gelu, slope, *parts = ffn_call("ffn_forward", body, rows, [], weights, [per] * 3)
    return act, gelu, slope, parts


def ffn_backward(rows, gelu, slope, weights):
    per = weights.shape[0]

    def body(x, stream_refs, w_refs, out_refs):
        gelu_ref, slope_ref = stream_refs
        d_act = contract(x, w_refs[2][...], 1, 1)
        d_gate = (d_act * slope_ref[...].astype(f32)).astype(bf16)
        d_up = (d_act * gelu_ref[...].astype(f32)).astype(bf16)
        out_refs[0][:, :per] = d_gate
        out_refs[0][:, per:] = d_up
        return (contract(d_gate, w_refs[0][...], 1, 0) + contract(d_up, w_refs[1][...], 1, 0)).astype(bf16)

    d_both, *parts = ffn_call("ffn_backward", body, rows, [gelu, slope], weights, [2 * per])
    return d_both, parts


def unit_grads(units, per, rows):
    parts, count = len(units), len(rows)
    tokens, wide = sum(u.shape[0] for u in units), units[0].shape[1]
    n = wide // per

    def body(*refs):
        unit_refs, row_refs = refs[:parts], refs[parts : parts + count]
        out_ref, held, sems = refs[parts + count :]
        copies = gather_rows(row_refs, held, sems)

        @pl.when(pl.program_id(0) == 0)
        def _():
            for copy in copies:
                copy.start()
            for copy in copies:
                copy.wait()

        total, at = None, 0
        for ref in unit_refs:
            part = contract(ref[...], held[at : at + ref.shape[0], :], 0, 0)
            total = part if total is None else total + part
            at += ref.shape[0]
        out_ref[...] = total.astype(bf16)

    return pl.pallas_call(
        body,
        grid=(n,),
        in_specs=[pl.BlockSpec((u.shape[0], per), lambda i: (0, i)) for u in units]
        + [pl.BlockSpec(memory_space=pl.ANY)] * count,
        out_specs=pl.BlockSpec((per, D), lambda i: (0, i)),
        out_shape=jax.ShapeDtypeStruct((per, n * D), bf16),
        scratch_shapes=[pltpu.VMEM((tokens, D), bf16), pltpu.SemaphoreType.DMA((count,))],
        compiler_params=pltpu.CompilerParams(vmem_limit_bytes=VMEM_LIMIT),
        cost_estimate=pl.CostEstimate(
            flops=2 * tokens * wide * D, bytes_accessed=0, transcendentals=0
        ),
        name="unit_grads",
    )(*units, *rows)


def after_ffn(out_parts, middle, cotangent, g_fpost):
    terms = len(out_parts)

    def body(*refs):
        mid_ref, cot_ref, g_ref, mixed_ref, d_ref, dg_ref = refs[terms:]
        total = refs[0][...].astype(f32)
        for ref in refs[1:terms]:
            total = total + ref[...].astype(f32)
        unit, scale = normed(total)
        mixed_ref[...] = (mid_ref[...] + unit * g_ref[...]).astype(bf16)
        upstream = cot_ref[...].astype(f32)
        dg_ref[...] = jnp.sum(upstream * unit, axis=0, keepdims=True)
        d_ref[...] = norm_back(unit, scale, upstream * g_ref[...]).astype(bf16)

    shape = out_parts[0].shape
    return run(
        "after_ffn",
        body,
        [*out_parts, middle, cotangent, g_fpost],
        "v" * (terms + 3),
        [(shape, bf16), (shape, bf16), ((1, D), f32)],
    )


def query_side(flat, d_query, raw, cosine, sine, g_q, a, w_qkv, heads, d_attn_out):
    tok = a.shape[0]
    wide = H * HD

    def body(
        dq_ref, raw_ref, cos_ref, sin_ref, g_ref, a_ref, w_ref, o_ref, dout_ref,
        lines, da_ref, dg_ref, low, grad, grad_o,
    ):
        cos, sin = cos_ref[...], sin_ref[...]
        dg = jnp.zeros((1, HD), f32)
        for h in range(H):
            cols = slice(h * HD, (h + 1) * HD)
            unit, scale = normed(raw_ref[:, cols])
            turned = rotate(dq_ref[:, cols], cos, -sin)
            dg = dg + jnp.sum(turned * unit, axis=0, keepdims=True)
            low[:, cols] = norm_back(unit, scale, turned * g_ref[...]).astype(bf16)
        dg_ref[...] = dg
        da_ref[...] = contract(low[...], w_ref[:, :wide], 1, 1)
        grad[...] = contract(a_ref[...], low[...], 0, 0)
        for j in range(wide // LANES):
            lines[pl.ds(j, D, stride=flat.q_across), :] = grad[:, j * LANES : (j + 1) * LANES]
        grad_o[...] = contract(o_ref[...], dout_ref[...], 0, 0)
        for j in range(flat.o_across):
            lines[pl.ds(flat.q_lines + j, wide, stride=flat.o_across), :] = grad_o[
                :, j * LANES : (j + 1) * LANES
            ]
        lines[flat.q_lines + flat.o_lines :, :] = jnp.zeros((16, LANES), f32)

    return run(
        "query_side",
        body,
        [d_query, raw, cosine, sine, g_q, a, w_qkv, heads, d_attn_out],
        "v" * 9,
        [((flat.q_lines + flat.o_lines + 16, LANES), f32), ((tok, D), f32), ((1, HD), f32)],
        [pltpu.VMEM((tok, wide), bf16), pltpu.VMEM((D, wide), f32), pltpu.VMEM((wide, D), f32)],
    )


def last_part(
    flat, order, groups, lines, kv_parts, raw, cosine, sine, g_k, a, w_qkv, tokens, g_pre, d_middle,
    da_query, gain_grads,
):
    tok = a.shape[0]
    terms = len(kv_parts)
    wide = H * HD
    each = flat.devices // groups

    def body(order_ref, lines_ref, *refs):
        kv_refs = refs[:terms]
        (
            raw_ref, cos_ref, sin_ref, gk_ref, a_ref, w_ref, tok_ref, gpre_ref, dmid_ref, da_ref,
            dgq, dgpost, dgfpre, dgfpost, in_ref, *outs, held, grad, gains, blocks, sems,
        ) = refs[terms:]
        q_copy = pltpu.make_async_copy(
            lines_ref.at[: flat.q_lines], held.at[: flat.q_lines], sems.at[0]
        )
        o_copy = pltpu.make_async_copy(
            lines_ref.at[flat.q_lines :], held.at[flat.q_lines :], sems.at[1]
        )
        q_copy.start()
        o_copy.start()
        d_kv = kv_refs[0][...].astype(f32)
        for ref in kv_refs[1:]:
            d_kv = d_kv + ref[...].astype(f32)
        unit, scale = normed(raw_ref[:, wide:])
        turned = rotate(d_kv[:, :HD], cos_ref[...], -sin_ref[...])
        dgk = jnp.sum(turned * unit, axis=0, keepdims=True)
        low = jnp.concatenate(
            [norm_back(unit, scale, turned * gk_ref[...]).astype(bf16), d_kv[:, HD:].astype(bf16)],
            axis=1,
        )
        grad[...] = contract(a_ref[...], low, 0, 0)
        d_a = da_ref[...] + contract(low, w_ref[:, wide:], 1, 1)
        unit, scale = normed(tok_ref[...].astype(f32))
        dgpre = jnp.sum(d_a * unit, axis=0, keepdims=True)
        in_ref[...] = (dmid_ref[...] + norm_back(unit, scale, d_a * gpre_ref[...])).astype(bf16)
        gains[...] = jnp.zeros_like(gains)
        at = 0
        for value in (dgpre, dgq[...], dgk, dgpost[...], dgfpre[...], dgfpost[...]):
            for i in range(value.shape[1] // LANES):
                gains[at : at + 1, :] = value[:, i * LANES : (i + 1) * LANES]
                at += 1
        q_copy.wait()
        for j in range(2 * HD // LANES):
            held[pl.ds(wide // LANES + j, D, stride=flat.q_across), :] = grad[
                :, j * LANES : (j + 1) * LANES
            ]
        o_copy.wait()
        for i in range(flat.devices):
            at = i * flat.lines
            blocks[i, : flat.gain_at, :] = held[at : at + flat.gain_at, :].astype(bf16)
            at = flat.gain_line(i)
            blocks[i, flat.gain_at :, :] = gains[at : at + 16, :].astype(bf16)
        copies = [
            pltpu.make_async_copy(
                blocks.at[order_ref[k]], outs[k // each].at[k % each], sems.at[2 + k]
            )
            for k in range(flat.devices)
        ]
        for copy in copies:
            copy.start()
        for copy in copies:
            copy.wait()

    return run(
        "last_part",
        body,
        [order, lines, *kv_parts, raw, cosine, sine, g_k, a, w_qkv, tokens, g_pre, d_middle]
        + [da_query, *gain_grads],
        "sh" + "v" * (terms + 14),
        [((tok, D), bf16)] + [((each, flat.rows, LANES), bf16)] * groups,
        [
            pltpu.VMEM(lines.shape, f32),
            pltpu.VMEM((D, 2 * HD), f32),
            pltpu.VMEM((-(-(flat.gain_lines + 16) // 8) * 8, LANES), f32),
            pltpu.VMEM((flat.devices, flat.rows, LANES), bf16),
            pltpu.SemaphoreType.DMA((2 + flat.devices,)),
        ],
        "v" + "h" * groups,
    )


class Ways:
    def __init__(self, sizes):
        self.sizes = sizes
        self.what = ""

    def size(self, axis):
        if isinstance(axis, str):
            return self.sizes[axis]
        n = 1
        for a in axis:
            n *= self.sizes[a]
        return n

    def fro(self, value, axis, offset):
        n = self.size(axis)
        if offset % n == 0:
            return value
        with jax.named_scope(self.what + "_" + "".join(axis) + str(offset)):
            return lax.ppermute(value, axis, [((i + offset) % n, i) for i in range(n)])

    def places(self):
        nx, ny = self.sizes["x"], self.sizes["y"]
        return [(ox, oy) for ox in range(nx) for oy in range(ny)]

    def outers(self):
        return [(ou, ov) for ou in range(self.sizes["u"]) for ov in range(self.sizes["v"])]

    def plane_gather(self, value, beside=None):
        nx, ny = self.sizes["x"], self.sizes["y"]
        half = halfway(value.shape[0])
        found = {(0, 0): value}
        for ox in range(1, nx):
            found[ox, 0] = self.fro(value, "x", ox)
        for oy in range(1, ny):
            found[0, oy] = self.fro(value, "y", oy)
        if beside is not None:
            found, beside = lax.optimization_barrier((found, beside))
        for ox in range(1, nx):
            for oy in range(1, ny):
                first = self.fro(found[ox, 0][:half], "y", oy)
                second = self.fro(found[0, oy][half:], "x", ox)
                found[ox, oy] = jnp.concatenate([first, second], axis=0)
        found = {at: [block, self.fro(block, "c", 1)] for at, block in found.items()}
        return found if beside is None else (found, beside)

    def plane_scatter(self, parts, beside=None):
        nx, ny = self.sizes["x"], self.sizes["y"]
        low = {
            at: add_low(parts[at][0], self.fro(parts[at][1], "c", 1))
            for at in sorted(parts, reverse=True)
        }
        half = halfway(low[0, 0].shape[0])
        along_x = {ox: [low[ox, 0][:half]] for ox in range(1, nx)}
        along_y = {oy: [low[0, oy][half:]] for oy in range(1, ny)}
        for ox in range(1, nx):
            for oy in range(1, ny):
                along_x[ox].append(self.fro(low[ox, oy][:half], "y", -oy))
                along_y[oy].append(self.fro(low[ox, oy][half:], "x", -ox))
        by_x = {
            ox: jnp.concatenate([add_low(*v), low[ox, 0][half:]], axis=0) for ox, v in along_x.items()
        }
        by_y = {
            oy: jnp.concatenate([low[0, oy][:half], add_low(*v)], axis=0) for oy, v in along_y.items()
        }
        if beside is not None:
            by_x, by_y, beside = lax.optimization_barrier((by_x, by_y, beside))
        terms = [low[0, 0]]
        terms += [self.fro(v, "x", -ox) for ox, v in by_x.items()]
        terms += [self.fro(v, "y", -oy) for oy, v in by_y.items()]
        return terms if beside is None else (terms, beside)

    def z_begin(self, value):
        n = self.sizes["z"]
        if n != 4:
            return ()
        return self.fro(value, "z", 1), self.fro(value, "z", -1)

    def z_end(self, value, begun, halves=None):
        n = self.sizes["z"]
        if n != 4:
            return [self.fro(value, "z", oz) for oz in range(n)]
        above, below = begun
        half = halfway(value.shape[0])
        first, second = self.fro(above[:half], "z", 1), self.fro(below[half:], "z", -1)
        return [value, above, jnp.concatenate([first, second], axis=0), below]

    def z_gather(self, value):
        return self.z_end(value, self.z_begin(value))

    def z_pair(self, one, other, begun_one, begun_other):
        if self.sizes["z"] != 4:
            return self.z_end(one, ()), self.z_end(other, ())
        far_one = self.fro(begun_one[0], "z", 1)
        far_other = self.fro(begun_other[1], "z", -1)
        return [one, begun_one[0], far_one, begun_one[1]], [
            other, begun_other[0], far_other, begun_other[1]
        ]

    def z_scatter_begin(self, far):
        if self.sizes["z"] != 4:
            return ()
        half = halfway(far.shape[0])
        return self.fro(far[:half], "z", -1), self.fro(far[half:], "z", 1)

    def z_scatter_go(self, parts, begun):
        n = self.sizes["z"]
        if n != 4:
            return [self.fro(parts[oz], "z", -oz) for oz in range(1, n)]
        half = halfway(parts[0].shape[0])
        above = jnp.concatenate([add_low(parts[1][:half], begun[0]), parts[1][half:]], axis=0)
        below = jnp.concatenate([parts[3][:half], add_low(parts[3][half:], begun[1])], axis=0)
        return [self.fro(above, "z", -1), self.fro(below, "z", 1)]

    def z_scatter(self, parts):
        return [parts[0], *self.z_scatter_go(parts, self.z_scatter_begin(parts[len(parts) // 2]))]


SEQ = ("u", "y", "c")
CTX = ("z", "v", "x")
ACROSS = ("v", "x")


def make_shards(sizes):
    ways = Ways(sizes)
    ns, nctx, nx = ways.size(SEQ), ways.size(CTX), ways.size(ACROSS)
    nz, nc = sizes["z"], sizes["c"]
    devices = ns * nctx
    places, outers = ways.places(), ways.outers()

    def from_outers(value):
        if len(outers) == 1:
            return value
        return jnp.concatenate(
            [ways.fro(ways.fro(value, "u", ou), "v", ov) for ou, ov in outers], axis=0
        )

    def to_outers(value):
        if len(outers) == 1:
            return value
        rows = value.shape[0] // len(outers)
        return add_low(
            *[
                ways.fro(ways.fro(value[i * rows : (i + 1) * rows], "u", -ou), "v", -ov)
                for i, (ou, ov) in enumerate(outers)
            ]
        )

    def plane_rows(value):
        found = ways.plane_gather(value)
        return [block for p in places for block in found[p]]

    def by_device(parts):
        return {p: parts[i * nc : (i + 1) * nc] for i, p in enumerate(places)}

    def own_units(grad):
        return lax.psum_scatter(to_outers(grad), "z", scatter_dimension=0, tiled=True)

    def shards(
        tokens, cotangent, segments, positions, attn_w, attn_m, attn_v,
        mlp_w, mlp_m, mlp_v, gains, gain_m, gain_v,
    ):
        at = {a: lax.axis_index(a) for a in sizes}
        seq_place = lax.axis_index(SEQ)
        across_place = lax.axis_index(ACROSS)
        ctx_place = at["z"] * nx + across_place
        device = seq_place * nctx + ctx_place
        piece, gain_piece = attn_w.shape[0], gains.shape[0]
        flat = Flat(piece, gain_piece, devices)

        sides = [sizes[a] for a in ("x", "y", "c", "u", "v", "z")]
        here = [at[a] for a in ("x", "y", "c", "u", "v", "z")]
        ox, oy, oc, ou, ov, oz = (
            (jnp.asarray(o, jnp.int32) + h) % n
            for o, h, n in zip(np.unravel_index(np.arange(devices), sides), here, sides)
        )
        order = ((ou * sizes["y"] + oy) * sizes["c"] + oc) * nz + oz
        order = (order * sizes["v"] + ov) * sizes["x"] + ox

        ways.what = "attn_gather"
        gain_offset = gain_piece * device % LANES
        gain_window = lax.dynamic_update_slice(
            jnp.zeros((16 * LANES,), bf16), gains.astype(bf16), (gain_offset,)
        )
        low_piece = jnp.concatenate(
            [
                jnp.pad(
                    attn_w.astype(bf16).reshape(flat.lines, LANES),
                    ((0, flat.gain_at - flat.lines), (0, 0)),
                ),
                gain_window.reshape(16, LANES),
            ],
            axis=0,
        )
        line_blocks = ways.z_gather(low_piece)

        ways.what = "unit_exchange"
        units, width = mlp_w.shape
        share = units // ns
        held = -(-share // 32) * 32

        def seq_send(by_place):
            return [
                ways.fro(
                    lax.dynamic_index_in_dim(by_place, (seq_place - offset) % ns, 0, keepdims=False),
                    SEQ,
                    offset,
                )
                for offset in range(ns)
            ]

        def seq_place_all(heard):
            kept = jnp.zeros((ns,) + heard[0].shape, heard[0].dtype)
            for offset, value in enumerate(heard):
                kept = lax.dynamic_update_index_in_dim(kept, value, (seq_place + offset) % ns, 0)
            return kept

        heard = seq_send(mlp_w.astype(bf16).reshape(ns, share, width))
        line_blocks, heard = lax.optimization_barrier((line_blocks, heard))
        by_cols = seq_place_all(heard)
        rows_own = jnp.concatenate([by_cols[i] for i in range(ns)], axis=1)
        rows_own = jnp.pad(rows_own, ((0, held - share), (0, 0)))
        ways.what = "attn_gather"
        line_z = from_outers(jnp.concatenate(line_blocks, axis=0))
        gathered = ways.plane_gather(line_z)
        line_parts = [part.reshape(-1, flat.rows, LANES) for p in places for part in gathered[p]]
        units_here = from_outers(lax.all_gather(rows_own, "z", axis=0, tiled=True))

        tok_rows = tokens.shape[1]
        cosine, sine = angles(positions[0])
        (
            w_qkv, g_pre, g_q, g_k, g_post, g_fpre, g_fpost, normed_in, query, kv_local, raw,
        ) = first_part(flat, line_parts, order, tokens[0], cosine, sine)
        w_out = spread_out(flat, [after(part, kv_local) for part in line_parts], order)
        ways.what = "kv_gather"
        kv_all = jnp.stack(
            [ways.fro(block, ACROSS, oa) for block in ways.z_gather(kv_local) for oa in range(nx)]
        )

        doc_all = segments[0]
        first_docs, last_docs = doc_all[::tok_rows], doc_all[tok_rows - 1 :: tok_rows]
        key_at = np.arange(nctx)
        key_place = (at["z"] + jnp.asarray(key_at // nx, jnp.int32)) % nz * nx
        key_place = key_place + (across_place + jnp.asarray(key_at % nx, jnp.int32)) % nx
        is_place = key_place[:, None] == jnp.arange(nctx, dtype=jnp.int32)[None, :]
        key_first = jnp.sum(jnp.where(is_place, first_docs[None, :], 0), axis=1)
        key_last = jnp.sum(jnp.where(is_place, last_docs[None, :], 0), axis=1)
        live = (key_place < ctx_place) & (key_last >= key_first[0])
        one_doc = key_first == key_last[0]
        task = jnp.where(live, jnp.where(one_doc, WHOLE, MASKED), DEAD)
        task = jnp.where(key_place == ctx_place, MASKED, task)
        info = jnp.stack([key_place, task]).astype(jnp.int32)
        key_docs = doc_all[:, None]
        query_docs = lax.dynamic_slice_in_dim(doc_all, ctx_place * tok_rows, tok_rows)[None]

        heads, log_total, attn_out, middle, ffn_in = attend(
            info, query, kv_all, key_docs, query_docs, w_out, tokens[0], g_post, g_fpre
        )

        ways.what = "ffn_in_gather"
        ffn_rows = plane_rows(ffn_in)
        act, gelu, slope, parts = ffn_forward(ffn_rows, units_here)
        ways.what = "ffn_out_sum"
        out_parts = ways.plane_scatter(by_device(parts))
        mixed, d_mlp_out, d_gfpost = after_ffn(out_parts, middle, cotangent[0], g_fpost)

        ways.what = "d_out_gather"
        d_out_rows = plane_rows(d_mlp_out)
        held_here = units_here.shape[0]
        d_w_down = unit_grads([act], held_here, d_out_rows)
        ways.what = "ffn_grad_sum"
        owned_down = own_units(d_w_down)
        d_out_rows[0] = after(d_out_rows[0], d_w_down)
        d_both, parts = ffn_backward(d_out_rows, gelu, slope, units_here)
        ways.what = "d_in_sum"
        d_in_parts, d_both = ways.plane_scatter(by_device(parts), d_both)

        d_w_gate_up = unit_grads([d_both], held_here, ffn_rows)
        owned_gate_up = own_units(d_w_gate_up)
        d_in_parts = lax.optimization_barrier((d_in_parts, d_w_gate_up))[0]

        d_query, d_kv, d_attn_out, d_middle, d_gfpre, d_gpost = attend_back(
            info, query, kv_all, key_docs, query_docs, heads, log_total, d_in_parts, middle, attn_out,
            cotangent[0], w_out, g_post, g_fpre,
        )
        ways.what = "kv_sum"
        d_kv = d_kv.reshape(nz, nx, tok_rows, 2 * HD)

        def across(oz):
            return [ways.fro(d_kv[oz, oa], ACROSS, -oa) for oa in range(nx)]

        far = nz // 2
        kv_parts = {far: add_low(*across(far))}
        near = {oz: across(oz) for oz in range(nz) if oz != far}
        begun = ways.z_scatter_begin(kv_parts[far])
        if begun:
            begun, near = lax.optimization_barrier((begun, near))
        near[0], owned_down = lax.optimization_barrier((near[0], owned_down))
        kv_parts.update({oz: add_low(*terms) for oz, terms in near.items()})
        kv_parts = [kv_parts[0], *ways.z_scatter_go(kv_parts, begun)]
        lines, da_query, d_gq = query_side(
            flat, d_query, raw, cosine, sine, g_q, normed_in, w_qkv, heads, d_attn_out
        )
        input_grad, *packed = last_part(
            flat, order, len(places) * nc, lines, kv_parts, raw, cosine, sine, g_k, normed_in, w_qkv, tokens[0],
            g_pre, d_middle, da_query, [d_gq, d_gpost, d_gfpre, d_gfpost],
        )

        ways.what = "attn_grad_sum"
        packed = [part.reshape(-1, LANES) for part in packed]
        terms, owned_gate_up = ways.plane_scatter(
            {p: packed[i * nc : (i + 1) * nc] for i, p in enumerate(places)}, owned_gate_up
        )
        own_rows = jnp.concatenate([owned_gate_up[:share], owned_down[:share]], axis=1)
        by_cols = jnp.stack([own_rows[:, i * width : (i + 1) * width] for i in range(ns)])
        terms, by_cols = lax.optimization_barrier((terms, by_cols))
        plane_sum = to_outers(add_low(*terms))

        ways.what = "grad_exchange"
        mlp_red = seq_place_all(seq_send(by_cols)).astype(f32).reshape(units, width)
        mlp_m_new, mlp_v_new, mlp_new = adam_update(
            mlp_w, mlp_m, mlp_v, mlp_red, RATE_MATRIX, DECAY_MATRIX
        )

        ways.what = "attn_grad_sum"
        terms = ways.z_scatter([plane_sum[oz * flat.rows : (oz + 1) * flat.rows] for oz in range(nz)])
        terms, mlp_new = lax.optimization_barrier((terms, mlp_new))
        red = sum(part.astype(f32) for part in terms)
        attn_red = red[: flat.lines].reshape(-1)
        gain_red = lax.dynamic_slice(red[flat.gain_at :].reshape(-1), (gain_offset,), (gain_piece,))

        attn_m_new, attn_v_new, attn_new = adam_update(
            attn_w, attn_m, attn_v, attn_red, RATE_MATRIX, DECAY_MATRIX
        )
        gain_m_new, gain_v_new, gain_new = adam_update(
            gains, gain_m, gain_v, gain_red, RATE_GAIN, 0.0
        )
        return (
            mixed[None], input_grad[None],
            attn_red, attn_m_new, attn_v_new, attn_new,
            mlp_red, mlp_m_new, mlp_v_new, mlp_new,
            gain_red, gain_m_new, gain_v_new, gain_new,
        )

    return shards


def solution(mesh):
    seq, ctx = mesh.shape["seq"], mesh.shape["ctx"]
    nz = 4 if ctx % 4 == 0 else 1
    chips_y, chips_x = seq // 2, ctx // nz
    y, x = 2 - chips_y % 2, 2 - chips_x % 2
    sizes = {"u": chips_y // y, "y": y, "c": 2, "z": nz, "v": chips_x // x, "x": x}
    fine = Mesh(mesh.devices.reshape(*sizes.values()), tuple(sizes))
    s, x = SEQ, CTX
    both = s + x
    in_specs = (
        P(s, x, None), P(s, x, None), P(s, None), P(s, x),
        P(both), P(both), P(both),
        P(x, s), P(x, s), P(x, s),
        P(both), P(both), P(both),
    )
    out_specs = (
        P(s, x, None), P(s, x, None),
        P(both), P(both), P(both), P(both),
        P(x, s), P(x, s), P(x, s), P(x, s),
        P(both), P(both), P(both), P(both),
    )
    return jax.shard_map(
        make_shards(sizes), mesh=fine, in_specs=in_specs, out_specs=out_specs, check_vma=False
    )
```

```python
import jax
import jax.numpy as jnp
import numpy as np
from jax import lax
from jax.experimental import pallas as pl
from jax.experimental.pallas import tpu as pltpu
from jax.sharding import Mesh, PartitionSpec as P

D = 1152
H = 4
HD = 256
STEP = 5

NORM_EPS = 1e-06
SCORE_FLOOR = -1e30
ROPE_BASE = 1000000.0
BETA_MOMENT = 0.5
ADAM_EPS = 1e-08
RATE_MATRIX = 0.03
RATE_GAIN = 0.5
DECAY_MATRIX = 0.1

bf16 = jnp.bfloat16
f32 = jnp.float32
LANES = 128


def normed(value):
    factor = lax.rsqrt(jnp.mean(value * value, axis=-1, keepdims=True) + NORM_EPS)
    return (value * factor, factor)


def norm_back(unit, factor, d_unit):
    return factor * (d_unit - unit * jnp.mean(d_unit * unit, axis=-1, keepdims=True))


def angles(position):
    half_index = jnp.arange(HD // 2, dtype=f32)
    frequency = jnp.exp(half_index * (-2.0 * jnp.log(ROPE_BASE) / HD))
    angle = position.astype(f32)[:, None] * frequency[None, :]
    return (jnp.cos(angle), jnp.sin(angle))


def rotate(value, cosine, sine):
    half_width = value.shape[-1] // 2
    first_half = value[..., :half_width]
    second_half = value[..., half_width:]
    return jnp.concatenate(
        [first_half * cosine - second_half * sine, second_half * cosine + first_half * sine],
        axis=-1,
    )


def contract(left, right, left_dim, right_dim):
    return lax.dot_general(
        left, right, (((left_dim,), (right_dim,)), ((), ())), preferred_element_type=f32
    )


def adam_update(weight, moment_one, second, gradient, learn_rate, decay_rate):
    moment_new = BETA_MOMENT * moment_one + (1.0 - BETA_MOMENT) * gradient
    second_new = BETA_MOMENT * second + (1.0 - BETA_MOMENT) * gradient * gradient
    correction = 1.0 - BETA_MOMENT**STEP
    update = moment_new / correction / (jnp.sqrt(second_new / correction) + ADAM_EPS)
    return (moment_new, second_new, weight - learn_rate * (update + decay_rate * weight))


def add_low(*parts):
    total = parts[0].astype(f32)
    for part in parts[1:]:
        total = total + part.astype(f32)
    return total.astype(bf16)


def after(value, *earlier):
    return lax.optimization_barrier((value,) + earlier)[0]


def halfway(rows):
    return rows // 32 * 16 if rows >= 32 else rows // 2


VMEM_LIMIT = 56 * 1024 * 1024
SCORE_SCALE = HD ** (-0.5)
SPACES = {"v": pltpu.VMEM, "h": pl.ANY, "s": pltpu.SMEM}


def run(name, body, operands, spaces, out_shape, scratch=(), out_spaces=None, flops=0):
    return pl.pallas_call(
        body,
        out_shape=tuple(jax.ShapeDtypeStruct(s, d) for s, d in out_shape),
        in_specs=[pl.BlockSpec(memory_space=SPACES[s]) for s in spaces],
        out_specs=tuple(
            pl.BlockSpec(memory_space=SPACES[s]) for s in out_spaces or "v" * len(out_shape)
        ),
        scratch_shapes=list(scratch),
        compiler_params=pltpu.CompilerParams(vmem_limit_bytes=VMEM_LIMIT),
        cost_estimate=pl.CostEstimate(flops=flops, bytes_accessed=0, transcendentals=0),
        name=name,
    )(*operands)


class Flat:
    def __init__(self, piece, gain_piece, devices):
        self.devices = devices
        self.lines = piece // LANES
        self.gain_at = -(-self.lines // 16) * 16
        self.gain_piece = gain_piece
        self.rows = self.gain_at + 16
        self.q_across, self.o_across = (H + 2) * HD // LANES, D // LANES
        self.q_lines, self.o_lines = D * self.q_across, H * HD * self.o_across
        widths = [D, HD, HD, D, D, D]
        self.gain_rows = [w // LANES for w in widths]
        self.gain_lines = sum(self.gain_rows)

        across, kv = self.q_across, 2 * HD // LANES
        self.kv_across = kv
        self.late_rows = self.lines // across + (2 if self.lines % across else 0)
        self.late_lines = -(-self.late_rows * kv // 16) * 16

    def first_row(self, device):
        return self.lines * device // self.q_across

    def gain_line(self, device):
        return self.gain_piece * device // LANES


def fetch(order_ref, sources, held, sems):
    copies = []
    for source in sources:
        for i in range(source.shape[0]):
            k = len(copies)
            copies.append(pltpu.make_async_copy(source.at[i], held.at[order_ref[k]], sems.at[k]))
    for copy in copies:
        copy.start()
    return copies


def first_part(flat, parts, order, tokens, cosine, sine):
    tok_rows = tokens.shape[0]
    wide = (H + 2) * HD
    blocks = -(-flat.q_lines // flat.lines)

    def body(order_ref, *refs):
        sources = refs[: len(parts)]
        (
            tok_ref, cos_ref, sin_ref, w_ref, g_pre, g_q, g_k, g_post, g_fpre, g_fpost,
            a_ref, q_ref, kv_ref, raw_ref, held, lines, gains, sems,
        ) = refs[len(parts) :]
        copies = fetch(order_ref, sources, held, sems)
        unit, _ = normed(tok_ref[...].astype(f32))
        gains[...] = jnp.zeros_like(gains)
        for copy in copies:
            copy.wait()
        for i in range(flat.devices):
            at = flat.gain_line(i)
            gains[at : at + 3, :] += held[i, flat.gain_at :, :].astype(f32)[:3]
        at = 0
        for ref, rows in zip((g_pre, g_q, g_k, g_post, g_fpre, g_fpost), flat.gain_rows):
            for i in range(rows):
                ref[:, i * LANES : (i + 1) * LANES] = gains[at + i : at + i + 1, :]
            at += rows
        a_ref[...] = (unit * g_pre[...]).astype(bf16)
        for i in range(blocks):
            lines[i * flat.lines : (i + 1) * flat.lines, :] = held[i, : flat.gain_at, :].astype(f32)[
                : flat.lines
            ]
        for j in range(flat.q_across):
            w_ref[:, j * LANES : (j + 1) * LANES] = lines[
                pl.ds(j, D, stride=flat.q_across), :
            ].astype(bf16)
        qkv = contract(a_ref[...], w_ref[...], 1, 0)
        raw_ref[...] = qkv[:, : (H + 1) * HD]
        cos, sin = cos_ref[...], sin_ref[...]
        for h in range(H):
            head = normed(qkv[:, h * HD : (h + 1) * HD])[0] * g_q[...]
            low = rotate(head, cos, sin).astype(bf16)
            q_ref[:, h * HD : (h + 1) * HD] = (low.astype(f32) * SCORE_SCALE).astype(bf16)
        key = normed(qkv[:, H * HD : (H + 1) * HD])[0] * g_k[...]
        kv_ref[:, :HD] = rotate(key, cos, sin).astype(bf16)
        kv_ref[:, HD:] = qkv[:, (H + 1) * HD :].astype(bf16)

    row = [((1, w * LANES), f32) for w in flat.gain_rows]
    return run(
        "first_part",
        body,
        [order, *parts, tokens, cosine, sine],
        "s" + "h" * len(parts) + "vvv",
        [((D, wide), bf16), *row]
        + [((tok_rows, D), bf16), ((tok_rows, H * HD), bf16), ((tok_rows, 2 * HD), bf16)]
        + [((tok_rows, (H + 1) * HD), f32)],
        [
            pltpu.VMEM((flat.devices, flat.rows, LANES), bf16),
            pltpu.VMEM((blocks * flat.lines, LANES), f32),
            pltpu.VMEM((-(-(flat.gain_lines + 3) // 8) * 8, LANES), f32),
            pltpu.SemaphoreType.DMA((flat.devices,)),
        ],
        flops=8 * 2 * tok_rows * D * wide,
    )


def spread_out(flat, parts, order):
    start = flat.q_lines // flat.lines

    def body(order_ref, *refs):
        sources = refs[: len(parts)]
        w_ref, held, lines, sems = refs[len(parts) :]
        for copy in fetch(order_ref, sources, held, sems):
            copy.wait()
        for i in range(start, flat.devices):
            at = (i - start) * flat.lines
            lines[at : at + flat.lines, :] = held[i, : flat.gain_at, :].astype(f32)[: flat.lines]
        for j in range(flat.o_across):
            w_ref[:, j * LANES : (j + 1) * LANES] = lines[
                pl.ds(flat.q_lines - start * flat.lines + j, H * HD, stride=flat.o_across), :
            ].astype(bf16)

    return run(
        "spread_out",
        body,
        [order, *parts],
        "s" + "h" * len(parts),
        [((H * HD, D), bf16)],
        [
            pltpu.VMEM((flat.devices, flat.rows, LANES), bf16),
            pltpu.VMEM(((flat.devices - start) * flat.lines, LANES), f32),
            pltpu.SemaphoreType.DMA((flat.devices,)),
        ],
    )[0]


DEAD, WHOLE, MASKED = 0, 1, 2


def allowed_of(kdoc_ref, qdoc_ref, shift):
    keys, queries = kdoc_ref.shape[0], qdoc_ref.shape[1]
    key_at = lax.broadcasted_iota(jnp.int32, (keys, queries), 0) + shift
    query_at = lax.broadcasted_iota(jnp.int32, (keys, queries), 1)
    return (kdoc_ref[...] == qdoc_ref[...]) & (key_at <= query_at)


def same(shape):
    return pl.BlockSpec(shape, lambda i, info: (0,) * len(shape))


def attend(info, query, kv, key_docs, query_docs, w_out, tokens, g_post, g_fpre):
    blocks, rows, _ = kv.shape

    def body(
        info_ref, q_ref, kv_ref, kdoc_ref, qdoc_ref, w_ref, tok_ref, g_post_ref, g_fpre_ref,
        o_ref, lse_ref, out_ref, mid_ref, in_ref, peak, total, acc,
    ):
        step = pl.program_id(0)

        @pl.when(step == 0)
        def _():
            peak[...] = jnp.full_like(peak, SCORE_FLOOR)
            total[...] = jnp.zeros_like(total)
            acc[...] = jnp.zeros_like(acc)

        def visit(masked):
            key = kv_ref[0, :, :HD]
            value_t = kv_ref[0, :, HD:].T
            if masked:
                allowed = allowed_of(
                    kdoc_ref, qdoc_ref, (info_ref[0, step] - info_ref[0, 0]) * rows
                )
            for h in range(H):
                score = contract(key, q_ref[:, h * HD : (h + 1) * HD], 1, 1)
                if masked:
                    score = jnp.where(allowed, score, SCORE_FLOOR)
                old = peak[h : h + 1, :]
                new = jnp.maximum(old, jnp.max(score, axis=0, keepdims=True))
                weight = jnp.exp(score - new)
                shrink = jnp.exp(old - new)
                peak[h : h + 1, :] = new
                total[h : h + 1, :] = total[h : h + 1, :] * shrink + jnp.sum(
                    weight, axis=0, keepdims=True
                )
                acc[h] = acc[h] * shrink + contract(value_t, weight.astype(bf16), 1, 0)

        pl.when(info_ref[1, step] == WHOLE)(lambda: visit(False))
        pl.when(info_ref[1, step] == MASKED)(lambda: visit(True))

        @pl.when(step == blocks - 1)
        def _():
            lse_ref[...] = jnp.zeros_like(lse_ref)
            for h in range(H):
                lse_ref[h : h + 1, :] = peak[h : h + 1, :] + jnp.log(total[h : h + 1, :])
                o_ref[:, h * HD : (h + 1) * HD] = (acc[h] / total[h : h + 1, :]).T.astype(bf16)
            attn_out = contract(o_ref[...], w_ref[...], 1, 0)
            out_ref[...] = attn_out
            middle = tok_ref[...].astype(f32) + normed(attn_out)[0] * g_post_ref[...]
            mid_ref[...] = middle
            in_ref[...] = (normed(middle)[0] * g_fpre_ref[...]).astype(bf16)

    return pl.pallas_call(
        body,
        grid_spec=pltpu.PrefetchScalarGridSpec(
            num_scalar_prefetch=1,
            grid=(blocks,),
            in_specs=[
                same((rows, H * HD)),
                pl.BlockSpec((1, rows, 2 * HD), lambda i, info: (i, 0, 0)),
                pl.BlockSpec((rows, 1), lambda i, info: (info[0, i], 0)),
                same((1, rows)),
                same((H * HD, D)),
                same((rows, D)),
                same((1, D)),
                same((1, D)),
            ],
            out_specs=[
                same((rows, H * HD)),
                same((8, rows)),
                same((rows, D)),
                same((rows, D)),
                same((rows, D)),
            ],
            scratch_shapes=[
                pltpu.VMEM((8, rows), f32),
                pltpu.VMEM((8, rows), f32),
                pltpu.VMEM((H, HD, rows), f32),
            ],
        ),
        out_shape=(
            jax.ShapeDtypeStruct((rows, H * HD), bf16),
            jax.ShapeDtypeStruct((8, rows), f32),
            jax.ShapeDtypeStruct((rows, D), f32),
            jax.ShapeDtypeStruct((rows, D), f32),
            jax.ShapeDtypeStruct((rows, D), bf16),
        ),
        compiler_params=pltpu.CompilerParams(vmem_limit_bytes=VMEM_LIMIT),
        cost_estimate=pl.CostEstimate(
            flops=8 * 4 * blocks * rows * rows * H * HD, bytes_accessed=0, transcendentals=0
        ),
        name="attend",
    )(info, query, kv, key_docs, query_docs, w_out, tokens, g_post, g_fpre)


def attend_back(
    info, query, kv, key_docs, query_docs, heads, log_total, d_in, middle, attn_out, cotangent,
    w_out, g_post, g_fpre,
):
    blocks, rows, _ = kv.shape
    terms = len(d_in)

    def body(info_ref, q_ref, kv_ref, kdoc_ref, qdoc_ref, o_ref, lse_ref, *refs):
        terms_ref = refs[:terms]
        (
            mid_ref, out_ref, cot_ref, w_ref, g_post_ref, g_fpre_ref,
            dq_ref, dkv_ref, dout_ref, dmid_ref, dg_fpre_ref, dg_post_ref, do_ref, delta_ref,
        ) = refs[terms:]
        step = pl.program_id(0)

        @pl.when(step == 0)
        def _():
            d_rows = sum(ref[...].astype(f32) for ref in terms_ref)
            unit, scale = normed(mid_ref[...])
            dg_fpre_ref[...] = jnp.sum(d_rows * unit, axis=0, keepdims=True)
            d_middle = cot_ref[...].astype(f32) + norm_back(unit, scale, d_rows * g_fpre_ref[...])
            dmid_ref[...] = d_middle
            unit, scale = normed(out_ref[...])
            dg_post_ref[...] = jnp.sum(d_middle * unit, axis=0, keepdims=True)
            d_out = norm_back(unit, scale, d_middle * g_post_ref[...]).astype(bf16)
            dout_ref[...] = d_out
            delta_ref[...] = jnp.zeros_like(delta_ref)
            for h in range(H):
                cols = slice(h * HD, (h + 1) * HD)
                d_o = contract(d_out, w_ref[cols, :], 1, 1).astype(bf16)
                do_ref[:, cols] = d_o
                each = (d_o.astype(f32) * o_ref[:, cols].astype(f32)).T
                delta_ref[h : h + 1, :] = jnp.sum(each, axis=0, keepdims=True)
            dq_ref[...] = jnp.zeros_like(dq_ref)

        def visit(masked):
            key, value = kv_ref[0, :, :HD], kv_ref[0, :, HD:]
            if masked:
                allowed = allowed_of(
                    kdoc_ref, qdoc_ref, (info_ref[0, step] - info_ref[0, 0]) * rows
                )
            d_key = jnp.zeros((rows, HD), f32)
            d_value = jnp.zeros((rows, HD), f32)
            for h in range(H):
                cols = slice(h * HD, (h + 1) * HD)
                q, d_o = q_ref[:, cols], do_ref[:, cols]
                prob = jnp.exp(contract(key, q, 1, 1) - lse_ref[h : h + 1, :])
                if masked:
                    prob = jnp.where(allowed, prob, 0.0)
                d_value = d_value + contract(prob.astype(bf16), d_o, 1, 0)
                d_prob = contract(value, d_o, 1, 1)
                d_score = (prob * (d_prob - delta_ref[h : h + 1, :])).astype(bf16)
                d_key = d_key + contract(d_score, q, 1, 0)
                dq_ref[:, cols] = dq_ref[:, cols] + contract(d_score, key, 0, 0)
            dkv_ref[0, :, :HD] = d_key.astype(bf16)
            dkv_ref[0, :, HD:] = d_value.astype(bf16)

        pl.when(info_ref[1, step] == WHOLE)(lambda: visit(False))
        pl.when(info_ref[1, step] == MASKED)(lambda: visit(True))

        @pl.when(info_ref[1, step] == DEAD)
        def _():
            dkv_ref[...] = jnp.zeros_like(dkv_ref)

        @pl.when(step == blocks - 1)
        def _():
            dq_ref[...] = dq_ref[...] * SCORE_SCALE

    block = pl.BlockSpec((1, rows, 2 * HD), lambda i, info: (i, 0, 0))
    return pl.pallas_call(
        body,
        grid_spec=pltpu.PrefetchScalarGridSpec(
            num_scalar_prefetch=1,
            grid=(blocks,),
            in_specs=[
                same((rows, H * HD)),
                block,
                pl.BlockSpec((rows, 1), lambda i, info: (info[0, i], 0)),
                same((1, rows)),
                same((rows, H * HD)),
                same((8, rows)),
                *[same((rows, D))] * (terms + 3),
                same((H * HD, D)),
                same((1, D)),
                same((1, D)),
            ],
            out_specs=[
                same((rows, H * HD)),
                block,
                same((rows, D)),
                same((rows, D)),
                same((1, D)),
                same((1, D)),
            ],
            scratch_shapes=[pltpu.VMEM((rows, H * HD), bf16), pltpu.VMEM((8, rows), f32)],
        ),
        out_shape=(
            jax.ShapeDtypeStruct((rows, H * HD), f32),
            jax.ShapeDtypeStruct(kv.shape, bf16),
            jax.ShapeDtypeStruct((rows, D), bf16),
            jax.ShapeDtypeStruct((rows, D), f32),
            jax.ShapeDtypeStruct((1, D), f32),
            jax.ShapeDtypeStruct((1, D), f32),
        ),
        compiler_params=pltpu.CompilerParams(vmem_limit_bytes=VMEM_LIMIT),
        cost_estimate=pl.CostEstimate(flops=0, bytes_accessed=0, transcendentals=0),
        name="attend_back",
    )(
        info, query, kv, key_docs, query_docs, heads, log_total, *d_in, middle, attn_out, cotangent,
        w_out, g_post, g_fpre,
    )


def gelu_parts(gate):
    scale = 0.7978845608028654
    square = gate * gate
    inner = jnp.tanh(scale * gate * (1.0 + 0.044715 * square))
    half_up = 0.5 * (1.0 + inner)
    slope = half_up + 0.5 * gate * (1.0 - inner * inner) * scale * (1.0 + 3 * 0.044715 * square)
    return gate * half_up, slope


def gather_rows(refs, held, sems):
    tok = refs[0].shape[0]
    return [
        pltpu.make_async_copy(ref, held.at[k * tok : (k + 1) * tok], sems.at[k])
        for k, ref in enumerate(refs)
    ]


def scatter_rows(held, refs, sems):
    tok = refs[0].shape[0]
    return [
        pltpu.make_async_copy(held.at[k * tok : (k + 1) * tok], ref, sems.at[k])
        for k, ref in enumerate(refs)
    ]


def by_chunk(step, chunks, copies, do):
    per = len(copies) // chunks
    for k in range(chunks):

        @pl.when(step == k)
        def _(k=k):
            for copy in copies[k * per : (k + 1) * per]:
                do(copy)


def ffn_call(name, body, rows, streams, weights, outs, order):
    count, (tok, wide) = len(rows), rows[0].shape
    chunks = -(-count * tok // 512)
    both = count * tok // chunks
    blocks = len(weights)
    starts = np.cumsum([0] + [w.shape[0] for w in weights]).tolist()
    per = starts[-1]

    def kernel(*refs):
        row_refs, refs = refs[:count], refs[count:]
        stream_refs, refs = refs[: len(streams)], refs[len(streams) :]
        w_refs, refs = refs[:blocks], refs[blocks:]
        out_refs, refs = refs[: len(outs)], refs[len(outs) :]
        sum_refs, (held, given, units, sems_in, sems_out, sems_w) = refs[:count], refs[count:]
        step = pl.program_id(0)
        coming = gather_rows(row_refs, held, sems_in)
        going = scatter_rows(given, sum_refs, sems_out)
        brought = {
            k: [
                pltpu.make_async_copy(
                    ref.at[:, k * D : (k + 1) * D],
                    units.at[k, starts[i] : starts[i + 1]],
                    sems_w.at[k * blocks + i],
                )
                for i, ref in enumerate(w_refs)
            ]
            for k in order
        }

        @pl.when(step == 0)
        def _():
            first = len(coming) // chunks
            bringing = [c for k in order for c in brought[k]]
            for copy in coming[:first] + bringing + coming[first:]:
                copy.start()
            for copy in bringing:
                copy.wait()

        by_chunk(step, chunks, coming, lambda copy: copy.wait())
        here = pl.ds(pl.multiple_of(step * both, both), both)
        given[here, :] = body(held[here, :], stream_refs, units, out_refs)
        by_chunk(step, chunks, going, lambda copy: copy.start())

        @pl.when(step == chunks - 1)
        def _():
            for copy in going:
                copy.wait()

    def chunk(width):
        return pl.BlockSpec((both, width), lambda i: (i, 0))

    anywhere = pl.BlockSpec(memory_space=pl.ANY)
    return pl.pallas_call(
        kernel,
        grid=(chunks,),
        in_specs=[anywhere] * count
        + [chunk(s.shape[1]) for s in streams]
        + [anywhere] * blocks,
        out_specs=tuple([chunk(w) for w in outs] + [anywhere] * count),
        out_shape=tuple(
            [jax.ShapeDtypeStruct((count * tok, w), bf16) for w in outs]
            + [jax.ShapeDtypeStruct((tok, wide), bf16)] * count
        ),
        scratch_shapes=[
            pltpu.VMEM((count * tok, wide), bf16),
            pltpu.VMEM((count * tok, wide), bf16),
            pltpu.VMEM((3, per, D), bf16),
            pltpu.SemaphoreType.DMA((count,)),
            pltpu.SemaphoreType.DMA((count,)),
            pltpu.SemaphoreType.DMA((3 * blocks,)),
        ],
        compiler_params=pltpu.CompilerParams(vmem_limit_bytes=VMEM_LIMIT),
        cost_estimate=pl.CostEstimate(
            flops=6 * count * tok * per * D, bytes_accessed=0, transcendentals=0
        ),
        name=name,
    )(*rows, *streams, *weights)


def ffn_forward(rows, weights):
    def body(x, _, weight, out_refs):
        act_ref, gelu_ref, slope_ref = out_refs
        gate = contract(x, weight[0], 1, 1)
        up = contract(x, weight[1], 1, 1)
        gelu, slope = gelu_parts(gate)
        act = (gelu * up).astype(bf16)
        act_ref[...] = act
        gelu_ref[...] = gelu.astype(bf16)
        slope_ref[...] = (slope * up).astype(bf16)
        return contract(act, weight[2], 1, 0).astype(bf16)

    units = sum(w.shape[0] for w in weights)
    act, gelu, slope, *parts = ffn_call("ffn_forward", body, rows, [], weights, [units] * 3, (0, 1, 2))
    return act, gelu, slope, parts


def ffn_backward(rows, gelu, slope, weights):
    units = sum(w.shape[0] for w in weights)

    def body(x, stream_refs, weight, out_refs):
        gelu_ref, slope_ref = stream_refs
        d_act = contract(x, weight[2], 1, 1)
        d_gate = (d_act * slope_ref[...].astype(f32)).astype(bf16)
        d_up = (d_act * gelu_ref[...].astype(f32)).astype(bf16)
        out_refs[0][:, :units] = d_gate
        out_refs[0][:, units:] = d_up
        return (contract(d_gate, weight[0], 1, 0) + contract(d_up, weight[1], 1, 0)).astype(bf16)

    d_both, *parts = ffn_call(
        "ffn_backward", body, rows, [gelu, slope], weights, [2 * units], (2, 0, 1)
    )
    return d_both, parts


def unit_grads(units, part, blocks, per, rows):
    count = len(rows)
    tokens, both = units.shape[0], blocks * per

    def body(unit_ref, *refs):
        row_refs, out_refs, (held, sems) = refs[:count], refs[count : count + blocks], refs[-2:]
        copies = gather_rows(row_refs, held, sems)
        for copy in copies:
            copy.start()
        for copy in copies:
            copy.wait()
        total = contract(unit_ref[...], held[...], 0, 0).astype(bf16)
        for i, ref in enumerate(out_refs):
            ref[...] = total[i * per : (i + 1) * per]

    return pl.pallas_call(
        body,
        grid=(1,),
        in_specs=[pl.BlockSpec((tokens, both), lambda i: (0, part))]
        + [pl.BlockSpec(memory_space=pl.ANY)] * count,
        out_specs=[pl.BlockSpec((per, D), lambda i: (0, 0))] * blocks,
        out_shape=[jax.ShapeDtypeStruct((per, D), bf16)] * blocks,
        scratch_shapes=[pltpu.VMEM((tokens, D), bf16), pltpu.SemaphoreType.DMA((count,))],
        compiler_params=pltpu.CompilerParams(vmem_limit_bytes=VMEM_LIMIT),
        cost_estimate=pl.CostEstimate(
            flops=2 * tokens * both * D, bytes_accessed=0, transcendentals=0
        ),
        name="unit_grads",
    )(units, *rows)


def after_ffn(out_parts, middle, cotangent, g_fpost):
    terms = len(out_parts)

    def body(*refs):
        mid_ref, cot_ref, g_ref, mixed_ref, d_ref, dg_ref = refs[terms:]
        total = refs[0][...].astype(f32)
        for ref in refs[1:terms]:
            total = total + ref[...].astype(f32)
        unit, scale = normed(total)
        mixed_ref[...] = (mid_ref[...] + unit * g_ref[...]).astype(bf16)
        upstream = cot_ref[...].astype(f32)
        dg_ref[...] = jnp.sum(upstream * unit, axis=0, keepdims=True)
        d_ref[...] = norm_back(unit, scale, upstream * g_ref[...]).astype(bf16)

    shape = out_parts[0].shape
    return run(
        "after_ffn",
        body,
        [*out_parts, middle, cotangent, g_fpost],
        "v" * (terms + 3),
        [(shape, bf16), (shape, bf16), ((1, D), f32)],
    )


def query_side(flat, d_query, raw, cosine, sine, g_q, a, w_qkv, heads, d_attn_out):
    tok = a.shape[0]
    wide = H * HD

    def body(
        dq_ref, raw_ref, cos_ref, sin_ref, g_ref, a_ref, w_ref, o_ref, dout_ref,
        lines, da_ref, dg_ref, low, grad, grad_o,
    ):
        cos, sin = cos_ref[...], sin_ref[...]
        dg = jnp.zeros((1, HD), f32)
        for h in range(H):
            cols = slice(h * HD, (h + 1) * HD)
            unit, scale = normed(raw_ref[:, cols])
            turned = rotate(dq_ref[:, cols], cos, -sin)
            dg = dg + jnp.sum(turned * unit, axis=0, keepdims=True)
            low[:, cols] = norm_back(unit, scale, turned * g_ref[...]).astype(bf16)
        dg_ref[...] = dg
        da_ref[...] = contract(low[...], w_ref[:, :wide], 1, 1)
        grad[...] = contract(a_ref[...], low[...], 0, 0)
        for j in range(wide // LANES):
            lines[pl.ds(j, D, stride=flat.q_across), :] = grad[:, j * LANES : (j + 1) * LANES]
        grad_o[...] = contract(o_ref[...], dout_ref[...], 0, 0)
        for j in range(flat.o_across):
            lines[pl.ds(flat.q_lines + j, wide, stride=flat.o_across), :] = grad_o[
                :, j * LANES : (j + 1) * LANES
            ]
        lines[flat.q_lines + flat.o_lines :, :] = jnp.zeros((16, LANES), f32)

    return run(
        "query_side",
        body,
        [d_query, raw, cosine, sine, g_q, a, w_qkv, heads, d_attn_out],
        "v" * 9,
        [((flat.q_lines + flat.o_lines + 16, LANES), f32), ((tok, D), f32), ((1, HD), f32)],
        [pltpu.VMEM((tok, wide), bf16), pltpu.VMEM((D, wide), f32), pltpu.VMEM((wide, D), f32)],
    )


def last_part(
    flat, order, groups, lines, kv_parts, raw, cosine, sine, g_k, a, w_qkv, tokens, g_pre, d_middle,
    da_query, gain_grads,
):
    tok = a.shape[0]
    terms = len(kv_parts)
    wide = H * HD
    each = flat.devices // groups

    def body(order_ref, lines_ref, *refs):
        kv_refs = refs[:terms]
        (
            raw_ref, cos_ref, sin_ref, gk_ref, a_ref, w_ref, tok_ref, gpre_ref, dmid_ref, da_ref,
            dgq, dgpost, dgfpre, dgfpost, in_ref, *outs, held, grad, gains, blocks, sems,
        ) = refs[terms:]
        q_copy = pltpu.make_async_copy(
            lines_ref.at[: flat.q_lines], held.at[: flat.q_lines], sems.at[0]
        )
        o_copy = pltpu.make_async_copy(
            lines_ref.at[flat.q_lines :], held.at[flat.q_lines :], sems.at[1]
        )
        q_copy.start()
        o_copy.start()
        d_kv = kv_refs[0][...].astype(f32)
        for ref in kv_refs[1:]:
            d_kv = d_kv + ref[...].astype(f32)
        unit, scale = normed(raw_ref[:, wide:])
        turned = rotate(d_kv[:, :HD], cos_ref[...], -sin_ref[...])
        dgk = jnp.sum(turned * unit, axis=0, keepdims=True)
        low = jnp.concatenate(
            [norm_back(unit, scale, turned * gk_ref[...]).astype(bf16), d_kv[:, HD:].astype(bf16)],
            axis=1,
        )
        grad[...] = contract(a_ref[...], low, 0, 0)
        d_a = da_ref[...] + contract(low, w_ref[:, wide:], 1, 1)
        unit, scale = normed(tok_ref[...].astype(f32))
        dgpre = jnp.sum(d_a * unit, axis=0, keepdims=True)
        in_ref[...] = (dmid_ref[...] + norm_back(unit, scale, d_a * gpre_ref[...])).astype(bf16)
        gains[...] = jnp.zeros_like(gains)
        at = 0
        for value in (dgpre, dgq[...], dgk, dgpost[...], dgfpre[...], dgfpost[...]):
            for i in range(value.shape[1] // LANES):
                gains[at : at + 1, :] = value[:, i * LANES : (i + 1) * LANES]
                at += 1
        q_copy.wait()
        for j in range(2 * HD // LANES):
            held[pl.ds(wide // LANES + j, D, stride=flat.q_across), :] = grad[
                :, j * LANES : (j + 1) * LANES
            ]
        o_copy.wait()
        for i in range(flat.devices):
            at = i * flat.lines
            blocks[i, : flat.gain_at, :] = held[at : at + flat.gain_at, :].astype(bf16)
            at = flat.gain_line(i)
            blocks[i, flat.gain_at :, :] = gains[at : at + 16, :].astype(bf16)
        copies = [
            pltpu.make_async_copy(
                blocks.at[order_ref[k]], outs[k // each].at[k % each], sems.at[2 + k]
            )
            for k in range(flat.devices)
        ]
        for copy in copies:
            copy.start()
        for copy in copies:
            copy.wait()

    return run(
        "last_part",
        body,
        [order, lines, *kv_parts, raw, cosine, sine, g_k, a, w_qkv, tokens, g_pre, d_middle]
        + [da_query, *gain_grads],
        "sh" + "v" * (terms + 14),
        [((tok, D), bf16)] + [((each, flat.rows, LANES), bf16)] * groups,
        [
            pltpu.VMEM(lines.shape, f32),
            pltpu.VMEM((D, 2 * HD), f32),
            pltpu.VMEM((-(-(flat.gain_lines + 16) // 8) * 8, LANES), f32),
            pltpu.VMEM((flat.devices, flat.rows, LANES), bf16),
            pltpu.SemaphoreType.DMA((2 + flat.devices,)),
        ],
        "v" + "h" * groups,
    )


class Ways:
    def __init__(self, sizes):
        self.sizes = sizes
        self.what = ""

    def size(self, axis):
        if isinstance(axis, str):
            return self.sizes[axis]
        n = 1
        for a in axis:
            n *= self.sizes[a]
        return n

    def fro(self, value, axis, offset):
        n = self.size(axis)
        if offset % n == 0:
            return value
        with jax.named_scope(self.what + "_" + "".join(axis) + str(offset)):
            return lax.ppermute(value, axis, [((i + offset) % n, i) for i in range(n)])

    def places(self):
        nx, ny = self.sizes["x"], self.sizes["y"]
        return [(ox, oy) for ox in range(nx) for oy in range(ny)]

    def outers(self):
        return [(ou, ov) for ou in range(self.sizes["u"]) for ov in range(self.sizes["v"])]

    def plane_gather(self, value, beside=(None, None)):
        early, late = beside
        nx, ny = self.sizes["x"], self.sizes["y"]
        half = halfway(value.shape[0])
        found = {(0, 0): value}
        for ox in range(1, nx):
            found[ox, 0] = self.fro(value, "x", ox)
        for oy in range(1, ny):
            found[0, oy] = self.fro(value, "y", oy)
        if early is not None:
            found, early = lax.optimization_barrier((found, early))
        halves = {}
        for ox in range(1, nx):
            for oy in range(1, ny):
                first = self.fro(found[ox, 0][:half], "y", oy)
                second = self.fro(found[0, oy][half:], "x", ox)
                halves[ox, oy] = [first, second]
        if late is not None:
            halves, late = lax.optimization_barrier((halves, late))
        found.update({at: jnp.concatenate(v, axis=0) for at, v in halves.items()})
        found = {at: [block, self.fro(block, "c", 1)] for at, block in found.items()}
        return found, (early, late)

    def plane_scatter(self, parts, first=None, second=None):
        nx, ny = self.sizes["x"], self.sizes["y"]
        low = {
            at: add_low(parts[at][0], self.fro(parts[at][1], "c", 1))
            for at in sorted(parts, reverse=True)
        }
        what = self.what
        if first is not None:
            low = first(low)
            self.what = what
        half = halfway(low[0, 0].shape[0])
        along_x = {ox: [low[ox, 0][:half]] for ox in range(1, nx)}
        along_y = {oy: [low[0, oy][half:]] for oy in range(1, ny)}
        for ox in range(1, nx):
            for oy in range(1, ny):
                along_x[ox].append(self.fro(low[ox, oy][:half], "y", -oy))
                along_y[oy].append(self.fro(low[ox, oy][half:], "x", -ox))
        by_x = {
            ox: jnp.concatenate([add_low(*v), low[ox, 0][half:]], axis=0) for ox, v in along_x.items()
        }
        by_y = {
            oy: jnp.concatenate([low[0, oy][:half], add_low(*v)], axis=0) for oy, v in along_y.items()
        }
        if second is not None:
            by_x, by_y = second((by_x, by_y))
            self.what = what
        terms = [low[0, 0]]
        terms += [self.fro(v, "x", -ox) for ox, v in by_x.items()]
        terms += [self.fro(v, "y", -oy) for oy, v in by_y.items()]
        return terms

    def z_begin(self, value):
        n = self.sizes["z"]
        if n != 4:
            return ()
        return self.fro(value, "z", 1), self.fro(value, "z", -1)

    def z_end(self, value, begun, halves=None):
        n = self.sizes["z"]
        if n != 4:
            return [self.fro(value, "z", oz) for oz in range(n)]
        above, below = begun
        half = halfway(value.shape[0])
        first, second = self.fro(above[:half], "z", 1), self.fro(below[half:], "z", -1)
        return [value, above, jnp.concatenate([first, second], axis=0), below]

    def z_gather(self, value):
        return self.z_end(value, self.z_begin(value))

    def z_pair(self, one, other, begun_one, begun_other):
        if self.sizes["z"] != 4:
            return self.z_end(one, ()), self.z_end(other, ())
        far_one = self.fro(begun_one[0], "z", 1)
        far_other = self.fro(begun_other[1], "z", -1)
        return [one, begun_one[0], far_one, begun_one[1]], [
            other, begun_other[0], far_other, begun_other[1]
        ]

    def z_scatter_begin(self, far):
        if self.sizes["z"] != 4:
            return ()
        half = halfway(far.shape[0])
        return self.fro(far[:half], "z", -1), self.fro(far[half:], "z", 1)

    def z_scatter_go(self, parts, begun):
        n = self.sizes["z"]
        if n != 4:
            return [self.fro(parts[oz], "z", -oz) for oz in range(1, n)]
        half = halfway(parts[0].shape[0])
        above = jnp.concatenate([add_low(parts[1][:half], begun[0]), parts[1][half:]], axis=0)
        below = jnp.concatenate([parts[3][:half], add_low(parts[3][half:], begun[1])], axis=0)
        return [self.fro(above, "z", -1), self.fro(below, "z", 1)]

    def z_scatter(self, parts):
        return [parts[0], *self.z_scatter_go(parts, self.z_scatter_begin(parts[len(parts) // 2]))]


SEQ = ("u", "y", "c")
CTX = ("z", "v", "x")
ACROSS = ("v", "x")


def make_shards(sizes):
    ways = Ways(sizes)
    ns, nctx, nx = ways.size(SEQ), ways.size(CTX), ways.size(ACROSS)
    nz, nc = sizes["z"], sizes["c"]
    devices = ns * nctx
    places, outers = ways.places(), ways.outers()

    def from_outers(value):
        if len(outers) == 1:
            return value
        return jnp.concatenate(
            [ways.fro(ways.fro(value, "u", ou), "v", ov) for ou, ov in outers], axis=0
        )

    def to_outers(value):
        if len(outers) == 1:
            return value
        rows = value.shape[0] // len(outers)
        return add_low(
            *[
                ways.fro(ways.fro(value[i * rows : (i + 1) * rows], "u", -ou), "v", -ov)
                for i, (ou, ov) in enumerate(outers)
            ]
        )

    def plane_rows(value, *beside):
        found, beside = ways.plane_gather(value, beside or (None, None))
        return [block for p in places for block in found[p]], beside

    def by_device(parts):
        return {p: parts[i * nc : (i + 1) * nc] for i, p in enumerate(places)}

    def shards(
        tokens, cotangent, segments, positions, attn_w, attn_m, attn_v,
        mlp_w, mlp_m, mlp_v, gains, gain_m, gain_v,
    ):
        at = {a: lax.axis_index(a) for a in sizes}
        seq_place = lax.axis_index(SEQ)
        across_place = lax.axis_index(ACROSS)
        ctx_place = at["z"] * nx + across_place
        device = seq_place * nctx + ctx_place
        piece, gain_piece = attn_w.shape[0], gains.shape[0]
        flat = Flat(piece, gain_piece, devices)

        sides = [sizes[a] for a in ("x", "y", "c", "u", "v", "z")]
        here = [at[a] for a in ("x", "y", "c", "u", "v", "z")]
        ox, oy, oc, ou, ov, oz = (
            (jnp.asarray(o, jnp.int32) + h) % n
            for o, h, n in zip(np.unravel_index(np.arange(devices), sides), here, sides)
        )
        order = ((ou * sizes["y"] + oy) * sizes["c"] + oc) * nz + oz
        order = (order * sizes["v"] + ov) * sizes["x"] + ox

        ways.what = "attn_gather"
        gain_offset = gain_piece * device % LANES
        gain_window = lax.dynamic_update_slice(
            jnp.zeros((16 * LANES,), bf16), gains.astype(bf16), (gain_offset,)
        )
        low_piece = jnp.concatenate(
            [
                jnp.pad(
                    attn_w.astype(bf16).reshape(flat.lines, LANES),
                    ((0, flat.gain_at - flat.lines), (0, 0)),
                ),
                gain_window.reshape(16, LANES),
            ],
            axis=0,
        )
        line_blocks = ways.z_gather(low_piece)

        ways.what = "unit_exchange"
        units, width = mlp_w.shape
        share = units // ns
        held = -(-share // 32) * 32

        def seq_send(by_place):
            return [
                ways.fro(
                    lax.dynamic_index_in_dim(by_place, (seq_place - offset) % ns, 0, keepdims=False),
                    SEQ,
                    offset,
                )
                for offset in range(ns)
            ]

        def seq_place_all(heard):
            kept = jnp.zeros((ns,) + heard[0].shape, heard[0].dtype)
            for offset, value in enumerate(heard):
                kept = lax.dynamic_update_index_in_dim(kept, value, (seq_place + offset) % ns, 0)
            return kept

        heard = seq_send(mlp_w.astype(bf16).reshape(ns, share, width))
        line_blocks, heard = lax.optimization_barrier((line_blocks, heard))
        by_cols = seq_place_all(heard)
        rows_own = jnp.concatenate([by_cols[i] for i in range(ns)], axis=1)
        rows_own = jnp.pad(rows_own, ((0, held - share), (0, 0)))
        ways.what = "attn_gather"
        line_z, rows_own = lax.optimization_barrier(
            (from_outers(jnp.concatenate(line_blocks, axis=0)), rows_own)
        )
        def next_units(ring, *beside):
            if beside:
                ring[-1], *beside = lax.optimization_barrier((ring[-1],) + beside)
            what, ways.what = ways.what, "unit_gather"
            ring.append(ways.fro(ring[-1], "z", 1))
            ways.what = what
            return beside[0] if len(beside) == 1 else beside

        steps = nz == 4
        cut = halfway(held)
        whole = [rows_own]
        next_units(whole)
        gathered, _ = ways.plane_gather(line_z)
        line_parts = [part.reshape(-1, flat.rows, LANES) for p in places for part in gathered[p]]
        line_parts, whole[-1] = lax.optimization_barrier((line_parts, whole[-1]))
        rings = [[v[:cut] for v in whole], [v[cut:] for v in whole]]
        if steps:
            next_units(rings[0])
        else:
            for ring in rings:
                for _ in range(2, nz):
                    next_units(ring)

        tok_rows = tokens.shape[1]
        cosine, sine = angles(positions[0])
        (
            w_qkv, g_pre, g_q, g_k, g_post, g_fpre, g_fpost, normed_in, query, kv_local, raw,
        ) = first_part(flat, line_parts, order, tokens[0], cosine, sine)
        w_out = spread_out(flat, [after(part, kv_local) for part in line_parts], order)
        ways.what = "kv_gather"
        if steps:
            half = halfway(tok_rows)
            above, below = ways.z_begin(kv_local)
            above, below, rings[0][-1] = next_units(rings[1], above, below, rings[0][-1])
            far = ways.fro(above[:half], "z", 1), ways.fro(below[half:], "z", -1)
            far = next_units(rings[0], *far)
            kv_blocks = [kv_local, above, jnp.concatenate(far, axis=0), below]
        else:
            kv_blocks = ways.z_gather(kv_local)
        kv_all = jnp.stack([ways.fro(block, ACROSS, oa) for block in kv_blocks for oa in range(nx)])

        doc_all = segments[0]
        first_docs, last_docs = doc_all[::tok_rows], doc_all[tok_rows - 1 :: tok_rows]
        key_at = np.arange(nctx)
        key_place = (at["z"] + jnp.asarray(key_at // nx, jnp.int32)) % nz * nx
        key_place = key_place + (across_place + jnp.asarray(key_at % nx, jnp.int32)) % nx
        is_place = key_place[:, None] == jnp.arange(nctx, dtype=jnp.int32)[None, :]
        key_first = jnp.sum(jnp.where(is_place, first_docs[None, :], 0), axis=1)
        key_last = jnp.sum(jnp.where(is_place, last_docs[None, :], 0), axis=1)
        live = (key_place < ctx_place) & (key_last >= key_first[0])
        one_doc = key_first == key_last[0]
        task = jnp.where(live, jnp.where(one_doc, WHOLE, MASKED), DEAD)
        task = jnp.where(key_place == ctx_place, MASKED, task)
        info = jnp.stack([key_place, task]).astype(jnp.int32)
        key_docs = doc_all[:, None]
        query_docs = lax.dynamic_slice_in_dim(doc_all, ctx_place * tok_rows, tok_rows)[None]

        heads, log_total, attn_out, middle, ffn_in = attend(
            info, query, kv_all, key_docs, query_docs, w_out, tokens[0], g_post, g_fpre
        )

        ways.what = "ffn_in_gather"
        if steps:
            ffn_in = next_units(rings[1], ffn_in)
            ffn_rows, (rings[0][-1], rings[1][-1]) = plane_rows(ffn_in, rings[0][-1], rings[1][-1])
        else:
            ffn_rows, _ = plane_rows(ffn_in)
        units_here = [from_outers(block) for block in whole[:nz]]
        units_here += [from_outers(block) for pair in zip(rings[0][2:], rings[1][2:]) for block in pair]
        act, gelu, slope, parts = ffn_forward(ffn_rows, units_here)
        ways.what = "ffn_out_sum"
        out_parts = ways.plane_scatter(by_device(parts))
        mixed, d_mlp_out, d_gfpost = after_ffn(out_parts, middle, cotangent[0], g_fpost)

        ways.what = "d_out_gather"
        d_out_rows, _ = plane_rows(d_mlp_out)
        per = units_here[0].shape[0]

        def z_step(blocks, far, *earlier):
            value = blocks[far] if not earlier else add_low(blocks[far], *earlier)
            return ways.fro(value, "z", -1)

        class Ring:
            def __init__(self, name, blocks):
                self.name, self.blocks, self.at, self.heard = name, [to_outers(b) for b in blocks], nz, None

            def step(self, beside=None):
                if not steps:
                    return beside
                if self.heard is not None and beside is not None:
                    self.heard, beside = lax.optimization_barrier((self.heard, beside))
                self.at -= 1
                if self.at > 0:
                    value = self.blocks[self.at]
                    if self.heard is not None:
                        value = add_low(value, self.heard)
                    what, ways.what = ways.what, self.name
                    self.heard = ways.fro(value, "z", -1)
                    ways.what = what
                return beside

            def result(self):
                if steps:
                    return add_low(self.blocks[0], self.heard)
                return add_low(*[ways.fro(v, "z", -i) for i, v in enumerate(self.blocks)])

        down = Ring("down_grad_sum", unit_grads(act, 0, nz, per, d_out_rows))
        down.step()
        d_out_rows[0] = after(d_out_rows[0], down.blocks[0])
        d_both, parts = ffn_backward(d_out_rows, gelu, slope, units_here)
        parts[-1] = down.step(parts[-1])
        rings = {}

        def gate_then(low):
            low, both = lax.optimization_barrier((low, d_both))
            rings["gate"] = Ring("gate_grad_sum", unit_grads(both, 0, nz, per, ffn_rows))
            rings["gate"].step()
            return low

        def up_then(summed):
            summed = down.step(summed)
            summed, both = lax.optimization_barrier((summed, d_both))
            rings["up"] = Ring("up_grad_sum", unit_grads(both, 1, nz, per, ffn_rows))
            rings["up"].step()
            return summed

        ways.what = "d_in_sum"
        d_in_parts = ways.plane_scatter(by_device(parts), gate_then, up_then)
        d_in_parts = lax.optimization_barrier((d_in_parts, rings["up"].blocks[0]))[0]
        d_in_parts = rings["gate"].step(d_in_parts)

        d_query, d_kv, d_attn_out, d_middle, d_gfpre, d_gpost = attend_back(
            info, query, kv_all, key_docs, query_docs, heads, log_total, d_in_parts, middle, attn_out,
            cotangent[0], w_out, g_post, g_fpre,
        )
        d_kv = rings["up"].step(d_kv)
        d_kv = down.step(d_kv)
        ways.what = "kv_sum"
        d_kv = d_kv.reshape(nz, nx, tok_rows, 2 * HD)

        def across(oz):
            return [ways.fro(d_kv[oz, oa], ACROSS, -oa) for oa in range(nx)]

        far = nz // 2
        kv_parts = {far: add_low(*across(far))}
        near = {oz: across(oz) for oz in range(nz) if oz != far}
        begun = ways.z_scatter_begin(kv_parts[far])
        near, begun = rings["gate"].step(lax.optimization_barrier((near, begun)))
        kv_parts.update({oz: add_low(*terms) for oz, terms in near.items()})
        kv_parts = [kv_parts[0], *ways.z_scatter_go(kv_parts, begun)]
        kv_parts = rings["up"].step(kv_parts)
        lines, da_query, d_gq = query_side(
            flat, after(d_query, *near[0]), raw, cosine, sine, g_q, normed_in, w_qkv, heads, d_attn_out
        )
        input_grad, *packed = last_part(
            flat, order, len(places) * nc, lines, kv_parts, raw, cosine, sine, g_k, normed_in, w_qkv, tokens[0],
            g_pre, d_middle, da_query, [d_gq, d_gpost, d_gfpre, d_gfpost],
        )

        ways.what = "attn_grad_sum"
        packed = [part.reshape(-1, LANES) for part in packed]
        terms = ways.plane_scatter({p: packed[i * nc : (i + 1) * nc] for i, p in enumerate(places)})
        owned = [rings["gate"].result(), rings["up"].result(), down.result()]
        own_rows = jnp.concatenate([v[:share] for v in owned], axis=1)
        by_cols = jnp.stack([own_rows[:, i * width : (i + 1) * width] for i in range(ns)])
        terms, by_cols = lax.optimization_barrier((terms, by_cols))
        plane_sum = to_outers(add_low(*terms))

        ways.what = "grad_exchange"
        mlp_red = seq_place_all(seq_send(by_cols)).astype(f32).reshape(units, width)
        mlp_m_new, mlp_v_new, mlp_new = adam_update(
            mlp_w, mlp_m, mlp_v, mlp_red, RATE_MATRIX, DECAY_MATRIX
        )

        ways.what = "attn_grad_sum"
        terms = ways.z_scatter([plane_sum[oz * flat.rows : (oz + 1) * flat.rows] for oz in range(nz)])
        terms, mlp_new = lax.optimization_barrier((terms, mlp_new))
        red = sum(part.astype(f32) for part in terms)
        attn_red = red[: flat.lines].reshape(-1)
        gain_red = lax.dynamic_slice(red[flat.gain_at :].reshape(-1), (gain_offset,), (gain_piece,))

        attn_m_new, attn_v_new, attn_new = adam_update(
            attn_w, attn_m, attn_v, attn_red, RATE_MATRIX, DECAY_MATRIX
        )
        gain_m_new, gain_v_new, gain_new = adam_update(
            gains, gain_m, gain_v, gain_red, RATE_GAIN, 0.0
        )
        return (
            mixed[None], input_grad[None],
            attn_red, attn_m_new, attn_v_new, attn_new,
            mlp_red, mlp_m_new, mlp_v_new, mlp_new,
            gain_red, gain_m_new, gain_v_new, gain_new,
        )

    return shards


def solution(mesh):
    seq, ctx = mesh.shape["seq"], mesh.shape["ctx"]
    nz = 4 if ctx % 4 == 0 else 1
    chips_y, chips_x = seq // 2, ctx // nz
    y, x = 2 - chips_y % 2, 2 - chips_x % 2
    sizes = {"u": chips_y // y, "y": y, "c": 2, "z": nz, "v": chips_x // x, "x": x}
    fine = Mesh(mesh.devices.reshape(*sizes.values()), tuple(sizes))
    s, x = SEQ, CTX
    both = s + x
    in_specs = (
        P(s, x, None), P(s, x, None), P(s, None), P(s, x),
        P(both), P(both), P(both),
        P(x, s), P(x, s), P(x, s),
        P(both), P(both), P(both),
    )
    out_specs = (
        P(s, x, None), P(s, x, None),
        P(both), P(both), P(both), P(both),
        P(x, s), P(x, s), P(x, s), P(x, s),
        P(both), P(both), P(both), P(both),
    )
    return jax.shard_map(
        make_shards(sizes), mesh=fine, in_specs=in_specs, out_specs=out_specs, check_vma=False
    )
```

```python
import jax
import jax.numpy as jnp
import numpy as np
from jax import lax
from jax.experimental import pallas as pl
from jax.experimental.pallas import tpu as pltpu
from jax.sharding import Mesh, PartitionSpec as P

D = 1152
H = 4
HD = 256
STEP = 5

NORM_EPS = 1e-06
SCORE_FLOOR = -1e30
ROPE_BASE = 1000000.0
BETA_MOMENT = 0.5
ADAM_EPS = 1e-08
RATE_MATRIX = 0.03
RATE_GAIN = 0.5
DECAY_MATRIX = 0.1

bf16 = jnp.bfloat16
f32 = jnp.float32
LANES = 128


def normed(value):
    factor = lax.rsqrt(jnp.mean(value * value, axis=-1, keepdims=True) + NORM_EPS)
    return (value * factor, factor)


def norm_back(unit, factor, d_unit):
    return factor * (d_unit - unit * jnp.mean(d_unit * unit, axis=-1, keepdims=True))


def angles(position):
    half_index = jnp.arange(HD // 2, dtype=f32)
    frequency = jnp.exp(half_index * (-2.0 * jnp.log(ROPE_BASE) / HD))
    angle = position.astype(f32)[:, None] * frequency[None, :]
    return (jnp.cos(angle), jnp.sin(angle))


def rotate(value, cosine, sine):
    half_width = value.shape[-1] // 2
    first_half = value[..., :half_width]
    second_half = value[..., half_width:]
    return jnp.concatenate(
        [first_half * cosine - second_half * sine, second_half * cosine + first_half * sine],
        axis=-1,
    )


def contract(left, right, left_dim, right_dim):
    return lax.dot_general(
        left, right, (((left_dim,), (right_dim,)), ((), ())), preferred_element_type=f32
    )


def adam_update(weight, moment_one, second, gradient, learn_rate, decay_rate):
    moment_new = BETA_MOMENT * moment_one + (1.0 - BETA_MOMENT) * gradient
    second_new = BETA_MOMENT * second + (1.0 - BETA_MOMENT) * gradient * gradient
    correction = 1.0 - BETA_MOMENT**STEP
    update = moment_new / correction / (jnp.sqrt(second_new / correction) + ADAM_EPS)
    return (moment_new, second_new, weight - learn_rate * (update + decay_rate * weight))


def add_low(*parts):
    total = parts[0].astype(f32)
    for part in parts[1:]:
        total = total + part.astype(f32)
    return total.astype(bf16)


def after(value, *earlier):
    return lax.optimization_barrier((value,) + earlier)[0]


def halfway(rows):
    return rows // 32 * 16 if rows >= 32 else rows // 2


VMEM_LIMIT = 56 * 1024 * 1024
VMEM_LIMITS = {"after_ffn": 40 * 1024 * 1024}
SCORE_SCALE = HD ** (-0.5)
SPACES = {"v": pltpu.VMEM, "h": pl.ANY, "s": pltpu.SMEM}


def run(name, body, operands, spaces, out_shape, scratch=(), out_spaces=None, flops=0):
    return pl.pallas_call(
        body,
        out_shape=tuple(jax.ShapeDtypeStruct(s, d) for s, d in out_shape),
        in_specs=[pl.BlockSpec(memory_space=SPACES[s]) for s in spaces],
        out_specs=tuple(
            pl.BlockSpec(memory_space=SPACES[s]) for s in out_spaces or "v" * len(out_shape)
        ),
        scratch_shapes=list(scratch),
        compiler_params=pltpu.CompilerParams(vmem_limit_bytes=VMEM_LIMITS.get(name, VMEM_LIMIT)),
        cost_estimate=pl.CostEstimate(flops=flops, bytes_accessed=0, transcendentals=0),
        name=name,
    )(*operands)


class Flat:
    def __init__(self, piece, gain_piece, devices):
        self.devices = devices
        self.lines = piece // LANES
        self.gain_at = -(-self.lines // 16) * 16
        self.gain_piece = gain_piece
        self.rows = self.gain_at + 16
        self.q_across, self.o_across = (H + 2) * HD // LANES, D // LANES
        self.q_lines, self.o_lines = D * self.q_across, H * HD * self.o_across
        widths = [D, HD, HD, D, D, D]
        self.gain_rows = [w // LANES for w in widths]
        self.gain_lines = sum(self.gain_rows)

        across, kv = self.q_across, 2 * HD // LANES
        self.kv_across = kv
        self.late_rows = self.lines // across + (2 if self.lines % across else 0)
        self.late_lines = -(-self.late_rows * kv // 16) * 16

    def first_row(self, device):
        return self.lines * device // self.q_across

    def gain_line(self, device):
        return self.gain_piece * device // LANES


def fetch(order_ref, sources, held, sems):
    copies = []
    for source in sources:
        for i in range(source.shape[0]):
            k = len(copies)
            copies.append(pltpu.make_async_copy(source.at[i], held.at[order_ref[k]], sems.at[k]))
    for copy in copies:
        copy.start()
    return copies


def first_part(flat, parts, order, tokens, cosine, sine):
    tok_rows = tokens.shape[0]
    wide = (H + 2) * HD
    blocks = -(-flat.q_lines // flat.lines)

    def body(order_ref, *refs):
        sources = refs[: len(parts)]
        (
            tok_ref, cos_ref, sin_ref, w_ref, g_pre, g_q, g_k, g_post, g_fpre, g_fpost,
            a_ref, q_ref, kv_ref, raw_ref, held, lines, gains, sems,
        ) = refs[len(parts) :]
        copies = fetch(order_ref, sources, held, sems)
        unit, _ = normed(tok_ref[...].astype(f32))
        gains[...] = jnp.zeros_like(gains)
        for copy in copies:
            copy.wait()
        for i in range(flat.devices):
            at = flat.gain_line(i)
            gains[at : at + 3, :] += held[i, flat.gain_at :, :].astype(f32)[:3]
        at = 0
        for ref, rows in zip((g_pre, g_q, g_k, g_post, g_fpre, g_fpost), flat.gain_rows):
            for i in range(rows):
                ref[:, i * LANES : (i + 1) * LANES] = gains[at + i : at + i + 1, :]
            at += rows
        a_ref[...] = (unit * g_pre[...]).astype(bf16)
        for i in range(blocks):
            lines[i * flat.lines : (i + 1) * flat.lines, :] = held[i, : flat.gain_at, :].astype(f32)[
                : flat.lines
            ]
        for j in range(flat.q_across):
            w_ref[:, j * LANES : (j + 1) * LANES] = lines[
                pl.ds(j, D, stride=flat.q_across), :
            ].astype(bf16)
        qkv = contract(a_ref[...], w_ref[...], 1, 0)
        raw_ref[...] = qkv[:, : (H + 1) * HD]
        cos, sin = cos_ref[...], sin_ref[...]
        for h in range(H):
            head = normed(qkv[:, h * HD : (h + 1) * HD])[0] * g_q[...]
            low = rotate(head, cos, sin).astype(bf16)
            q_ref[:, h * HD : (h + 1) * HD] = (low.astype(f32) * SCORE_SCALE).astype(bf16)
        key = normed(qkv[:, H * HD : (H + 1) * HD])[0] * g_k[...]
        kv_ref[:, :HD] = rotate(key, cos, sin).astype(bf16)
        kv_ref[:, HD:] = qkv[:, (H + 1) * HD :].astype(bf16)

    row = [((1, w * LANES), f32) for w in flat.gain_rows]
    return run(
        "first_part",
        body,
        [order, *parts, tokens, cosine, sine],
        "s" + "h" * len(parts) + "vvv",
        [((D, wide), bf16), *row]
        + [((tok_rows, D), bf16), ((tok_rows, H * HD), bf16), ((tok_rows, 2 * HD), bf16)]
        + [((tok_rows, (H + 1) * HD), f32)],
        [
            pltpu.VMEM((flat.devices, flat.rows, LANES), bf16),
            pltpu.VMEM((blocks * flat.lines, LANES), f32),
            pltpu.VMEM((-(-(flat.gain_lines + 3) // 8) * 8, LANES), f32),
            pltpu.SemaphoreType.DMA((flat.devices,)),
        ],
        flops=8 * 2 * tok_rows * D * wide,
    )


def spread_out(flat, parts, order):
    start = flat.q_lines // flat.lines

    def body(order_ref, *refs):
        sources = refs[: len(parts)]
        w_ref, held, lines, sems = refs[len(parts) :]
        for copy in fetch(order_ref, sources, held, sems):
            copy.wait()
        for i in range(start, flat.devices):
            at = (i - start) * flat.lines
            lines[at : at + flat.lines, :] = held[i, : flat.gain_at, :].astype(f32)[: flat.lines]
        for j in range(flat.o_across):
            w_ref[:, j * LANES : (j + 1) * LANES] = lines[
                pl.ds(flat.q_lines - start * flat.lines + j, H * HD, stride=flat.o_across), :
            ].astype(bf16)

    return run(
        "spread_out",
        body,
        [order, *parts],
        "s" + "h" * len(parts),
        [((H * HD, D), bf16)],
        [
            pltpu.VMEM((flat.devices, flat.rows, LANES), bf16),
            pltpu.VMEM(((flat.devices - start) * flat.lines, LANES), f32),
            pltpu.SemaphoreType.DMA((flat.devices,)),
        ],
    )[0]


DEAD, WHOLE, MASKED = 0, 1, 2


def allowed_of(kdoc_ref, qdoc_ref, shift):
    keys, queries = kdoc_ref.shape[0], qdoc_ref.shape[1]
    key_at = lax.broadcasted_iota(jnp.int32, (keys, queries), 0) + shift
    query_at = lax.broadcasted_iota(jnp.int32, (keys, queries), 1)
    return (kdoc_ref[...] == qdoc_ref[...]) & (key_at <= query_at)


def same(shape):
    return pl.BlockSpec(shape, lambda i, info: (0,) * len(shape))


def attend(info, query, kv, key_docs, query_docs, w_out, tokens, g_post, g_fpre):
    blocks, rows, _ = kv.shape

    def body(
        info_ref, q_ref, kv_ref, kdoc_ref, qdoc_ref, w_ref, tok_ref, g_post_ref, g_fpre_ref,
        o_ref, lse_ref, out_ref, mid_ref, in_ref, peak, total, acc,
    ):
        step = pl.program_id(0)

        @pl.when(step == 0)
        def _():
            peak[...] = jnp.full_like(peak, SCORE_FLOOR)
            total[...] = jnp.zeros_like(total)
            acc[...] = jnp.zeros_like(acc)

        def visit(masked):
            key = kv_ref[0, :, :HD]
            value_t = kv_ref[0, :, HD:].T
            if masked:
                allowed = allowed_of(
                    kdoc_ref, qdoc_ref, (info_ref[0, step] - info_ref[0, 0]) * rows
                )
            for h in range(H):
                score = contract(key, q_ref[:, h * HD : (h + 1) * HD], 1, 1)
                if masked:
                    score = jnp.where(allowed, score, SCORE_FLOOR)
                old = peak[h : h + 1, :]
                new = jnp.maximum(old, jnp.max(score, axis=0, keepdims=True))
                weight = jnp.exp(score - new)
                shrink = jnp.exp(old - new)
                peak[h : h + 1, :] = new
                total[h : h + 1, :] = total[h : h + 1, :] * shrink + jnp.sum(
                    weight, axis=0, keepdims=True
                )
                acc[h] = acc[h] * shrink + contract(value_t, weight.astype(bf16), 1, 0)

        pl.when(info_ref[1, step] == WHOLE)(lambda: visit(False))
        pl.when(info_ref[1, step] == MASKED)(lambda: visit(True))

        @pl.when(step == blocks - 1)
        def _():
            lse_ref[...] = jnp.zeros_like(lse_ref)
            for h in range(H):
                lse_ref[h : h + 1, :] = peak[h : h + 1, :] + jnp.log(total[h : h + 1, :])
                o_ref[:, h * HD : (h + 1) * HD] = (acc[h] / total[h : h + 1, :]).T.astype(bf16)
            attn_out = contract(o_ref[...], w_ref[...], 1, 0)
            out_ref[...] = attn_out
            middle = tok_ref[...].astype(f32) + normed(attn_out)[0] * g_post_ref[...]
            mid_ref[...] = middle
            in_ref[...] = (normed(middle)[0] * g_fpre_ref[...]).astype(bf16)

    return pl.pallas_call(
        body,
        grid_spec=pltpu.PrefetchScalarGridSpec(
            num_scalar_prefetch=1,
            grid=(blocks,),
            in_specs=[
                same((rows, H * HD)),
                pl.BlockSpec((1, rows, 2 * HD), lambda i, info: (i, 0, 0)),
                pl.BlockSpec((rows, 1), lambda i, info: (info[0, i], 0)),
                same((1, rows)),
                same((H * HD, D)),
                same((rows, D)),
                same((1, D)),
                same((1, D)),
            ],
            out_specs=[
                same((rows, H * HD)),
                same((8, rows)),
                same((rows, D)),
                same((rows, D)),
                same((rows, D)),
            ],
            scratch_shapes=[
                pltpu.VMEM((8, rows), f32),
                pltpu.VMEM((8, rows), f32),
                pltpu.VMEM((H, HD, rows), f32),
            ],
        ),
        out_shape=(
            jax.ShapeDtypeStruct((rows, H * HD), bf16),
            jax.ShapeDtypeStruct((8, rows), f32),
            jax.ShapeDtypeStruct((rows, D), f32),
            jax.ShapeDtypeStruct((rows, D), f32),
            jax.ShapeDtypeStruct((rows, D), bf16),
        ),
        compiler_params=pltpu.CompilerParams(vmem_limit_bytes=44 * 1024 * 1024),
        cost_estimate=pl.CostEstimate(
            flops=8 * 4 * blocks * rows * rows * H * HD, bytes_accessed=0, transcendentals=0
        ),
        name="attend",
    )(info, query, kv, key_docs, query_docs, w_out, tokens, g_post, g_fpre)


def attend_back(
    info, query, kv, key_docs, query_docs, heads, log_total, d_in, middle, attn_out, cotangent,
    w_out, g_post, g_fpre,
):
    blocks, rows, _ = kv.shape
    terms = len(d_in)

    def body(info_ref, q_ref, kv_ref, kdoc_ref, qdoc_ref, o_ref, lse_ref, *refs):
        terms_ref = refs[:terms]
        (
            mid_ref, out_ref, cot_ref, w_ref, g_post_ref, g_fpre_ref,
            dq_ref, dout_ref, dmid_ref, dg_fpre_ref, dg_post_ref, *dkv_refs, do_ref, delta_ref,
        ) = refs[terms:]
        step = pl.program_id(0)

        def give(d_key, d_value):
            for k, ref in enumerate(dkv_refs):

                @pl.when(step == k)
                def _(ref=ref):
                    ref[:, :HD] = d_key.astype(bf16)
                    ref[:, HD:] = d_value.astype(bf16)

        @pl.when(step == 0)
        def _():
            d_rows = sum(ref[...].astype(f32) for ref in terms_ref)
            unit, scale = normed(mid_ref[...])
            dg_fpre_ref[...] = jnp.sum(d_rows * unit, axis=0, keepdims=True)
            d_middle = cot_ref[...].astype(f32) + norm_back(unit, scale, d_rows * g_fpre_ref[...])
            dmid_ref[...] = d_middle
            unit, scale = normed(out_ref[...])
            dg_post_ref[...] = jnp.sum(d_middle * unit, axis=0, keepdims=True)
            d_out = norm_back(unit, scale, d_middle * g_post_ref[...]).astype(bf16)
            dout_ref[...] = d_out
            delta_ref[...] = jnp.zeros_like(delta_ref)
            for h in range(H):
                cols = slice(h * HD, (h + 1) * HD)
                d_o = contract(d_out, w_ref[cols, :], 1, 1).astype(bf16)
                do_ref[:, cols] = d_o
                each = (d_o.astype(f32) * o_ref[:, cols].astype(f32)).T
                delta_ref[h : h + 1, :] = jnp.sum(each, axis=0, keepdims=True)
            dq_ref[...] = jnp.zeros_like(dq_ref)

        def visit(masked):
            key, value = kv_ref[0, :, :HD], kv_ref[0, :, HD:]
            if masked:
                allowed = allowed_of(
                    kdoc_ref, qdoc_ref, (info_ref[0, step] - info_ref[0, 0]) * rows
                )
            d_key = jnp.zeros((rows, HD), f32)
            d_value = jnp.zeros((rows, HD), f32)
            for h in range(H):
                cols = slice(h * HD, (h + 1) * HD)
                q, d_o = q_ref[:, cols], do_ref[:, cols]
                prob = jnp.exp(contract(key, q, 1, 1) - lse_ref[h : h + 1, :])
                if masked:
                    prob = jnp.where(allowed, prob, 0.0)
                d_value = d_value + contract(prob.astype(bf16), d_o, 1, 0)
                d_prob = contract(value, d_o, 1, 1)
                d_score = (prob * (d_prob - delta_ref[h : h + 1, :])).astype(bf16)
                d_key = d_key + contract(d_score, q, 1, 0)
                dq_ref[:, cols] = dq_ref[:, cols] + contract(d_score, key, 0, 0)
            give(d_key, d_value)

        pl.when(info_ref[1, step] == WHOLE)(lambda: visit(False))
        pl.when(info_ref[1, step] == MASKED)(lambda: visit(True))

        @pl.when(info_ref[1, step] == DEAD)
        def _():
            give(jnp.zeros((rows, HD), f32), jnp.zeros((rows, HD), f32))

        @pl.when(step == blocks - 1)
        def _():
            dq_ref[...] = dq_ref[...] * SCORE_SCALE

    block = pl.BlockSpec((1, rows, 2 * HD), lambda i, info: (i, 0, 0))
    return pl.pallas_call(
        body,
        grid_spec=pltpu.PrefetchScalarGridSpec(
            num_scalar_prefetch=1,
            grid=(blocks,),
            in_specs=[
                same((rows, H * HD)),
                block,
                pl.BlockSpec((rows, 1), lambda i, info: (info[0, i], 0)),
                same((1, rows)),
                same((rows, H * HD)),
                same((8, rows)),
                *[same((rows, D))] * (terms + 3),
                same((H * HD, D)),
                same((1, D)),
                same((1, D)),
            ],
            out_specs=[
                same((rows, H * HD)),
                same((rows, D)),
                same((rows, D)),
                same((1, D)),
                same((1, D)),
                *[same((rows, 2 * HD))] * blocks,
            ],
            scratch_shapes=[pltpu.VMEM((rows, H * HD), bf16), pltpu.VMEM((8, rows), f32)],
        ),
        out_shape=(
            jax.ShapeDtypeStruct((rows, H * HD), f32),
            jax.ShapeDtypeStruct((rows, D), bf16),
            jax.ShapeDtypeStruct((rows, D), f32),
            jax.ShapeDtypeStruct((1, D), f32),
            jax.ShapeDtypeStruct((1, D), f32),
            *[jax.ShapeDtypeStruct((rows, 2 * HD), bf16)] * blocks,
        ),
        compiler_params=pltpu.CompilerParams(vmem_limit_bytes=VMEM_LIMIT),
        cost_estimate=pl.CostEstimate(flops=0, bytes_accessed=0, transcendentals=0),
        name="attend_back",
    )(
        info, query, kv, key_docs, query_docs, heads, log_total, *d_in, middle, attn_out, cotangent,
        w_out, g_post, g_fpre,
    )


def gelu_parts(gate):
    scale = 0.7978845608028654
    square = gate * gate
    inner = jnp.tanh(scale * gate * (1.0 + 0.044715 * square))
    half_up = 0.5 * (1.0 + inner)
    slope = half_up + 0.5 * gate * (1.0 - inner * inner) * scale * (1.0 + 3 * 0.044715 * square)
    return gate * half_up, slope


def gather_rows(refs, held, sems):
    tok = refs[0].shape[0]
    return [
        pltpu.make_async_copy(ref, held.at[k * tok : (k + 1) * tok], sems.at[k])
        for k, ref in enumerate(refs)
    ]


def scatter_rows(held, refs, sems):
    tok = refs[0].shape[0]
    return [
        pltpu.make_async_copy(held.at[k * tok : (k + 1) * tok], ref, sems.at[k])
        for k, ref in enumerate(refs)
    ]


def by_chunk(step, chunks, copies, do):
    per = len(copies) // chunks
    for k in range(chunks):

        @pl.when(step == k)
        def _(k=k):
            for copy in copies[k * per : (k + 1) * per]:
                do(copy)


def ffn_call(name, body, rows, streams, weights, outs, order):
    count, (tok, wide) = len(rows), rows[0].shape
    chunks = -(-count * tok // 512)
    both = count * tok // chunks
    blocks = len(weights)
    starts = np.cumsum([0] + [w.shape[0] for w in weights]).tolist()
    per = starts[-1]

    def kernel(*refs):
        row_refs, refs = refs[:count], refs[count:]
        stream_refs, refs = refs[: len(streams)], refs[len(streams) :]
        w_refs, refs = refs[:blocks], refs[blocks:]
        out_refs, refs = refs[: len(outs)], refs[len(outs) :]
        sum_refs, (held, given, units, sems_in, sems_out, sems_w) = refs[:count], refs[count:]
        step = pl.program_id(0)
        coming = gather_rows(row_refs, held, sems_in)
        going = scatter_rows(given, sum_refs, sems_out)
        brought = {
            k: [
                pltpu.make_async_copy(
                    ref.at[:, k * D : (k + 1) * D],
                    units.at[k, starts[i] : starts[i + 1]],
                    sems_w.at[k * blocks + i],
                )
                for i, ref in enumerate(w_refs)
            ]
            for k in order
        }

        @pl.when(step == 0)
        def _():
            first = len(coming) // chunks
            bringing = [c for k in order for c in brought[k]]
            for copy in coming[:first] + bringing + coming[first:]:
                copy.start()

        by_chunk(step, chunks, coming, lambda copy: copy.wait())
        here = pl.ds(pl.multiple_of(step * both, both), both)

        def arrived(k):
            for copy in brought[k]:
                copy.wait()
            return units[k]

        @pl.when(step == 0)
        def _():
            given[here, :] = body(held[here, :], stream_refs, arrived, out_refs)

        @pl.when(step > 0)
        def _():
            given[here, :] = body(held[here, :], stream_refs, lambda k: units[k], out_refs)

        by_chunk(step, chunks, going, lambda copy: copy.start())

        @pl.when(step == chunks - 1)
        def _():
            for copy in going:
                copy.wait()

    def chunk(width):
        return pl.BlockSpec((both, width), lambda i: (i, 0))

    anywhere = pl.BlockSpec(memory_space=pl.ANY)
    return pl.pallas_call(
        kernel,
        grid=(chunks,),
        in_specs=[anywhere] * count
        + [chunk(s.shape[1]) for s in streams]
        + [anywhere] * blocks,
        out_specs=tuple([chunk(w) for w in outs] + [anywhere] * count),
        out_shape=tuple(
            [jax.ShapeDtypeStruct((count * tok, w), bf16) for w in outs]
            + [jax.ShapeDtypeStruct((tok, wide), bf16)] * count
        ),
        scratch_shapes=[
            pltpu.VMEM((count * tok, wide), bf16),
            pltpu.VMEM((count * tok, wide), bf16),
            pltpu.VMEM((3, per, D), bf16),
            pltpu.SemaphoreType.DMA((count,)),
            pltpu.SemaphoreType.DMA((count,)),
            pltpu.SemaphoreType.DMA((3 * blocks,)),
        ],
        compiler_params=pltpu.CompilerParams(vmem_limit_bytes=VMEM_LIMIT),
        cost_estimate=pl.CostEstimate(
            flops=6 * count * tok * per * D, bytes_accessed=0, transcendentals=0
        ),
        name=name,
    )(*rows, *streams, *weights)


def ffn_forward(rows, weights):
    def body(x, _, weight, out_refs):
        act_ref, gelu_ref, slope_ref = out_refs
        gate = contract(x, weight(0), 1, 1)
        up = contract(x, weight(1), 1, 1)
        gelu, slope = gelu_parts(gate)
        act = (gelu * up).astype(bf16)
        act_ref[...] = act
        gelu_ref[...] = gelu.astype(bf16)
        slope_ref[...] = (slope * up).astype(bf16)
        return contract(act, weight(2), 1, 0).astype(bf16)

    units = sum(w.shape[0] for w in weights)
    act, gelu, slope, *parts = ffn_call("ffn_forward", body, rows, [], weights, [units] * 3, (0, 1, 2))
    return act, gelu, slope, parts


def ffn_backward(rows, gelu, slope, weights):
    units = sum(w.shape[0] for w in weights)

    def body(x, stream_refs, weight, out_refs):
        gelu_ref, slope_ref = stream_refs
        d_act = contract(x, weight(2), 1, 1)
        d_gate = (d_act * slope_ref[...].astype(f32)).astype(bf16)
        d_up = (d_act * gelu_ref[...].astype(f32)).astype(bf16)
        out_refs[0][:, :units] = d_gate
        out_refs[0][:, units:] = d_up
        return (contract(d_gate, weight(0), 1, 0) + contract(d_up, weight(1), 1, 0)).astype(bf16)

    d_both, *parts = ffn_call(
        "ffn_backward", body, rows, [gelu, slope], weights, [2 * units], (2, 0, 1)
    )
    return d_both, parts


def unit_grads(units, part, blocks, per, rows):
    count = len(rows)
    tokens, both = units.shape[0], blocks * per

    def body(unit_ref, *refs):
        row_refs, out_refs, (held, sems) = refs[:count], refs[count : count + blocks], refs[-2:]
        copies = gather_rows(row_refs, held, sems)
        for copy in copies:
            copy.start()
        for copy in copies:
            copy.wait()
        total = contract(unit_ref[...], held[...], 0, 0).astype(bf16)
        for i, ref in enumerate(out_refs):
            ref[...] = total[i * per : (i + 1) * per]

    return pl.pallas_call(
        body,
        grid=(1,),
        in_specs=[pl.BlockSpec((tokens, both), lambda i: (0, part))]
        + [pl.BlockSpec(memory_space=pl.ANY)] * count,
        out_specs=[pl.BlockSpec((per, D), lambda i: (0, 0))] * blocks,
        out_shape=[jax.ShapeDtypeStruct((per, D), bf16)] * blocks,
        scratch_shapes=[pltpu.VMEM((tokens, D), bf16), pltpu.SemaphoreType.DMA((count,))],
        compiler_params=pltpu.CompilerParams(vmem_limit_bytes=40 * 1024 * 1024),
        cost_estimate=pl.CostEstimate(
            flops=2 * tokens * both * D, bytes_accessed=0, transcendentals=0
        ),
        name="unit_grads",
    )(units, *rows)


def after_ffn(out_parts, middle, cotangent, g_fpost):
    terms = len(out_parts)

    def body(*refs):
        mid_ref, cot_ref, g_ref, mixed_ref, d_ref, dg_ref = refs[terms:]
        total = refs[0][...].astype(f32)
        for ref in refs[1:terms]:
            total = total + ref[...].astype(f32)
        unit, scale = normed(total)
        mixed_ref[...] = (mid_ref[...] + unit * g_ref[...]).astype(bf16)
        upstream = cot_ref[...].astype(f32)
        dg_ref[...] = jnp.sum(upstream * unit, axis=0, keepdims=True)
        d_ref[...] = norm_back(unit, scale, upstream * g_ref[...]).astype(bf16)

    shape = out_parts[0].shape
    return run(
        "after_ffn",
        body,
        [*out_parts, middle, cotangent, g_fpost],
        "v" * (terms + 3),
        [(shape, bf16), (shape, bf16), ((1, D), f32)],
    )


def query_side(flat, d_query, raw, cosine, sine, g_q, a, w_qkv, heads, d_attn_out):
    tok = a.shape[0]
    wide = H * HD

    def body(
        dq_ref, raw_ref, cos_ref, sin_ref, g_ref, a_ref, w_ref, o_ref, dout_ref,
        lines, da_ref, dg_ref, low, grad, grad_o,
    ):
        cos, sin = cos_ref[...], sin_ref[...]
        dg = jnp.zeros((1, HD), f32)
        for h in range(H):
            cols = slice(h * HD, (h + 1) * HD)
            unit, scale = normed(raw_ref[:, cols])
            turned = rotate(dq_ref[:, cols], cos, -sin)
            dg = dg + jnp.sum(turned * unit, axis=0, keepdims=True)
            low[:, cols] = norm_back(unit, scale, turned * g_ref[...]).astype(bf16)
        dg_ref[...] = dg
        da_ref[...] = contract(low[...], w_ref[:, :wide], 1, 1)
        grad[...] = contract(a_ref[...], low[...], 0, 0)
        for j in range(wide // LANES):
            lines[pl.ds(j, D, stride=flat.q_across), :] = grad[:, j * LANES : (j + 1) * LANES]
        grad_o[...] = contract(o_ref[...], dout_ref[...], 0, 0)
        for j in range(flat.o_across):
            lines[pl.ds(flat.q_lines + j, wide, stride=flat.o_across), :] = grad_o[
                :, j * LANES : (j + 1) * LANES
            ]
        lines[flat.q_lines + flat.o_lines :, :] = jnp.zeros((16, LANES), f32)

    return run(
        "query_side",
        body,
        [d_query, raw, cosine, sine, g_q, a, w_qkv, heads, d_attn_out],
        "v" * 9,
        [((flat.q_lines + flat.o_lines + 16, LANES), f32), ((tok, D), f32), ((1, HD), f32)],
        [pltpu.VMEM((tok, wide), bf16), pltpu.VMEM((D, wide), f32), pltpu.VMEM((wide, D), f32)],
    )


def last_part(
    flat, order, groups, lines, kv_parts, raw, cosine, sine, g_k, a, w_qkv, tokens, g_pre, d_middle,
    da_query, gain_grads,
):
    tok = a.shape[0]
    terms = len(kv_parts)
    wide = H * HD
    each = flat.devices // groups

    def body(order_ref, lines_ref, *refs):
        kv_refs = refs[:terms]
        (
            raw_ref, cos_ref, sin_ref, gk_ref, a_ref, w_ref, tok_ref, gpre_ref, dmid_ref, da_ref,
            dgq, dgpost, dgfpre, dgfpost, in_ref, *outs, held, grad, gains, blocks, sems,
        ) = refs[terms:]
        q_copy = pltpu.make_async_copy(
            lines_ref.at[: flat.q_lines], held.at[: flat.q_lines], sems.at[0]
        )
        o_copy = pltpu.make_async_copy(
            lines_ref.at[flat.q_lines :], held.at[flat.q_lines :], sems.at[1]
        )
        q_copy.start()
        o_copy.start()
        d_kv = kv_refs[0][...].astype(f32)
        for ref in kv_refs[1:]:
            d_kv = d_kv + ref[...].astype(f32)
        unit, scale = normed(raw_ref[:, wide:])
        turned = rotate(d_kv[:, :HD], cos_ref[...], -sin_ref[...])
        dgk = jnp.sum(turned * unit, axis=0, keepdims=True)
        low = jnp.concatenate(
            [norm_back(unit, scale, turned * gk_ref[...]).astype(bf16), d_kv[:, HD:].astype(bf16)],
            axis=1,
        )
        grad[...] = contract(a_ref[...], low, 0, 0)
        d_a = da_ref[...] + contract(low, w_ref[:, wide:], 1, 1)
        unit, scale = normed(tok_ref[...].astype(f32))
        dgpre = jnp.sum(d_a * unit, axis=0, keepdims=True)
        in_ref[...] = (dmid_ref[...] + norm_back(unit, scale, d_a * gpre_ref[...])).astype(bf16)
        gains[...] = jnp.zeros_like(gains)
        at = 0
        for value in (dgpre, dgq[...], dgk, dgpost[...], dgfpre[...], dgfpost[...]):
            for i in range(value.shape[1] // LANES):
                gains[at : at + 1, :] = value[:, i * LANES : (i + 1) * LANES]
                at += 1
        q_copy.wait()
        for j in range(2 * HD // LANES):
            held[pl.ds(wide // LANES + j, D, stride=flat.q_across), :] = grad[
                :, j * LANES : (j + 1) * LANES
            ]
        o_copy.wait()
        for i in range(flat.devices):
            at = i * flat.lines
            blocks[i, : flat.gain_at, :] = held[at : at + flat.gain_at, :].astype(bf16)
            at = flat.gain_line(i)
            blocks[i, flat.gain_at :, :] = gains[at : at + 16, :].astype(bf16)
        copies = [
            pltpu.make_async_copy(
                blocks.at[order_ref[k]], outs[k // each].at[k % each], sems.at[2 + k]
            )
            for k in range(flat.devices)
        ]
        for copy in copies:
            copy.start()
        for copy in copies:
            copy.wait()

    return run(
        "last_part",
        body,
        [order, lines, *kv_parts, raw, cosine, sine, g_k, a, w_qkv, tokens, g_pre, d_middle]
        + [da_query, *gain_grads],
        "sh" + "v" * (terms + 14),
        [((tok, D), bf16)] + [((each, flat.rows, LANES), bf16)] * groups,
        [
            pltpu.VMEM(lines.shape, f32),
            pltpu.VMEM((D, 2 * HD), f32),
            pltpu.VMEM((-(-(flat.gain_lines + 16) // 8) * 8, LANES), f32),
            pltpu.VMEM((flat.devices, flat.rows, LANES), bf16),
            pltpu.SemaphoreType.DMA((2 + flat.devices,)),
        ],
        "v" + "h" * groups,
    )


class Ways:
    def __init__(self, sizes):
        self.sizes = sizes
        self.what = ""

    def size(self, axis):
        if isinstance(axis, str):
            return self.sizes[axis]
        n = 1
        for a in axis:
            n *= self.sizes[a]
        return n

    def fro(self, value, axis, offset):
        n = self.size(axis)
        if offset % n == 0:
            return value
        with jax.named_scope(self.what + "_" + "".join(axis) + str(offset)):
            return lax.ppermute(value, axis, [((i + offset) % n, i) for i in range(n)])

    def places(self):
        nx, ny = self.sizes["x"], self.sizes["y"]
        return [(ox, oy) for ox in range(nx) for oy in range(ny)]

    def outers(self):
        return [(ou, ov) for ou in range(self.sizes["u"]) for ov in range(self.sizes["v"])]

    def plane_gather(self, value, beside=(None, None)):
        early, late = beside
        nx, ny = self.sizes["x"], self.sizes["y"]
        half = halfway(value.shape[0])
        found = {(0, 0): value}
        for ox in range(1, nx):
            found[ox, 0] = self.fro(value, "x", ox)
        for oy in range(1, ny):
            found[0, oy] = self.fro(value, "y", oy)
        if early is not None:
            found, early = lax.optimization_barrier((found, early))
        halves = {}
        for ox in range(1, nx):
            for oy in range(1, ny):
                first = self.fro(found[ox, 0][:half], "y", oy)
                second = self.fro(found[0, oy][half:], "x", ox)
                halves[ox, oy] = [first, second]
        if late is not None:
            halves, late = lax.optimization_barrier((halves, late))
        found.update({at: jnp.concatenate(v, axis=0) for at, v in halves.items()})
        found = {at: [block, self.fro(block, "c", 1)] for at, block in found.items()}
        return found, (early, late)

    def plane_scatter(self, parts, first=None, second=None):
        nx, ny = self.sizes["x"], self.sizes["y"]
        low = {
            at: add_low(parts[at][0], self.fro(parts[at][1], "c", 1))
            for at in sorted(parts, reverse=True)
        }
        what = self.what
        if first is not None:
            last = max(low)
            low[last] = first(low[last])
            self.what = what
        half = halfway(low[0, 0].shape[0])
        along_x = {ox: [low[ox, 0][:half]] for ox in range(1, nx)}
        along_y = {oy: [low[0, oy][half:]] for oy in range(1, ny)}
        for ox in range(1, nx):
            for oy in range(1, ny):
                along_x[ox].append(self.fro(low[ox, oy][:half], "y", -oy))
                along_y[oy].append(self.fro(low[ox, oy][half:], "x", -ox))
        by_x = {
            ox: jnp.concatenate([add_low(*v), low[ox, 0][half:]], axis=0) for ox, v in along_x.items()
        }
        by_y = {
            oy: jnp.concatenate([low[0, oy][:half], add_low(*v)], axis=0) for oy, v in along_y.items()
        }
        if second is not None:
            by_x, by_y = second((by_x, by_y))
            self.what = what
        terms = [low[0, 0]]
        terms += [self.fro(v, "x", -ox) for ox, v in by_x.items()]
        terms += [self.fro(v, "y", -oy) for oy, v in by_y.items()]
        return terms

    def z_begin(self, value):
        n = self.sizes["z"]
        if n != 4:
            return ()
        return self.fro(value, "z", 1), self.fro(value, "z", -1)

    def z_end(self, value, begun, halves=None):
        n = self.sizes["z"]
        if n != 4:
            return [self.fro(value, "z", oz) for oz in range(n)]
        above, below = begun
        half = halfway(value.shape[0])
        first, second = self.fro(above[:half], "z", 1), self.fro(below[half:], "z", -1)
        return [value, above, jnp.concatenate([first, second], axis=0), below]

    def z_gather(self, value):
        return self.z_end(value, self.z_begin(value))

    def z_pair(self, one, other, begun_one, begun_other):
        if self.sizes["z"] != 4:
            return self.z_end(one, ()), self.z_end(other, ())
        far_one = self.fro(begun_one[0], "z", 1)
        far_other = self.fro(begun_other[1], "z", -1)
        return [one, begun_one[0], far_one, begun_one[1]], [
            other, begun_other[0], far_other, begun_other[1]
        ]

    def z_scatter_begin(self, far):
        if self.sizes["z"] != 4:
            return ()
        half = halfway(far.shape[0])
        return self.fro(far[:half], "z", -1), self.fro(far[half:], "z", 1)

    def z_scatter_go(self, parts, begun):
        n = self.sizes["z"]
        if n != 4:
            return [self.fro(parts[oz], "z", -oz) for oz in range(1, n)]
        half = halfway(parts[0].shape[0])
        above = jnp.concatenate([add_low(parts[1][:half], begun[0]), parts[1][half:]], axis=0)
        below = jnp.concatenate([parts[3][:half], add_low(parts[3][half:], begun[1])], axis=0)
        return [self.fro(above, "z", -1), self.fro(below, "z", 1)]

    def z_scatter(self, parts):
        return [parts[0], *self.z_scatter_go(parts, self.z_scatter_begin(parts[len(parts) // 2]))]


SEQ = ("u", "y", "c")
CTX = ("z", "v", "x")
ACROSS = ("v", "x")


def make_shards(sizes):
    ways = Ways(sizes)
    ns, nctx, nx = ways.size(SEQ), ways.size(CTX), ways.size(ACROSS)
    nz, nc = sizes["z"], sizes["c"]
    devices = ns * nctx
    places, outers = ways.places(), ways.outers()

    def from_outers(value):
        if len(outers) == 1:
            return value
        return jnp.concatenate(
            [ways.fro(ways.fro(value, "u", ou), "v", ov) for ou, ov in outers], axis=0
        )

    def to_outers(value):
        if len(outers) == 1:
            return value
        rows = value.shape[0] // len(outers)
        return add_low(
            *[
                ways.fro(ways.fro(value[i * rows : (i + 1) * rows], "u", -ou), "v", -ov)
                for i, (ou, ov) in enumerate(outers)
            ]
        )

    def plane_rows(value, *beside):
        found, beside = ways.plane_gather(value, beside or (None, None))
        return [block for p in places for block in found[p]], beside

    def by_device(parts):
        return {p: parts[i * nc : (i + 1) * nc] for i, p in enumerate(places)}

    def shards(
        tokens, cotangent, segments, positions, attn_w, attn_m, attn_v,
        mlp_w, mlp_m, mlp_v, gains, gain_m, gain_v,
    ):
        at = {a: lax.axis_index(a) for a in sizes}
        seq_place = lax.axis_index(SEQ)
        across_place = lax.axis_index(ACROSS)
        ctx_place = at["z"] * nx + across_place
        device = seq_place * nctx + ctx_place
        piece, gain_piece = attn_w.shape[0], gains.shape[0]
        flat = Flat(piece, gain_piece, devices)

        sides = [sizes[a] for a in ("x", "y", "c", "u", "v", "z")]
        here = [at[a] for a in ("x", "y", "c", "u", "v", "z")]
        ox, oy, oc, ou, ov, oz = (
            (jnp.asarray(o, jnp.int32) + h) % n
            for o, h, n in zip(np.unravel_index(np.arange(devices), sides), here, sides)
        )
        order = ((ou * sizes["y"] + oy) * sizes["c"] + oc) * nz + oz
        order = (order * sizes["v"] + ov) * sizes["x"] + ox

        ways.what = "attn_gather"
        gain_offset = gain_piece * device % LANES
        gain_window = lax.dynamic_update_slice(
            jnp.zeros((16 * LANES,), bf16), gains.astype(bf16), (gain_offset,)
        )
        low_piece = jnp.concatenate(
            [
                jnp.pad(
                    attn_w.astype(bf16).reshape(flat.lines, LANES),
                    ((0, flat.gain_at - flat.lines), (0, 0)),
                ),
                gain_window.reshape(16, LANES),
            ],
            axis=0,
        )
        ways.what = "unit_exchange"
        units, width = mlp_w.shape
        share = units // ns
        held = -(-share // 32) * 32

        def seq_send(by_place):
            return [ways.fro(v, SEQ, offset) for offset, v in enumerate(seq_parts(by_place))]

        def seq_parts(by_place):
            return [
                lax.dynamic_index_in_dim(by_place, (seq_place - offset) % ns, 0, keepdims=False)
                for offset in range(ns)
            ]

        def seq_place_all(heard):
            kept = jnp.zeros((ns,) + heard[0].shape, heard[0].dtype)
            for offset, value in enumerate(heard):
                kept = lax.dynamic_update_index_in_dim(kept, value, (seq_place + offset) % ns, 0)
            return kept

        sent = seq_parts(mlp_w.astype(bf16).reshape(ns, share, width))
        sent, low_piece = lax.optimization_barrier((sent, low_piece))
        heard = [ways.fro(v, SEQ, offset) for offset, v in enumerate(sent)]
        ways.what = "attn_gather"
        line_blocks = ways.z_gather(low_piece)
        line_blocks, heard = lax.optimization_barrier((line_blocks, heard))
        by_cols = seq_place_all(heard)
        rows_own = jnp.concatenate([by_cols[i] for i in range(ns)], axis=1)
        rows_own = jnp.pad(rows_own, ((0, held - share), (0, 0)))
        ways.what = "attn_gather"
        line_z, rows_own = lax.optimization_barrier(
            (from_outers(jnp.concatenate(line_blocks, axis=0)), rows_own)
        )
        def next_units(ring, *beside):
            if beside:
                ring[-1], *beside = lax.optimization_barrier((ring[-1],) + beside)
            what, ways.what = ways.what, "unit_gather"
            ring.append(ways.fro(ring[-1], "z", 1))
            ways.what = what
            return beside[0] if len(beside) == 1 else beside

        steps = nz == 4
        cut = halfway(held)
        whole = [rows_own]
        next_units(whole)
        gathered, _ = ways.plane_gather(line_z)
        line_parts = [part.reshape(-1, flat.rows, LANES) for p in places for part in gathered[p]]
        line_parts, whole[-1] = lax.optimization_barrier((line_parts, whole[-1]))
        rings = [[v[:cut] for v in whole], [v[cut:] for v in whole]]
        if steps:
            next_units(rings[0])
        else:
            for ring in rings:
                for _ in range(2, nz):
                    next_units(ring)

        tok_rows = tokens.shape[1]
        cosine, sine = angles(positions[0])
        (
            w_qkv, g_pre, g_q, g_k, g_post, g_fpre, g_fpost, normed_in, query, kv_local, raw,
        ) = first_part(flat, line_parts, order, tokens[0], cosine, sine)
        w_out = spread_out(flat, [after(part, kv_local) for part in line_parts], order)
        ways.what = "kv_gather"
        if steps:
            half = halfway(tok_rows)
            above, below = ways.z_begin(kv_local)
            above, below, rings[0][-1] = next_units(rings[1], above, below, rings[0][-1])
            far = ways.fro(above[:half], "z", 1), ways.fro(below[half:], "z", -1)
            far = next_units(rings[0], *far)
            kv_blocks = [kv_local, above, jnp.concatenate(far, axis=0), below]
        else:
            kv_blocks = ways.z_gather(kv_local)
        kv_all = jnp.stack([ways.fro(block, ACROSS, oa) for block in kv_blocks for oa in range(nx)])

        doc_all = segments[0]
        first_docs, last_docs = doc_all[::tok_rows], doc_all[tok_rows - 1 :: tok_rows]
        key_at = np.arange(nctx)
        key_place = (at["z"] + jnp.asarray(key_at // nx, jnp.int32)) % nz * nx
        key_place = key_place + (across_place + jnp.asarray(key_at % nx, jnp.int32)) % nx
        is_place = key_place[:, None] == jnp.arange(nctx, dtype=jnp.int32)[None, :]
        key_first = jnp.sum(jnp.where(is_place, first_docs[None, :], 0), axis=1)
        key_last = jnp.sum(jnp.where(is_place, last_docs[None, :], 0), axis=1)
        live = (key_place < ctx_place) & (key_last >= key_first[0])
        one_doc = key_first == key_last[0]
        task = jnp.where(live, jnp.where(one_doc, WHOLE, MASKED), DEAD)
        task = jnp.where(key_place == ctx_place, MASKED, task)
        info = jnp.stack([key_place, task]).astype(jnp.int32)
        key_docs = doc_all[:, None]
        query_docs = lax.dynamic_slice_in_dim(doc_all, ctx_place * tok_rows, tok_rows)[None]

        heads, log_total, attn_out, middle, ffn_in = attend(
            info, query, kv_all, key_docs, query_docs, w_out, tokens[0], g_post, g_fpre
        )

        ways.what = "ffn_in_gather"
        if steps:
            ffn_in = next_units(rings[1], ffn_in)
            ffn_rows, (rings[0][-1], rings[1][-1]) = plane_rows(ffn_in, rings[0][-1], rings[1][-1])
        else:
            ffn_rows, _ = plane_rows(ffn_in)
        units_here = [from_outers(block) for block in whole[:nz]]
        units_here += [from_outers(block) for pair in zip(rings[0][2:], rings[1][2:]) for block in pair]
        act, gelu, slope, parts = ffn_forward(ffn_rows, units_here)
        ways.what = "ffn_out_sum"
        out_parts = ways.plane_scatter(by_device(parts))
        mixed, d_mlp_out, d_gfpost = after_ffn(out_parts, middle, cotangent[0], g_fpost)

        ways.what = "d_out_gather"
        d_out_rows, _ = plane_rows(d_mlp_out)
        per = units_here[0].shape[0]

        def z_step(blocks, far, *earlier):
            value = blocks[far] if not earlier else add_low(blocks[far], *earlier)
            return ways.fro(value, "z", -1)

        class Ring:
            def __init__(self, name, blocks):
                self.name, self.blocks, self.at, self.heard = name, [to_outers(b) for b in blocks], nz, None

            def step(self, beside=None):
                if not steps:
                    return beside
                if self.heard is not None and beside is not None:
                    self.heard, beside = lax.optimization_barrier((self.heard, beside))
                self.at -= 1
                if self.at > 0:
                    value = self.blocks[self.at]
                    if self.heard is not None:
                        value = add_low(value, self.heard)
                    what, ways.what = ways.what, self.name
                    self.heard = ways.fro(value, "z", -1)
                    ways.what = what
                return beside

            def result(self):
                if steps:
                    return add_low(self.blocks[0], self.heard)
                return add_low(*[ways.fro(v, "z", -i) for i, v in enumerate(self.blocks)])

        down = Ring("down_grad_sum", unit_grads(act, 0, nz, per, d_out_rows))
        down.step()
        d_out_rows[0] = after(d_out_rows[0], down.blocks[0])
        d_both, parts = ffn_backward(d_out_rows, gelu, slope, units_here)
        parts[-1] = down.step(parts[-1])
        rings = {}

        def gate_then(low):
            low, both = lax.optimization_barrier((low, d_both))
            rings["gate"] = Ring("gate_grad_sum", unit_grads(both, 0, nz, per, ffn_rows))
            rings["gate"].step()
            return low

        def up_then(summed):
            summed = down.step(summed)
            summed, both = lax.optimization_barrier((summed, d_both))
            rings["up"] = Ring("up_grad_sum", unit_grads(both, 1, nz, per, ffn_rows))
            rings["up"].step()
            return summed

        ways.what = "d_in_sum"
        d_in_parts = ways.plane_scatter(by_device(parts), gate_then, up_then)
        d_in_parts = lax.optimization_barrier((d_in_parts, rings["up"].blocks[0]))[0]
        d_in_parts = rings["gate"].step(d_in_parts)

        d_query, d_attn_out, d_middle, d_gfpre, d_gpost, *d_kv = attend_back(
            info, query, kv_all, key_docs, query_docs, heads, log_total, d_in_parts, middle, attn_out,
            cotangent[0], w_out, g_post, g_fpre,
        )
        d_kv = rings["up"].step(d_kv)
        d_kv = down.step(d_kv)
        ways.what = "kv_sum"

        def across(oz):
            return [ways.fro(d_kv[oz * nx + oa], ACROSS, -oa) for oa in range(nx)]

        far = nz // 2
        kv_parts = {far: add_low(*across(far))}
        near = {oz: across(oz) for oz in range(nz) if oz != far}
        begun = ways.z_scatter_begin(kv_parts[far])
        near, begun = rings["gate"].step(lax.optimization_barrier((near, begun)))
        kv_parts.update({oz: add_low(*terms) for oz, terms in near.items()})
        kv_parts = [kv_parts[0], *ways.z_scatter_go(kv_parts, begun)]
        kv_parts = rings["up"].step(kv_parts)
        lines, da_query, d_gq = query_side(
            flat, after(d_query, *near[0]), raw, cosine, sine, g_q, normed_in, w_qkv, heads, d_attn_out
        )
        input_grad, *packed = last_part(
            flat, order, len(places) * nc, lines, kv_parts, raw, cosine, sine, g_k, normed_in, w_qkv, tokens[0],
            g_pre, d_middle, da_query, [d_gq, d_gpost, d_gfpre, d_gfpost],
        )

        ways.what = "attn_grad_sum"
        packed = [part.reshape(-1, LANES) for part in packed]
        terms = ways.plane_scatter({p: packed[i * nc : (i + 1) * nc] for i, p in enumerate(places)})
        owned = [rings["gate"].result(), rings["up"].result(), down.result()]
        own_rows = jnp.concatenate([v[:share] for v in owned], axis=1)
        by_cols = jnp.stack([own_rows[:, i * width : (i + 1) * width] for i in range(ns)])
        terms, by_cols = lax.optimization_barrier((terms, by_cols))
        plane_sum = to_outers(add_low(*terms))

        ways.what = "grad_exchange"
        mlp_red = seq_place_all(seq_send(by_cols)).astype(f32).reshape(units, width)
        mlp_m_new, mlp_v_new, mlp_new = adam_update(
            mlp_w, mlp_m, mlp_v, mlp_red, RATE_MATRIX, DECAY_MATRIX
        )

        ways.what = "attn_grad_sum"
        terms = ways.z_scatter([plane_sum[oz * flat.rows : (oz + 1) * flat.rows] for oz in range(nz)])
        terms, mlp_new = lax.optimization_barrier((terms, mlp_new))
        red = sum(part.astype(f32) for part in terms)
        attn_red = red[: flat.lines].reshape(-1)
        gain_red = lax.dynamic_slice(red[flat.gain_at :].reshape(-1), (gain_offset,), (gain_piece,))

        attn_m_new, attn_v_new, attn_new = adam_update(
            attn_w, attn_m, attn_v, attn_red, RATE_MATRIX, DECAY_MATRIX
        )
        gain_m_new, gain_v_new, gain_new = adam_update(
            gains, gain_m, gain_v, gain_red, RATE_GAIN, 0.0
        )
        return (
            mixed[None], input_grad[None],
            attn_red, attn_m_new, attn_v_new, attn_new,
            mlp_red, mlp_m_new, mlp_v_new, mlp_new,
            gain_red, gain_m_new, gain_v_new, gain_new,
        )

    return shards


def solution(mesh):
    seq, ctx = mesh.shape["seq"], mesh.shape["ctx"]
    nz = 4 if ctx % 4 == 0 else 1
    chips_y, chips_x = seq // 2, ctx // nz
    y, x = 2 - chips_y % 2, 2 - chips_x % 2
    sizes = {"u": chips_y // y, "y": y, "c": 2, "z": nz, "v": chips_x // x, "x": x}
    fine = Mesh(mesh.devices.reshape(*sizes.values()), tuple(sizes))
    s, x = SEQ, CTX
    both = s + x
    in_specs = (
        P(s, x, None), P(s, x, None), P(s, None), P(s, x),
        P(both), P(both), P(both),
        P(x, s), P(x, s), P(x, s),
        P(both), P(both), P(both),
    )
    out_specs = (
        P(s, x, None), P(s, x, None),
        P(both), P(both), P(both), P(both),
        P(x, s), P(x, s), P(x, s), P(x, s),
        P(both), P(both), P(both), P(both),
    )
    return jax.shard_map(
        make_shards(sizes), mesh=fine, in_specs=in_specs, out_specs=out_specs, check_vma=False
    )
```

```python
import jax
import jax.numpy as jnp
import numpy as np
from jax import lax
from jax.experimental import pallas as pl
from jax.experimental.pallas import tpu as pltpu
from jax.sharding import Mesh, PartitionSpec as P

D = 1152
H = 4
HD = 256
STEP = 5

NORM_EPS = 1e-06
SCORE_FLOOR = -1e30
ROPE_BASE = 1000000.0
BETA_MOMENT = 0.5
ADAM_EPS = 1e-08
RATE_MATRIX = 0.03
RATE_GAIN = 0.5
DECAY_MATRIX = 0.1

bf16 = jnp.bfloat16
f32 = jnp.float32
LANES = 128


def normed(value):
    factor = lax.rsqrt(jnp.mean(value * value, axis=-1, keepdims=True) + NORM_EPS)
    return (value * factor, factor)


def norm_back(unit, factor, d_unit):
    return factor * (d_unit - unit * jnp.mean(d_unit * unit, axis=-1, keepdims=True))


def angles(position):
    half_index = jnp.arange(HD // 2, dtype=f32)
    frequency = jnp.exp(half_index * (-2.0 * jnp.log(ROPE_BASE) / HD))
    angle = position.astype(f32)[:, None] * frequency[None, :]
    return (jnp.cos(angle), jnp.sin(angle))


def rotate(value, cosine, sine):
    half_width = value.shape[-1] // 2
    first_half = value[..., :half_width]
    second_half = value[..., half_width:]
    return jnp.concatenate(
        [first_half * cosine - second_half * sine, second_half * cosine + first_half * sine],
        axis=-1,
    )


def contract(left, right, left_dim, right_dim):
    return lax.dot_general(
        left, right, (((left_dim,), (right_dim,)), ((), ())), preferred_element_type=f32
    )


def adam_update(weight, moment_one, second, gradient, learn_rate, decay_rate):
    moment_new = BETA_MOMENT * moment_one + (1.0 - BETA_MOMENT) * gradient
    second_new = BETA_MOMENT * second + (1.0 - BETA_MOMENT) * gradient * gradient
    correction = 1.0 - BETA_MOMENT**STEP
    update = moment_new / correction / (jnp.sqrt(second_new / correction) + ADAM_EPS)
    return (moment_new, second_new, weight - learn_rate * (update + decay_rate * weight))


def add_low(*parts):
    total = parts[0].astype(f32)
    for part in parts[1:]:
        total = total + part.astype(f32)
    return total.astype(bf16)


def after(value, *earlier):
    return lax.optimization_barrier((value,) + earlier)[0]


def halfway(rows):
    return rows // 32 * 16 if rows >= 32 else rows // 2


VMEM_LIMIT = 56 * 1024 * 1024
VMEM_LIMITS = {"after_ffn": 40 * 1024 * 1024}
SCORE_SCALE = HD ** (-0.5)
SPACES = {"v": pltpu.VMEM, "h": pl.ANY, "s": pltpu.SMEM}


def run(name, body, operands, spaces, out_shape, scratch=(), out_spaces=None, flops=0):
    return pl.pallas_call(
        body,
        out_shape=tuple(jax.ShapeDtypeStruct(s, d) for s, d in out_shape),
        in_specs=[pl.BlockSpec(memory_space=SPACES[s]) for s in spaces],
        out_specs=tuple(
            pl.BlockSpec(memory_space=SPACES[s]) for s in out_spaces or "v" * len(out_shape)
        ),
        scratch_shapes=list(scratch),
        compiler_params=pltpu.CompilerParams(vmem_limit_bytes=VMEM_LIMITS.get(name, VMEM_LIMIT)),
        cost_estimate=pl.CostEstimate(flops=flops, bytes_accessed=0, transcendentals=0),
        name=name,
    )(*operands)


class Flat:
    def __init__(self, piece, gain_piece, devices):
        self.devices = devices
        self.lines = piece // LANES
        self.gain_at = -(-self.lines // 16) * 16
        self.gain_piece = gain_piece
        self.rows = self.gain_at + 16
        self.q_across, self.o_across = (H + 2) * HD // LANES, D // LANES
        self.q_lines, self.o_lines = D * self.q_across, H * HD * self.o_across
        widths = [D, HD, HD, D, D, D]
        self.gain_rows = [w // LANES for w in widths]
        self.gain_lines = sum(self.gain_rows)

        across, kv = self.q_across, 2 * HD // LANES
        self.kv_across = kv
        self.late_rows = self.lines // across + (2 if self.lines % across else 0)
        self.late_lines = -(-self.late_rows * kv // 16) * 16

    def first_row(self, device):
        return self.lines * device // self.q_across

    def gain_line(self, device):
        return self.gain_piece * device // LANES


def fetch(order_ref, sources, held, sems):
    copies = []
    for source in sources:
        for i in range(source.shape[0]):
            k = len(copies)
            copies.append(pltpu.make_async_copy(source.at[i], held.at[order_ref[k]], sems.at[k]))
    for copy in copies:
        copy.start()
    return copies


def first_part(flat, parts, order, tokens, cosine, sine):
    tok_rows = tokens.shape[0]
    wide = (H + 2) * HD
    blocks = -(-flat.q_lines // flat.lines)

    def body(order_ref, *refs):
        sources = refs[: len(parts)]
        (
            tok_ref, cos_ref, sin_ref, w_ref, g_pre, g_q, g_k, g_post, g_fpre, g_fpost,
            a_ref, q_ref, kv_ref, raw_ref, held, lines, gains, sems,
        ) = refs[len(parts) :]
        copies = fetch(order_ref, sources, held, sems)
        unit, _ = normed(tok_ref[...].astype(f32))
        gains[...] = jnp.zeros_like(gains)
        for copy in copies:
            copy.wait()
        for i in range(flat.devices):
            at = flat.gain_line(i)
            gains[at : at + 3, :] += held[i, flat.gain_at :, :].astype(f32)[:3]
        at = 0
        for ref, rows in zip((g_pre, g_q, g_k, g_post, g_fpre, g_fpost), flat.gain_rows):
            for i in range(rows):
                ref[:, i * LANES : (i + 1) * LANES] = gains[at + i : at + i + 1, :]
            at += rows
        a_ref[...] = (unit * g_pre[...]).astype(bf16)
        for i in range(blocks):
            lines[i * flat.lines : (i + 1) * flat.lines, :] = held[i, : flat.gain_at, :].astype(f32)[
                : flat.lines
            ]
        for j in range(flat.q_across):
            w_ref[:, j * LANES : (j + 1) * LANES] = lines[
                pl.ds(j, D, stride=flat.q_across), :
            ].astype(bf16)
        qkv = contract(a_ref[...], w_ref[...], 1, 0)
        raw_ref[...] = qkv[:, : (H + 1) * HD]
        cos, sin = cos_ref[...], sin_ref[...]
        for h in range(H):
            head = normed(qkv[:, h * HD : (h + 1) * HD])[0] * g_q[...]
            low = rotate(head, cos, sin).astype(bf16)
            q_ref[:, h * HD : (h + 1) * HD] = (low.astype(f32) * SCORE_SCALE).astype(bf16)
        key = normed(qkv[:, H * HD : (H + 1) * HD])[0] * g_k[...]
        kv_ref[:, :HD] = rotate(key, cos, sin).astype(bf16)
        kv_ref[:, HD:] = qkv[:, (H + 1) * HD :].astype(bf16)

    row = [((1, w * LANES), f32) for w in flat.gain_rows]
    return run(
        "first_part",
        body,
        [order, *parts, tokens, cosine, sine],
        "s" + "h" * len(parts) + "vvv",
        [((D, wide), bf16), *row]
        + [((tok_rows, D), bf16), ((tok_rows, H * HD), bf16), ((tok_rows, 2 * HD), bf16)]
        + [((tok_rows, (H + 1) * HD), f32)],
        [
            pltpu.VMEM((flat.devices, flat.rows, LANES), bf16),
            pltpu.VMEM((blocks * flat.lines + 16, LANES), f32),
            pltpu.VMEM((-(-(flat.gain_lines + 3) // 8) * 8, LANES), f32),
            pltpu.SemaphoreType.DMA((flat.devices,)),
        ],
        flops=8 * 2 * tok_rows * D * wide,
    )


def spread_out(flat, parts, order):
    start = flat.q_lines // flat.lines

    def body(order_ref, *refs):
        sources = refs[: len(parts)]
        w_ref, held, lines, sems = refs[len(parts) :]
        for copy in fetch(order_ref, sources, held, sems):
            copy.wait()
        for i in range(start, flat.devices):
            at = (i - start) * flat.lines
            lines[at : at + flat.lines, :] = held[i, : flat.gain_at, :].astype(f32)[: flat.lines]
        for j in range(flat.o_across):
            w_ref[:, j * LANES : (j + 1) * LANES] = lines[
                pl.ds(flat.q_lines - start * flat.lines + j, H * HD, stride=flat.o_across), :
            ].astype(bf16)

    return run(
        "spread_out",
        body,
        [order, *parts],
        "s" + "h" * len(parts),
        [((H * HD, D), bf16)],
        [
            pltpu.VMEM((flat.devices, flat.rows, LANES), bf16),
            pltpu.VMEM(((flat.devices - start) * flat.lines + 16, LANES), f32),
            pltpu.SemaphoreType.DMA((flat.devices,)),
        ],
    )[0]


DEAD, WHOLE, MASKED = 0, 1, 2


def allowed_of(kdoc_ref, qdoc_ref, shift):
    keys, queries = kdoc_ref.shape[0], qdoc_ref.shape[1]
    key_at = lax.broadcasted_iota(jnp.int32, (keys, queries), 0) + shift
    query_at = lax.broadcasted_iota(jnp.int32, (keys, queries), 1)
    return (kdoc_ref[...] == qdoc_ref[...]) & (key_at <= query_at)


def same(shape):
    return pl.BlockSpec(shape, lambda i, info: (0,) * len(shape))


def attend(info, query, kv, key_docs, query_docs, w_out, tokens, g_post, g_fpre):
    blocks, rows, _ = kv.shape

    def body(
        info_ref, q_ref, kv_ref, kdoc_ref, qdoc_ref, w_ref, tok_ref, g_post_ref, g_fpre_ref,
        o_ref, lse_ref, out_ref, mid_ref, in_ref, peak, total, acc,
    ):
        step = pl.program_id(0)

        @pl.when(step == 0)
        def _():
            peak[...] = jnp.full_like(peak, SCORE_FLOOR)
            total[...] = jnp.zeros_like(total)
            acc[...] = jnp.zeros_like(acc)

        def visit(masked):
            key = kv_ref[0, :, :HD]
            value_t = kv_ref[0, :, HD:].T
            if masked:
                allowed = allowed_of(
                    kdoc_ref, qdoc_ref, (info_ref[0, step] - info_ref[0, 0]) * rows
                )
            for h in range(H):
                score = contract(key, q_ref[:, h * HD : (h + 1) * HD], 1, 1)
                if masked:
                    score = jnp.where(allowed, score, SCORE_FLOOR)
                old = peak[h : h + 1, :]
                new = jnp.maximum(old, jnp.max(score, axis=0, keepdims=True))
                weight = jnp.exp(score - new)
                shrink = jnp.exp(old - new)
                peak[h : h + 1, :] = new
                total[h : h + 1, :] = total[h : h + 1, :] * shrink + jnp.sum(
                    weight, axis=0, keepdims=True
                )
                acc[h] = acc[h] * shrink + contract(value_t, weight.astype(bf16), 1, 0)

        pl.when(info_ref[1, step] == WHOLE)(lambda: visit(False))
        pl.when(info_ref[1, step] == MASKED)(lambda: visit(True))

        @pl.when(step == blocks - 1)
        def _():
            lse_ref[...] = jnp.zeros_like(lse_ref)
            for h in range(H):
                lse_ref[h : h + 1, :] = peak[h : h + 1, :] + jnp.log(total[h : h + 1, :])
                o_ref[:, h * HD : (h + 1) * HD] = (acc[h] / total[h : h + 1, :]).T.astype(bf16)
            attn_out = contract(o_ref[...], w_ref[...], 1, 0)
            out_ref[...] = attn_out
            middle = tok_ref[...].astype(f32) + normed(attn_out)[0] * g_post_ref[...]
            mid_ref[...] = middle
            in_ref[...] = (normed(middle)[0] * g_fpre_ref[...]).astype(bf16)

    return pl.pallas_call(
        body,
        grid_spec=pltpu.PrefetchScalarGridSpec(
            num_scalar_prefetch=1,
            grid=(blocks,),
            in_specs=[
                same((rows, H * HD)),
                pl.BlockSpec((1, rows, 2 * HD), lambda i, info: (i, 0, 0)),
                pl.BlockSpec((rows, 1), lambda i, info: (info[0, i], 0)),
                same((1, rows)),
                same((H * HD, D)),
                same((rows, D)),
                same((1, D)),
                same((1, D)),
            ],
            out_specs=[
                same((rows, H * HD)),
                same((8, rows)),
                same((rows, D)),
                same((rows, D)),
                same((rows, D)),
            ],
            scratch_shapes=[
                pltpu.VMEM((8, rows), f32),
                pltpu.VMEM((8, rows), f32),
                pltpu.VMEM((H, HD, rows), f32),
            ],
        ),
        out_shape=(
            jax.ShapeDtypeStruct((rows, H * HD), bf16),
            jax.ShapeDtypeStruct((8, rows), f32),
            jax.ShapeDtypeStruct((rows, D), f32),
            jax.ShapeDtypeStruct((rows, D), f32),
            jax.ShapeDtypeStruct((rows, D), bf16),
        ),
        compiler_params=pltpu.CompilerParams(vmem_limit_bytes=44 * 1024 * 1024),
        cost_estimate=pl.CostEstimate(
            flops=8 * 4 * blocks * rows * rows * H * HD, bytes_accessed=0, transcendentals=0
        ),
        name="attend",
    )(info, query, kv, key_docs, query_docs, w_out, tokens, g_post, g_fpre)


def attend_back(
    info, query, kv, key_docs, query_docs, heads, log_total, d_in, middle, attn_out, cotangent,
    w_out, g_post, g_fpre,
):
    blocks, rows, _ = kv.shape
    terms = len(d_in)

    def body(info_ref, q_ref, kv_ref, kdoc_ref, qdoc_ref, o_ref, lse_ref, *refs):
        terms_ref = refs[:terms]
        (
            mid_ref, out_ref, cot_ref, w_ref, g_post_ref, g_fpre_ref,
            dq_ref, dout_ref, dmid_ref, dg_fpre_ref, dg_post_ref, *dkv_refs, do_ref, delta_ref,
        ) = refs[terms:]
        step = pl.program_id(0)

        def give(d_key, d_value):
            for k, ref in enumerate(dkv_refs):

                @pl.when(step == k)
                def _(ref=ref):
                    ref[:, :HD] = d_key.astype(bf16)
                    ref[:, HD:] = d_value.astype(bf16)

        @pl.when(step == 0)
        def _():
            d_rows = sum(ref[...].astype(f32) for ref in terms_ref)
            unit, scale = normed(mid_ref[...])
            dg_fpre_ref[...] = jnp.sum(d_rows * unit, axis=0, keepdims=True)
            d_middle = cot_ref[...].astype(f32) + norm_back(unit, scale, d_rows * g_fpre_ref[...])
            dmid_ref[...] = d_middle
            unit, scale = normed(out_ref[...])
            dg_post_ref[...] = jnp.sum(d_middle * unit, axis=0, keepdims=True)
            d_out = norm_back(unit, scale, d_middle * g_post_ref[...]).astype(bf16)
            dout_ref[...] = d_out
            delta_ref[...] = jnp.zeros_like(delta_ref)
            for h in range(H):
                cols = slice(h * HD, (h + 1) * HD)
                d_o = contract(d_out, w_ref[cols, :], 1, 1).astype(bf16)
                do_ref[:, cols] = d_o
                each = (d_o.astype(f32) * o_ref[:, cols].astype(f32)).T
                delta_ref[h : h + 1, :] = jnp.sum(each, axis=0, keepdims=True)
            dq_ref[...] = jnp.zeros_like(dq_ref)

        def visit(masked):
            key, value = kv_ref[0, :, :HD], kv_ref[0, :, HD:]
            if masked:
                allowed = allowed_of(
                    kdoc_ref, qdoc_ref, (info_ref[0, step] - info_ref[0, 0]) * rows
                )
            d_key = jnp.zeros((rows, HD), f32)
            d_value = jnp.zeros((rows, HD), f32)
            for h in range(H):
                cols = slice(h * HD, (h + 1) * HD)
                q, d_o = q_ref[:, cols], do_ref[:, cols]
                prob = jnp.exp(contract(key, q, 1, 1) - lse_ref[h : h + 1, :])
                if masked:
                    prob = jnp.where(allowed, prob, 0.0)
                d_value = d_value + contract(prob.astype(bf16), d_o, 1, 0)
                d_prob = contract(value, d_o, 1, 1)
                d_score = (prob * (d_prob - delta_ref[h : h + 1, :])).astype(bf16)
                d_key = d_key + contract(d_score, q, 1, 0)
                dq_ref[:, cols] = dq_ref[:, cols] + contract(d_score, key, 0, 0)
            give(d_key, d_value)

        pl.when(info_ref[1, step] == WHOLE)(lambda: visit(False))
        pl.when(info_ref[1, step] == MASKED)(lambda: visit(True))

        @pl.when(info_ref[1, step] == DEAD)
        def _():
            give(jnp.zeros((rows, HD), f32), jnp.zeros((rows, HD), f32))

        @pl.when(step == blocks - 1)
        def _():
            dq_ref[...] = dq_ref[...] * SCORE_SCALE

    block = pl.BlockSpec((1, rows, 2 * HD), lambda i, info: (i, 0, 0))
    resident = pl.BlockSpec(memory_space=pltpu.VMEM)
    return pl.pallas_call(
        body,
        grid_spec=pltpu.PrefetchScalarGridSpec(
            num_scalar_prefetch=1,
            grid=(blocks,),
            in_specs=[
                resident,
                block,
                pl.BlockSpec((rows, 1), lambda i, info: (info[0, i], 0)),
                resident,
                resident,
                resident,
                *[resident] * (terms + 3),
                resident,
                resident,
                resident,
            ],
            out_specs=[
                resident,
                resident,
                resident,
                resident,
                resident,
                *[resident] * blocks,
            ],
            scratch_shapes=[pltpu.VMEM((rows, H * HD), bf16), pltpu.VMEM((8, rows), f32)],
        ),
        out_shape=(
            jax.ShapeDtypeStruct((rows, H * HD), f32),
            jax.ShapeDtypeStruct((rows, D), bf16),
            jax.ShapeDtypeStruct((rows, D), f32),
            jax.ShapeDtypeStruct((1, D), f32),
            jax.ShapeDtypeStruct((1, D), f32),
            *[jax.ShapeDtypeStruct((rows, 2 * HD), bf16)] * blocks,
        ),
        compiler_params=pltpu.CompilerParams(vmem_limit_bytes=44 * 1024 * 1024),
        cost_estimate=pl.CostEstimate(flops=0, bytes_accessed=0, transcendentals=0),
        name="attend_back",
    )(
        info, query, kv, key_docs, query_docs, heads, log_total, *d_in, middle, attn_out, cotangent,
        w_out, g_post, g_fpre,
    )


def gelu_parts(gate):
    scale = 0.7978845608028654
    square = gate * gate
    inner = jnp.tanh(scale * gate * (1.0 + 0.044715 * square))
    half_up = 0.5 * (1.0 + inner)
    slope = half_up + 0.5 * gate * (1.0 - inner * inner) * scale * (1.0 + 3 * 0.044715 * square)
    return gate * half_up, slope


def gather_rows(refs, held, sems):
    tok = refs[0].shape[0]
    return [
        pltpu.make_async_copy(ref, held.at[k * tok : (k + 1) * tok], sems.at[k])
        for k, ref in enumerate(refs)
    ]


def scatter_rows(held, refs, sems):
    tok = refs[0].shape[0]
    return [
        pltpu.make_async_copy(held.at[k * tok : (k + 1) * tok], ref, sems.at[k])
        for k, ref in enumerate(refs)
    ]


def by_chunk(step, chunks, copies, do):
    per = len(copies) // chunks
    for k in range(chunks):

        @pl.when(step == k)
        def _(k=k):
            for copy in copies[k * per : (k + 1) * per]:
                do(copy)


def ffn_call(name, body, rows, streams, weights, outs, order):
    count, (tok, wide) = len(rows), rows[0].shape
    chunks = -(-count * tok // 512)
    both = count * tok // chunks
    blocks = len(weights)
    starts = np.cumsum([0] + [w.shape[0] for w in weights]).tolist()
    per = starts[-1]

    def kernel(*refs):
        row_refs, refs = refs[:count], refs[count:]
        stream_refs, refs = refs[: len(streams)], refs[len(streams) :]
        w_refs, refs = refs[:blocks], refs[blocks:]
        out_refs, refs = refs[: len(outs)], refs[len(outs) :]
        sum_refs, (held, given, units, sems_in, sems_out, sems_w) = refs[:count], refs[count:]
        step = pl.program_id(0)
        coming = gather_rows(row_refs, held, sems_in)
        going = scatter_rows(given, sum_refs, sems_out)
        brought = {
            k: [
                pltpu.make_async_copy(
                    ref.at[:, k * D : (k + 1) * D],
                    units.at[k, starts[i] : starts[i + 1]],
                    sems_w.at[k * blocks + i],
                )
                for i, ref in enumerate(w_refs)
            ]
            for k in order
        }

        @pl.when(step == 0)
        def _():
            first = len(coming) // chunks
            bringing = [c for k in order for c in brought[k]]
            for copy in coming[:first] + bringing + coming[first:]:
                copy.start()

        by_chunk(step, chunks, coming, lambda copy: copy.wait())
        here = pl.ds(pl.multiple_of(step * both, both), both)

        def arrived(k):
            for copy in brought[k]:
                copy.wait()
            return units[k]

        @pl.when(step == 0)
        def _():
            given[here, :] = body(held[here, :], stream_refs, arrived, out_refs)

        @pl.when(step > 0)
        def _():
            given[here, :] = body(held[here, :], stream_refs, lambda k: units[k], out_refs)

        by_chunk(step, chunks, going, lambda copy: copy.start())

        @pl.when(step == chunks - 1)
        def _():
            for copy in going:
                copy.wait()

    def chunk(width):
        return pl.BlockSpec((both, width), lambda i: (i, 0))

    anywhere = pl.BlockSpec(memory_space=pl.ANY)
    return pl.pallas_call(
        kernel,
        grid=(chunks,),
        in_specs=[anywhere] * count
        + [chunk(s.shape[1]) for s in streams]
        + [anywhere] * blocks,
        out_specs=tuple([chunk(w) for w in outs] + [anywhere] * count),
        out_shape=tuple(
            [jax.ShapeDtypeStruct((count * tok, w), bf16) for w in outs]
            + [jax.ShapeDtypeStruct((tok, wide), bf16)] * count
        ),
        scratch_shapes=[
            pltpu.VMEM((count * tok, wide), bf16),
            pltpu.VMEM((count * tok, wide), bf16),
            pltpu.VMEM((3, per, D), bf16),
            pltpu.SemaphoreType.DMA((count,)),
            pltpu.SemaphoreType.DMA((count,)),
            pltpu.SemaphoreType.DMA((3 * blocks,)),
        ],
        compiler_params=pltpu.CompilerParams(vmem_limit_bytes={"ffn_forward": 46, "ffn_backward": 46}[name] * 1024 * 1024),
        cost_estimate=pl.CostEstimate(
            flops=6 * count * tok * per * D, bytes_accessed=0, transcendentals=0
        ),
        name=name,
    )(*rows, *streams, *weights)


def ffn_forward(rows, weights):
    def body(x, _, weight, out_refs):
        act_ref, gelu_ref, slope_ref = out_refs
        gate = contract(x, weight(0), 1, 1)
        up = contract(x, weight(1), 1, 1)
        gelu, slope = gelu_parts(gate)
        act = (gelu * up).astype(bf16)
        act_ref[...] = act
        gelu_ref[...] = gelu.astype(bf16)
        slope_ref[...] = (slope * up).astype(bf16)
        return contract(act, weight(2), 1, 0).astype(bf16)

    units = sum(w.shape[0] for w in weights)
    act, gelu, slope, *parts = ffn_call("ffn_forward", body, rows, [], weights, [units] * 3, (0, 1, 2))
    return act, gelu, slope, parts


def ffn_backward(rows, gelu, slope, weights):
    units = sum(w.shape[0] for w in weights)

    def body(x, stream_refs, weight, out_refs):
        gelu_ref, slope_ref = stream_refs
        d_act = contract(x, weight(2), 1, 1)
        d_gate = (d_act * slope_ref[...].astype(f32)).astype(bf16)
        d_up = (d_act * gelu_ref[...].astype(f32)).astype(bf16)
        out_refs[0][:, :units] = d_gate
        out_refs[0][:, units:] = d_up
        return (contract(d_gate, weight(0), 1, 0) + contract(d_up, weight(1), 1, 0)).astype(bf16)

    d_both, *parts = ffn_call(
        "ffn_backward", body, rows, [gelu, slope], weights, [2 * units], (2, 0, 1)
    )
    return d_both, parts


def unit_grads(units, part, blocks, per, rows):
    count = len(rows)
    tokens, both = units.shape[0], blocks * per

    def body(unit_ref, *refs):
        row_refs, out_refs, (held, sems) = refs[:count], refs[count : count + blocks], refs[-2:]
        copies = gather_rows(row_refs, held, sems)
        for copy in copies:
            copy.start()
        for copy in copies:
            copy.wait()
        total = contract(unit_ref[...], held[...], 0, 0).astype(bf16)
        for i, ref in enumerate(out_refs):
            ref[...] = total[i * per : (i + 1) * per]

    return pl.pallas_call(
        body,
        grid=(1,),
        in_specs=[pl.BlockSpec((tokens, both), lambda i: (0, part))]
        + [pl.BlockSpec(memory_space=pl.ANY)] * count,
        out_specs=[pl.BlockSpec((per, D), lambda i: (0, 0))] * blocks,
        out_shape=[jax.ShapeDtypeStruct((per, D), bf16)] * blocks,
        scratch_shapes=[pltpu.VMEM((tokens, D), bf16), pltpu.SemaphoreType.DMA((count,))],
        compiler_params=pltpu.CompilerParams(vmem_limit_bytes=40 * 1024 * 1024),
        cost_estimate=pl.CostEstimate(
            flops=2 * tokens * both * D, bytes_accessed=0, transcendentals=0
        ),
        name="unit_grads",
    )(units, *rows)


def after_ffn(out_parts, middle, cotangent, g_fpost):
    terms = len(out_parts)

    def body(*refs):
        mid_ref, cot_ref, g_ref, mixed_ref, d_ref, dg_ref = refs[terms:]
        total = refs[0][...].astype(f32)
        for ref in refs[1:terms]:
            total = total + ref[...].astype(f32)
        unit, scale = normed(total)
        mixed_ref[...] = (mid_ref[...] + unit * g_ref[...]).astype(bf16)
        upstream = cot_ref[...].astype(f32)
        dg_ref[...] = jnp.sum(upstream * unit, axis=0, keepdims=True)
        d_ref[...] = norm_back(unit, scale, upstream * g_ref[...]).astype(bf16)

    shape = out_parts[0].shape
    return run(
        "after_ffn",
        body,
        [*out_parts, middle, cotangent, g_fpost],
        "v" * (terms + 3),
        [(shape, bf16), (shape, bf16), ((1, D), f32)],
    )


def query_side(flat, d_query, raw, cosine, sine, g_q, a, w_qkv, heads, d_attn_out):
    tok = a.shape[0]
    wide = H * HD

    def body(
        dq_ref, raw_ref, cos_ref, sin_ref, g_ref, a_ref, w_ref, o_ref, dout_ref,
        lines, da_ref, dg_ref, low, grad, grad_o,
    ):
        cos, sin = cos_ref[...], sin_ref[...]
        dg = jnp.zeros((1, HD), f32)
        for h in range(H):
            cols = slice(h * HD, (h + 1) * HD)
            unit, scale = normed(raw_ref[:, cols])
            turned = rotate(dq_ref[:, cols], cos, -sin)
            dg = dg + jnp.sum(turned * unit, axis=0, keepdims=True)
            low[:, cols] = norm_back(unit, scale, turned * g_ref[...]).astype(bf16)
        dg_ref[...] = dg
        da_ref[...] = contract(low[...], w_ref[:, :wide], 1, 1)
        grad[...] = contract(a_ref[...], low[...], 0, 0)
        for j in range(wide // LANES):
            lines[pl.ds(j, D, stride=flat.q_across), :] = grad[:, j * LANES : (j + 1) * LANES]
        grad_o[...] = contract(o_ref[...], dout_ref[...], 0, 0)
        for j in range(flat.o_across):
            lines[pl.ds(flat.q_lines + j, wide, stride=flat.o_across), :] = grad_o[
                :, j * LANES : (j + 1) * LANES
            ]
        lines[flat.q_lines + flat.o_lines :, :] = jnp.zeros((16, LANES), f32)

    return run(
        "query_side",
        body,
        [d_query, raw, cosine, sine, g_q, a, w_qkv, heads, d_attn_out],
        "v" * 9,
        [((flat.q_lines + flat.o_lines + 16, LANES), f32), ((tok, D), f32), ((1, HD), f32)],
        [pltpu.VMEM((tok, wide), bf16), pltpu.VMEM((D, wide), f32), pltpu.VMEM((wide, D), f32)],
    )


def last_part(
    flat, order, groups, lines, kv_parts, raw, cosine, sine, g_k, a, w_qkv, tokens, g_pre, d_middle,
    da_query, gain_grads,
):
    tok = a.shape[0]
    terms = len(kv_parts)
    wide = H * HD
    each = flat.devices // groups

    def body(order_ref, lines_ref, *refs):
        kv_refs = refs[:terms]
        (
            raw_ref, cos_ref, sin_ref, gk_ref, a_ref, w_ref, tok_ref, gpre_ref, dmid_ref, da_ref,
            dgq, dgpost, dgfpre, dgfpost, in_ref, *outs, held, grad, gains, blocks, sems,
        ) = refs[terms:]
        q_copy = pltpu.make_async_copy(
            lines_ref.at[: flat.q_lines], held.at[: flat.q_lines], sems.at[0]
        )
        o_copy = pltpu.make_async_copy(
            lines_ref.at[flat.q_lines :], held.at[flat.q_lines :], sems.at[1]
        )
        q_copy.start()
        o_copy.start()
        d_kv = kv_refs[0][...].astype(f32)
        for ref in kv_refs[1:]:
            d_kv = d_kv + ref[...].astype(f32)
        unit, scale = normed(raw_ref[:, wide:])
        turned = rotate(d_kv[:, :HD], cos_ref[...], -sin_ref[...])
        dgk = jnp.sum(turned * unit, axis=0, keepdims=True)
        low = jnp.concatenate(
            [norm_back(unit, scale, turned * gk_ref[...]).astype(bf16), d_kv[:, HD:].astype(bf16)],
            axis=1,
        )
        grad[...] = contract(a_ref[...], low, 0, 0)
        d_a = da_ref[...] + contract(low, w_ref[:, wide:], 1, 1)
        unit, scale = normed(tok_ref[...].astype(f32))
        dgpre = jnp.sum(d_a * unit, axis=0, keepdims=True)
        in_ref[...] = (dmid_ref[...] + norm_back(unit, scale, d_a * gpre_ref[...])).astype(bf16)
        gains[...] = jnp.zeros_like(gains)
        at = 0
        for value in (dgpre, dgq[...], dgk, dgpost[...], dgfpre[...], dgfpost[...]):
            for i in range(value.shape[1] // LANES):
                gains[at : at + 1, :] = value[:, i * LANES : (i + 1) * LANES]
                at += 1
        q_copy.wait()
        for j in range(2 * HD // LANES):
            held[pl.ds(wide // LANES + j, D, stride=flat.q_across), :] = grad[
                :, j * LANES : (j + 1) * LANES
            ]
        o_copy.wait()
        for i in range(flat.devices):
            at = i * flat.lines
            blocks[i, : flat.gain_at, :] = held[at : at + flat.gain_at, :].astype(bf16)
            at = flat.gain_line(i)
            blocks[i, flat.gain_at :, :] = gains[at : at + 16, :].astype(bf16)
        copies = [
            pltpu.make_async_copy(
                blocks.at[order_ref[k]], outs[k // each].at[k % each], sems.at[2 + k]
            )
            for k in range(flat.devices)
        ]
        for copy in copies:
            copy.start()
        for copy in copies:
            copy.wait()

    return run(
        "last_part",
        body,
        [order, lines, *kv_parts, raw, cosine, sine, g_k, a, w_qkv, tokens, g_pre, d_middle]
        + [da_query, *gain_grads],
        "sh" + "v" * (terms + 14),
        [((tok, D), bf16)] + [((each, flat.rows, LANES), bf16)] * groups,
        [
            pltpu.VMEM(lines.shape, f32),
            pltpu.VMEM((D, 2 * HD), f32),
            pltpu.VMEM((-(-(flat.gain_lines + 16) // 8) * 8, LANES), f32),
            pltpu.VMEM((flat.devices, flat.rows, LANES), bf16),
            pltpu.SemaphoreType.DMA((2 + flat.devices,)),
        ],
        "v" + "h" * groups,
    )


class Ways:
    def __init__(self, sizes):
        self.sizes = sizes
        self.what = ""

    def size(self, axis):
        if isinstance(axis, str):
            return self.sizes[axis]
        n = 1
        for a in axis:
            n *= self.sizes[a]
        return n

    def fro(self, value, axis, offset):
        n = self.size(axis)
        if offset % n == 0:
            return value
        with jax.named_scope(self.what + "_" + "".join(axis) + str(offset)):
            return lax.ppermute(value, axis, [((i + offset) % n, i) for i in range(n)])

    def places(self):
        nx, ny = self.sizes["x"], self.sizes["y"]
        return [(ox, oy) for ox in range(nx) for oy in range(ny)]

    def outers(self):
        return [(ou, ov) for ou in range(self.sizes["u"]) for ov in range(self.sizes["v"])]

    def plane_gather(self, value, beside=(None, None)):
        early, late = beside
        nx, ny = self.sizes["x"], self.sizes["y"]
        half = halfway(value.shape[0])
        found = {(0, 0): value}
        for ox in range(1, nx):
            found[ox, 0] = self.fro(value, "x", ox)
        for oy in range(1, ny):
            found[0, oy] = self.fro(value, "y", oy)
        if early is not None:
            found, early = lax.optimization_barrier((found, early))
        halves = {}
        for ox in range(1, nx):
            for oy in range(1, ny):
                first = self.fro(found[ox, 0][:half], "y", oy)
                second = self.fro(found[0, oy][half:], "x", ox)
                halves[ox, oy] = [first, second]
        if late is not None:
            halves, late = lax.optimization_barrier((halves, late))
        found.update({at: jnp.concatenate(v, axis=0) for at, v in halves.items()})
        found = {at: [block, self.fro(block, "c", 1)] for at, block in found.items()}
        return found, (early, late)

    def plane_scatter(self, parts, first=None, second=None):
        nx, ny = self.sizes["x"], self.sizes["y"]
        low = {
            at: add_low(parts[at][0], self.fro(parts[at][1], "c", 1))
            for at in sorted(parts, reverse=True)
        }
        what = self.what
        if first is not None:
            last = max(low)
            low[last] = first(low[last])
            self.what = what
        half = halfway(low[0, 0].shape[0])
        along_x = {ox: [low[ox, 0][:half]] for ox in range(1, nx)}
        along_y = {oy: [low[0, oy][half:]] for oy in range(1, ny)}
        for ox in range(1, nx):
            for oy in range(1, ny):
                along_x[ox].append(self.fro(low[ox, oy][:half], "y", -oy))
                along_y[oy].append(self.fro(low[ox, oy][half:], "x", -ox))
        by_x = {
            ox: jnp.concatenate([add_low(*v), low[ox, 0][half:]], axis=0) for ox, v in along_x.items()
        }
        by_y = {
            oy: jnp.concatenate([low[0, oy][:half], add_low(*v)], axis=0) for oy, v in along_y.items()
        }
        if second is not None:
            by_x, by_y = second((by_x, by_y))
            self.what = what
        terms = [low[0, 0]]
        terms += [self.fro(v, "x", -ox) for ox, v in by_x.items()]
        terms += [self.fro(v, "y", -oy) for oy, v in by_y.items()]
        return terms

    def z_begin(self, value):
        n = self.sizes["z"]
        if n != 4:
            return ()
        return self.fro(value, "z", 1), self.fro(value, "z", -1)

    def z_end(self, value, begun, halves=None):
        n = self.sizes["z"]
        if n != 4:
            return [self.fro(value, "z", oz) for oz in range(n)]
        above, below = begun
        half = halfway(value.shape[0])
        first, second = self.fro(above[:half], "z", 1), self.fro(below[half:], "z", -1)
        return [value, above, jnp.concatenate([first, second], axis=0), below]

    def z_gather(self, value):
        return self.z_end(value, self.z_begin(value))

    def z_pair(self, one, other, begun_one, begun_other):
        if self.sizes["z"] != 4:
            return self.z_end(one, ()), self.z_end(other, ())
        far_one = self.fro(begun_one[0], "z", 1)
        far_other = self.fro(begun_other[1], "z", -1)
        return [one, begun_one[0], far_one, begun_one[1]], [
            other, begun_other[0], far_other, begun_other[1]
        ]

    def z_scatter_begin(self, far):
        if self.sizes["z"] != 4:
            return ()
        half = halfway(far.shape[0])
        return self.fro(far[:half], "z", -1), self.fro(far[half:], "z", 1)

    def z_scatter_go(self, parts, begun):
        n = self.sizes["z"]
        if n != 4:
            return [self.fro(parts[oz], "z", -oz) for oz in range(1, n)]
        half = halfway(parts[0].shape[0])
        above = jnp.concatenate([add_low(parts[1][:half], begun[0]), parts[1][half:]], axis=0)
        below = jnp.concatenate([parts[3][:half], add_low(parts[3][half:], begun[1])], axis=0)
        return [self.fro(above, "z", -1), self.fro(below, "z", 1)]

    def z_scatter(self, parts):
        return [parts[0], *self.z_scatter_go(parts, self.z_scatter_begin(parts[len(parts) // 2]))]


SEQ = ("u", "y", "c")
CTX = ("z", "v", "x")
ACROSS = ("v", "x")


def make_shards(sizes):
    ways = Ways(sizes)
    ns, nctx, nx = ways.size(SEQ), ways.size(CTX), ways.size(ACROSS)
    nz, nc = sizes["z"], sizes["c"]
    devices = ns * nctx
    places, outers = ways.places(), ways.outers()

    def from_outers(value):
        if len(outers) == 1:
            return value
        return jnp.concatenate(
            [ways.fro(ways.fro(value, "u", ou), "v", ov) for ou, ov in outers], axis=0
        )

    def to_outers(value):
        if len(outers) == 1:
            return value
        rows = value.shape[0] // len(outers)
        return add_low(
            *[
                ways.fro(ways.fro(value[i * rows : (i + 1) * rows], "u", -ou), "v", -ov)
                for i, (ou, ov) in enumerate(outers)
            ]
        )

    def plane_rows(value, *beside):
        found, beside = ways.plane_gather(value, beside or (None, None))
        return [block for p in places for block in found[p]], beside

    def by_device(parts):
        return {p: parts[i * nc : (i + 1) * nc] for i, p in enumerate(places)}

    def shards(
        tokens, cotangent, segments, positions, attn_w, attn_m, attn_v,
        mlp_w, mlp_m, mlp_v, gains, gain_m, gain_v,
    ):
        at = {a: lax.axis_index(a) for a in sizes}
        seq_place = lax.axis_index(SEQ)
        across_place = lax.axis_index(ACROSS)
        ctx_place = at["z"] * nx + across_place
        device = seq_place * nctx + ctx_place
        piece, gain_piece = attn_w.shape[0], gains.shape[0]
        flat = Flat(piece, gain_piece, devices)

        sides = [sizes[a] for a in ("x", "y", "c", "u", "v", "z")]
        here = [at[a] for a in ("x", "y", "c", "u", "v", "z")]
        ox, oy, oc, ou, ov, oz = (
            (jnp.asarray(o, jnp.int32) + h) % n
            for o, h, n in zip(np.unravel_index(np.arange(devices), sides), here, sides)
        )
        order = ((ou * sizes["y"] + oy) * sizes["c"] + oc) * nz + oz
        order = (order * sizes["v"] + ov) * sizes["x"] + ox

        ways.what = "attn_gather"
        gain_offset = gain_piece * device % LANES
        gain_window = lax.dynamic_update_slice(
            jnp.zeros((16 * LANES,), bf16), gains.astype(bf16), (gain_offset,)
        )
        low_piece = jnp.concatenate(
            [
                jnp.pad(
                    attn_w.astype(bf16).reshape(flat.lines, LANES),
                    ((0, flat.gain_at - flat.lines), (0, 0)),
                ),
                gain_window.reshape(16, LANES),
            ],
            axis=0,
        )
        ways.what = "unit_exchange"
        units, width = mlp_w.shape
        share = units // ns
        held = -(-share // 32) * 32

        def seq_send(by_place):
            return [ways.fro(v, SEQ, offset) for offset, v in enumerate(seq_parts(by_place))]

        def seq_parts(by_place):
            return [
                lax.dynamic_index_in_dim(by_place, (seq_place - offset) % ns, 0, keepdims=False)
                for offset in range(ns)
            ]

        def seq_place_all(heard):
            kept = jnp.zeros((ns,) + heard[0].shape, heard[0].dtype)
            for offset, value in enumerate(heard):
                kept = lax.dynamic_update_index_in_dim(kept, value, (seq_place + offset) % ns, 0)
            return kept

        sent = seq_parts(mlp_w.astype(bf16).reshape(ns, share, width))
        sent, low_piece = lax.optimization_barrier((sent, low_piece))
        heard = [ways.fro(v, SEQ, offset) for offset, v in enumerate(sent)]
        ways.what = "attn_gather"
        line_blocks = ways.z_gather(low_piece)
        line_blocks, heard = lax.optimization_barrier((line_blocks, heard))
        by_cols = seq_place_all(heard)
        rows_own = jnp.concatenate([by_cols[i] for i in range(ns)], axis=1)
        rows_own = jnp.pad(rows_own, ((0, held - share), (0, 0)))
        ways.what = "attn_gather"
        line_z, rows_own = lax.optimization_barrier(
            (from_outers(jnp.concatenate(line_blocks, axis=0)), rows_own)
        )
        def next_units(ring, *beside):
            if beside:
                ring[-1], *beside = lax.optimization_barrier((ring[-1],) + beside)
            what, ways.what = ways.what, "unit_gather"
            ring.append(ways.fro(ring[-1], "z", 1))
            ways.what = what
            return beside[0] if len(beside) == 1 else beside

        steps = nz == 4
        cut = halfway(held)
        whole = [rows_own]
        next_units(whole)
        gathered, _ = ways.plane_gather(line_z)
        line_parts = [part.reshape(-1, flat.rows, LANES) for p in places for part in gathered[p]]
        line_parts, whole[-1] = lax.optimization_barrier((line_parts, whole[-1]))
        rings = [[v[:cut] for v in whole], [v[cut:] for v in whole]]
        if steps:
            next_units(rings[0])
        else:
            for ring in rings:
                for _ in range(2, nz):
                    next_units(ring)

        tok_rows = tokens.shape[1]
        cosine, sine = angles(positions[0])
        (
            w_qkv, g_pre, g_q, g_k, g_post, g_fpre, g_fpost, normed_in, query, kv_local, raw,
        ) = first_part(flat, line_parts, order, tokens[0], cosine, sine)
        w_out = spread_out(flat, [after(part, kv_local) for part in line_parts], order)
        ways.what = "kv_gather"
        if steps:
            half = halfway(tok_rows)
            above, below = ways.z_begin(kv_local)
            above, below, rings[0][-1] = next_units(rings[1], above, below, rings[0][-1])
            far = ways.fro(above[:half], "z", 1), ways.fro(below[half:], "z", -1)
            far = next_units(rings[0], *far)
            kv_blocks = [kv_local, above, jnp.concatenate(far, axis=0), below]
        else:
            kv_blocks = ways.z_gather(kv_local)
        kv_all = jnp.stack([ways.fro(block, ACROSS, oa) for block in kv_blocks for oa in range(nx)])

        doc_all = segments[0]
        first_docs, last_docs = doc_all[::tok_rows], doc_all[tok_rows - 1 :: tok_rows]
        key_at = np.arange(nctx)
        key_place = (at["z"] + jnp.asarray(key_at // nx, jnp.int32)) % nz * nx
        key_place = key_place + (across_place + jnp.asarray(key_at % nx, jnp.int32)) % nx
        is_place = key_place[:, None] == jnp.arange(nctx, dtype=jnp.int32)[None, :]
        key_first = jnp.sum(jnp.where(is_place, first_docs[None, :], 0), axis=1)
        key_last = jnp.sum(jnp.where(is_place, last_docs[None, :], 0), axis=1)
        live = (key_place < ctx_place) & (key_last >= key_first[0])
        one_doc = key_first == key_last[0]
        task = jnp.where(live, jnp.where(one_doc, WHOLE, MASKED), DEAD)
        task = jnp.where(key_place == ctx_place, MASKED, task)
        info = jnp.stack([key_place, task]).astype(jnp.int32)
        key_docs = doc_all[:, None]
        query_docs = lax.dynamic_slice_in_dim(doc_all, ctx_place * tok_rows, tok_rows)[None]

        heads, log_total, attn_out, middle, ffn_in = attend(
            info, query, kv_all, key_docs, query_docs, w_out, tokens[0], g_post, g_fpre
        )

        ways.what = "ffn_in_gather"
        if steps:
            ffn_in = next_units(rings[1], ffn_in)
            ffn_rows, (rings[0][-1], rings[1][-1]) = plane_rows(ffn_in, rings[0][-1], rings[1][-1])
        else:
            ffn_rows, _ = plane_rows(ffn_in)
        units_here = [from_outers(block) for block in whole[:nz]]
        units_here += [from_outers(block) for pair in zip(rings[0][2:], rings[1][2:]) for block in pair]
        act, gelu, slope, parts = ffn_forward(ffn_rows, units_here)
        ways.what = "ffn_out_sum"
        out_parts = ways.plane_scatter(by_device(parts))
        mixed, d_mlp_out, d_gfpost = after_ffn(out_parts, middle, cotangent[0], g_fpost)

        ways.what = "d_out_gather"
        d_out_rows, _ = plane_rows(d_mlp_out)
        per = units_here[0].shape[0]

        def z_step(blocks, far, *earlier):
            value = blocks[far] if not earlier else add_low(blocks[far], *earlier)
            return ways.fro(value, "z", -1)

        class Ring:
            def __init__(self, name, blocks):
                self.name, self.blocks, self.at, self.heard = name, [to_outers(b) for b in blocks], nz, None

            def step(self, beside=None):
                if not steps:
                    return beside
                if self.heard is not None and beside is not None:
                    self.heard, beside = lax.optimization_barrier((self.heard, beside))
                self.at -= 1
                if self.at > 0:
                    value = self.blocks[self.at]
                    if self.heard is not None:
                        value = add_low(value, self.heard)
                    what, ways.what = ways.what, self.name
                    self.heard = ways.fro(value, "z", -1)
                    ways.what = what
                return beside

            def settle(self, beside):
                if steps:
                    self.heard, beside = lax.optimization_barrier((self.heard, beside))
                return beside

            def result(self):
                if steps:
                    return add_low(self.blocks[0], self.heard)
                return add_low(*[ways.fro(v, "z", -i) for i, v in enumerate(self.blocks)])

        down = Ring("down_grad_sum", unit_grads(act, 0, nz, per, d_out_rows))
        down.step()
        d_out_rows[0] = after(d_out_rows[0], down.blocks[0])
        d_both, parts = ffn_backward(d_out_rows, gelu, slope, units_here)
        parts[-1] = down.step(parts[-1])
        rings = {}

        def gate_then(low):
            low, both = lax.optimization_barrier((low, d_both))
            rings["gate"] = Ring("gate_grad_sum", unit_grads(both, 0, nz, per, ffn_rows))
            rings["gate"].step()
            return low

        def up_then(summed):
            summed = down.step(summed)
            summed, both = lax.optimization_barrier((summed, d_both))
            rings["up"] = Ring("up_grad_sum", unit_grads(both, 1, nz, per, ffn_rows))
            rings["up"].step()
            return summed

        ways.what = "d_in_sum"
        d_in_parts = ways.plane_scatter(by_device(parts), gate_then, up_then)
        d_in_parts = lax.optimization_barrier((d_in_parts, rings["up"].blocks[0]))[0]
        d_in_parts = rings["gate"].step(d_in_parts)

        d_query, d_attn_out, d_middle, d_gfpre, d_gpost, *d_kv = attend_back(
            info, query, kv_all, key_docs, query_docs, heads, log_total, d_in_parts, middle, attn_out,
            cotangent[0], w_out, g_post, g_fpre,
        )
        d_kv = down.step(rings["up"].settle(d_kv))
        ways.what = "kv_sum"

        def across(oz):
            return [ways.fro(d_kv[oz * nx + oa], ACROSS, -oa) for oa in range(nx)]

        far = nz // 2
        kv_parts = {far: add_low(*across(far))}
        near = {oz: across(oz) for oz in range(nz) if oz != far}
        begun = ways.z_scatter_begin(kv_parts[far])
        near, begun = lax.optimization_barrier((near, begun))
        kv_parts.update({oz: add_low(*terms) for oz, terms in near.items()})
        kv_parts = [kv_parts[0], *ways.z_scatter_go(kv_parts, begun)]
        lines, da_query, d_gq = query_side(
            flat, after(d_query, *near[0]), raw, cosine, sine, g_q, normed_in, w_qkv, heads, d_attn_out
        )
        da_query = rings["up"].step(rings["gate"].step(da_query))
        input_grad, *packed = last_part(
            flat, order, len(places) * nc, lines, kv_parts, raw, cosine, sine, g_k, normed_in, w_qkv, tokens[0],
            g_pre, d_middle, da_query, [d_gq, d_gpost, d_gfpre, d_gfpost],
        )

        ways.what = "attn_grad_sum"
        packed = [part.reshape(-1, LANES) for part in packed]
        terms = ways.plane_scatter(
            {p: packed[i * nc : (i + 1) * nc] for i, p in enumerate(places)}, rings["up"].step
        )
        owned = [rings["gate"].result(), rings["up"].result(), down.result()]
        own_rows = jnp.concatenate([v[:share] for v in owned], axis=1)
        by_cols = jnp.stack([own_rows[:, i * width : (i + 1) * width] for i in range(ns)])
        terms, by_cols = lax.optimization_barrier((terms, by_cols))
        plane_sum = to_outers(add_low(*terms))

        ways.what = "grad_exchange"
        mlp_red = seq_place_all(seq_send(by_cols)).astype(f32).reshape(units, width)
        mlp_m_new, mlp_v_new, mlp_new = adam_update(
            mlp_w, mlp_m, mlp_v, mlp_red, RATE_MATRIX, DECAY_MATRIX
        )

        ways.what = "attn_grad_sum"
        terms = ways.z_scatter([plane_sum[oz * flat.rows : (oz + 1) * flat.rows] for oz in range(nz)])
        terms, mlp_new = lax.optimization_barrier((terms, mlp_new))
        red = sum(part.astype(f32) for part in terms)
        attn_red = red[: flat.lines].reshape(-1)
        gain_red = lax.dynamic_slice(red[flat.gain_at :].reshape(-1), (gain_offset,), (gain_piece,))

        attn_m_new, attn_v_new, attn_new = adam_update(
            attn_w, attn_m, attn_v, attn_red, RATE_MATRIX, DECAY_MATRIX
        )
        gain_m_new, gain_v_new, gain_new = adam_update(
            gains, gain_m, gain_v, gain_red, RATE_GAIN, 0.0
        )
        return (
            mixed[None], input_grad[None],
            attn_red, attn_m_new, attn_v_new, attn_new,
            mlp_red, mlp_m_new, mlp_v_new, mlp_new,
            gain_red, gain_m_new, gain_v_new, gain_new,
        )

    return shards


def solution(mesh):
    seq, ctx = mesh.shape["seq"], mesh.shape["ctx"]
    nz = 4 if ctx % 4 == 0 else 1
    chips_y, chips_x = seq // 2, ctx // nz
    y, x = 2 - chips_y % 2, 2 - chips_x % 2
    sizes = {"u": chips_y // y, "y": y, "c": 2, "z": nz, "v": chips_x // x, "x": x}
    fine = Mesh(mesh.devices.reshape(*sizes.values()), tuple(sizes))
    s, x = SEQ, CTX
    both = s + x
    in_specs = (
        P(s, x, None), P(s, x, None), P(s, None), P(s, x),
        P(both), P(both), P(both),
        P(x, s), P(x, s), P(x, s),
        P(both), P(both), P(both),
    )
    out_specs = (
        P(s, x, None), P(s, x, None),
        P(both), P(both), P(both), P(both),
        P(x, s), P(x, s), P(x, s), P(x, s),
        P(both), P(both), P(both), P(both),
    )
    return jax.shard_map(
        make_shards(sizes), mesh=fine, in_specs=in_specs, out_specs=out_specs, check_vma=False
    )
```

```python
import jax
import jax.numpy as jnp
import numpy as np
from jax import lax
from jax.experimental import pallas as pl
from jax.experimental.pallas import tpu as pltpu
from jax.sharding import Mesh, PartitionSpec as P

D = 1152
H = 4
HD = 256
STEP = 5

NORM_EPS = 1e-06
SCORE_FLOOR = -1e30
ROPE_BASE = 1000000.0
BETA_MOMENT = 0.5
ADAM_EPS = 1e-08
RATE_MATRIX = 0.03
RATE_GAIN = 0.5
DECAY_MATRIX = 0.1

bf16 = jnp.bfloat16
f32 = jnp.float32
LANES = 128


def normed(value):
    factor = lax.rsqrt(jnp.mean(value * value, axis=-1, keepdims=True) + NORM_EPS)
    return (value * factor, factor)


def norm_back(unit, factor, d_unit):
    return factor * (d_unit - unit * jnp.mean(d_unit * unit, axis=-1, keepdims=True))


def angles(position):
    half_index = jnp.arange(HD // 2, dtype=f32)
    frequency = jnp.exp(half_index * (-2.0 * jnp.log(ROPE_BASE) / HD))
    angle = position.astype(f32)[:, None] * frequency[None, :]
    return (jnp.cos(angle), jnp.sin(angle))


def rotate(value, cosine, sine):
    half_width = value.shape[-1] // 2
    first_half = value[..., :half_width]
    second_half = value[..., half_width:]
    return jnp.concatenate(
        [first_half * cosine - second_half * sine, second_half * cosine + first_half * sine],
        axis=-1,
    )


def contract(left, right, left_dim, right_dim):
    return lax.dot_general(
        left, right, (((left_dim,), (right_dim,)), ((), ())), preferred_element_type=f32
    )


def adam_update(weight, moment_one, second, gradient, learn_rate, decay_rate):
    moment_new = BETA_MOMENT * moment_one + (1.0 - BETA_MOMENT) * gradient
    second_new = BETA_MOMENT * second + (1.0 - BETA_MOMENT) * gradient * gradient
    correction = 1.0 - BETA_MOMENT**STEP
    update = moment_new / correction / (jnp.sqrt(second_new / correction) + ADAM_EPS)
    return (moment_new, second_new, weight - learn_rate * (update + decay_rate * weight))


def add_low(*parts):
    total = parts[0].astype(f32)
    for part in parts[1:]:
        total = total + part.astype(f32)
    return total.astype(bf16)


def after(value, *earlier):
    return lax.optimization_barrier((value,) + earlier)[0]


def halfway(rows):
    return rows // 32 * 16 if rows >= 32 else rows // 2


VMEM_LIMIT = 56 * 1024 * 1024
VMEM_LIMITS = {"after_ffn": 40 * 1024 * 1024}
SCORE_SCALE = HD ** (-0.5)
SPACES = {"v": pltpu.VMEM, "h": pl.ANY, "s": pltpu.SMEM}


def run(name, body, operands, spaces, out_shape, scratch=(), out_spaces=None, flops=0):
    return pl.pallas_call(
        body,
        out_shape=tuple(jax.ShapeDtypeStruct(s, d) for s, d in out_shape),
        in_specs=[pl.BlockSpec(memory_space=SPACES[s]) for s in spaces],
        out_specs=tuple(
            pl.BlockSpec(memory_space=SPACES[s]) for s in out_spaces or "v" * len(out_shape)
        ),
        scratch_shapes=list(scratch),
        compiler_params=pltpu.CompilerParams(vmem_limit_bytes=VMEM_LIMITS.get(name, VMEM_LIMIT)),
        cost_estimate=pl.CostEstimate(flops=flops, bytes_accessed=0, transcendentals=0),
        name=name,
    )(*operands)


class Flat:
    def __init__(self, piece, gain_piece, devices):
        self.devices = devices
        self.lines = piece // LANES
        self.gain_at = -(-self.lines // 16) * 16
        self.gain_piece = gain_piece
        self.rows = self.gain_at + 16
        self.q_across, self.o_across = (H + 2) * HD // LANES, D // LANES
        self.q_lines, self.o_lines = D * self.q_across, H * HD * self.o_across
        widths = [D, HD, HD, D, D, D]
        self.gain_rows = [w // LANES for w in widths]
        self.gain_lines = sum(self.gain_rows)

        across, kv = self.q_across, 2 * HD // LANES
        self.kv_across = kv
        self.late_rows = self.lines // across + (2 if self.lines % across else 0)
        self.late_lines = -(-self.late_rows * kv // 16) * 16

    def first_row(self, device):
        return self.lines * device // self.q_across

    def gain_line(self, device):
        return self.gain_piece * device // LANES


def fetch(order_ref, sources, held, sems):
    copies = []
    for source in sources:
        for i in range(source.shape[0]):
            k = len(copies)
            copies.append(pltpu.make_async_copy(source.at[i], held.at[order_ref[k]], sems.at[k]))
    for copy in copies:
        copy.start()
    return copies


def first_part(flat, parts, order, tokens, cosine, sine):
    tok_rows = tokens.shape[0]
    wide = (H + 2) * HD
    blocks = -(-flat.q_lines // flat.lines)

    def body(order_ref, *refs):
        sources = refs[: len(parts)]
        (
            tok_ref, cos_ref, sin_ref, w_ref, g_pre, g_q, g_k, g_post, g_fpre, g_fpost,
            a_ref, q_ref, kv_ref, raw_ref, held, lines, gains, sems,
        ) = refs[len(parts) :]
        copies = fetch(order_ref, sources, held, sems)
        unit, _ = normed(tok_ref[...].astype(f32))
        gains[...] = jnp.zeros_like(gains)
        for copy in copies:
            copy.wait()
        for i in range(flat.devices):
            at = flat.gain_line(i)
            gains[at : at + 3, :] += held[i, flat.gain_at :, :].astype(f32)[:3]
        at = 0
        for ref, rows in zip((g_pre, g_q, g_k, g_post, g_fpre, g_fpost), flat.gain_rows):
            for i in range(rows):
                ref[:, i * LANES : (i + 1) * LANES] = gains[at + i : at + i + 1, :]
            at += rows
        a_ref[...] = (unit * g_pre[...]).astype(bf16)
        for i in range(blocks):
            lines[i * flat.lines : (i + 1) * flat.lines, :] = held[i, : flat.gain_at, :].astype(f32)[
                : flat.lines
            ]
        for j in range(flat.q_across):
            w_ref[:, j * LANES : (j + 1) * LANES] = lines[
                pl.ds(j, D, stride=flat.q_across), :
            ].astype(bf16)
        qkv = contract(a_ref[...], w_ref[...], 1, 0)
        raw_ref[...] = qkv[:, : (H + 1) * HD]
        cos, sin = cos_ref[...], sin_ref[...]
        for h in range(H):
            head = normed(qkv[:, h * HD : (h + 1) * HD])[0] * g_q[...]
            low = rotate(head, cos, sin).astype(bf16)
            q_ref[:, h * HD : (h + 1) * HD] = (low.astype(f32) * SCORE_SCALE).astype(bf16)
        key = normed(qkv[:, H * HD : (H + 1) * HD])[0] * g_k[...]
        kv_ref[:, :HD] = rotate(key, cos, sin).astype(bf16)
        kv_ref[:, HD:] = qkv[:, (H + 1) * HD :].astype(bf16)

    row = [((1, w * LANES), f32) for w in flat.gain_rows]
    return run(
        "first_part",
        body,
        [order, *parts, tokens, cosine, sine],
        "s" + "h" * len(parts) + "vvv",
        [((D, wide), bf16), *row]
        + [((tok_rows, D), bf16), ((tok_rows, H * HD), bf16), ((tok_rows, 2 * HD), bf16)]
        + [((tok_rows, (H + 1) * HD), f32)],
        [
            pltpu.VMEM((flat.devices, flat.rows, LANES), bf16),
            pltpu.VMEM((blocks * flat.lines + 16, LANES), f32),
            pltpu.VMEM((-(-(flat.gain_lines + 3) // 8) * 8, LANES), f32),
            pltpu.SemaphoreType.DMA((flat.devices,)),
        ],
        flops=8 * 2 * tok_rows * D * wide,
    )


def spread_out(flat, parts, order):
    start = flat.q_lines // flat.lines

    def body(order_ref, *refs):
        sources = refs[: len(parts)]
        w_ref, held, lines, sems = refs[len(parts) :]
        for copy in fetch(order_ref, sources, held, sems):
            copy.wait()
        for i in range(start, flat.devices):
            at = (i - start) * flat.lines
            lines[at : at + flat.lines, :] = held[i, : flat.gain_at, :].astype(f32)[: flat.lines]
        for j in range(flat.o_across):
            w_ref[:, j * LANES : (j + 1) * LANES] = lines[
                pl.ds(flat.q_lines - start * flat.lines + j, H * HD, stride=flat.o_across), :
            ].astype(bf16)

    return run(
        "spread_out",
        body,
        [order, *parts],
        "s" + "h" * len(parts),
        [((H * HD, D), bf16)],
        [
            pltpu.VMEM((flat.devices, flat.rows, LANES), bf16),
            pltpu.VMEM(((flat.devices - start) * flat.lines + 16, LANES), f32),
            pltpu.SemaphoreType.DMA((flat.devices,)),
        ],
    )[0]


DEAD, WHOLE, MASKED = 0, 1, 2


def allowed_of(kdoc_ref, qdoc_ref, shift):
    keys, queries = kdoc_ref.shape[0], qdoc_ref.shape[1]
    key_at = lax.broadcasted_iota(jnp.int32, (keys, queries), 0) + shift
    query_at = lax.broadcasted_iota(jnp.int32, (keys, queries), 1)
    return (kdoc_ref[...] == qdoc_ref[...]) & (key_at <= query_at)


def same(shape):
    return pl.BlockSpec(shape, lambda i, info: (0,) * len(shape))


def attend(info, query, kv, key_docs, query_docs, w_out, tokens, g_post, g_fpre):
    blocks, rows, _ = kv.shape

    def body(
        info_ref, q_ref, kv_ref, kdoc_ref, qdoc_ref, w_ref, tok_ref, g_post_ref, g_fpre_ref,
        o_ref, lse_ref, out_ref, mid_ref, in_ref, peak, total, acc,
    ):
        step = pl.program_id(0)

        @pl.when(step == 0)
        def _():
            peak[...] = jnp.full_like(peak, SCORE_FLOOR)
            total[...] = jnp.zeros_like(total)
            acc[...] = jnp.zeros_like(acc)

        def visit(masked):
            key = kv_ref[0, :, :HD]
            value_t = kv_ref[0, :, HD:].T
            if masked:
                allowed = allowed_of(
                    kdoc_ref, qdoc_ref, (info_ref[0, step] - info_ref[0, 0]) * rows
                )
            for h in range(H):
                score = contract(key, q_ref[:, h * HD : (h + 1) * HD], 1, 1)
                if masked:
                    score = jnp.where(allowed, score, SCORE_FLOOR)
                old = peak[h : h + 1, :]
                new = jnp.maximum(old, jnp.max(score, axis=0, keepdims=True))
                weight = jnp.exp(score - new)
                shrink = jnp.exp(old - new)
                peak[h : h + 1, :] = new
                total[h : h + 1, :] = total[h : h + 1, :] * shrink + jnp.sum(
                    weight, axis=0, keepdims=True
                )
                acc[h] = acc[h] * shrink + contract(value_t, weight.astype(bf16), 1, 0)

        pl.when(info_ref[1, step] == WHOLE)(lambda: visit(False))
        pl.when(info_ref[1, step] == MASKED)(lambda: visit(True))

        @pl.when(step == blocks - 1)
        def _():
            lse_ref[...] = jnp.zeros_like(lse_ref)
            for h in range(H):
                lse_ref[h : h + 1, :] = peak[h : h + 1, :] + jnp.log(total[h : h + 1, :])
                o_ref[:, h * HD : (h + 1) * HD] = (acc[h] / total[h : h + 1, :]).T.astype(bf16)
            attn_out = contract(o_ref[...], w_ref[...], 1, 0)
            out_ref[...] = attn_out
            middle = tok_ref[...].astype(f32) + normed(attn_out)[0] * g_post_ref[...]
            mid_ref[...] = middle
            in_ref[...] = (normed(middle)[0] * g_fpre_ref[...]).astype(bf16)

    return pl.pallas_call(
        body,
        grid_spec=pltpu.PrefetchScalarGridSpec(
            num_scalar_prefetch=1,
            grid=(blocks,),
            in_specs=[
                same((rows, H * HD)),
                pl.BlockSpec((1, rows, 2 * HD), lambda i, info: (i, 0, 0)),
                pl.BlockSpec((rows, 1), lambda i, info: (info[0, i], 0)),
                same((1, rows)),
                same((H * HD, D)),
                same((rows, D)),
                same((1, D)),
                same((1, D)),
            ],
            out_specs=[
                same((rows, H * HD)),
                same((8, rows)),
                same((rows, D)),
                same((rows, D)),
                same((rows, D)),
            ],
            scratch_shapes=[
                pltpu.VMEM((8, rows), f32),
                pltpu.VMEM((8, rows), f32),
                pltpu.VMEM((H, HD, rows), f32),
            ],
        ),
        out_shape=(
            jax.ShapeDtypeStruct((rows, H * HD), bf16),
            jax.ShapeDtypeStruct((8, rows), f32),
            jax.ShapeDtypeStruct((rows, D), f32),
            jax.ShapeDtypeStruct((rows, D), f32),
            jax.ShapeDtypeStruct((rows, D), bf16),
        ),
        compiler_params=pltpu.CompilerParams(vmem_limit_bytes=48 * 1024 * 1024),
        cost_estimate=pl.CostEstimate(
            flops=8 * 4 * blocks * rows * rows * H * HD, bytes_accessed=0, transcendentals=0
        ),
        name="attend",
    )(info, query, kv, key_docs, query_docs, w_out, tokens, g_post, g_fpre)


def attend_back(
    info, query, kv, key_docs, query_docs, heads, log_total, d_in, middle, attn_out, cotangent,
    w_out, g_post, g_fpre,
):
    blocks, rows, _ = kv.shape
    terms = len(d_in)

    def body(info_ref, q_ref, kv_ref, kdoc_ref, qdoc_ref, o_ref, lse_ref, *refs):
        terms_ref = refs[:terms]
        (
            mid_ref, out_ref, cot_ref, w_ref, g_post_ref, g_fpre_ref,
            dq_ref, dout_ref, dmid_ref, dg_fpre_ref, dg_post_ref, *dkv_refs, do_ref, delta_ref,
        ) = refs[terms:]
        step = pl.program_id(0)

        def give(d_key, d_value):
            for k, ref in enumerate(dkv_refs):

                @pl.when(step == k)
                def _(ref=ref):
                    ref[:, :HD] = d_key.astype(bf16)
                    ref[:, HD:] = d_value.astype(bf16)

        @pl.when(step == 0)
        def _():
            d_rows = sum(ref[...].astype(f32) for ref in terms_ref)
            unit, scale = normed(mid_ref[...])
            dg_fpre_ref[...] = jnp.sum(d_rows * unit, axis=0, keepdims=True)
            d_middle = cot_ref[...].astype(f32) + norm_back(unit, scale, d_rows * g_fpre_ref[...])
            dmid_ref[...] = d_middle
            unit, scale = normed(out_ref[...])
            dg_post_ref[...] = jnp.sum(d_middle * unit, axis=0, keepdims=True)
            d_out = norm_back(unit, scale, d_middle * g_post_ref[...]).astype(bf16)
            dout_ref[...] = d_out
            delta_ref[...] = jnp.zeros_like(delta_ref)
            for h in range(H):
                cols = slice(h * HD, (h + 1) * HD)
                d_o = contract(d_out, w_ref[cols, :], 1, 1).astype(bf16)
                do_ref[:, cols] = d_o
                each = (d_o.astype(f32) * o_ref[:, cols].astype(f32)).T
                delta_ref[h : h + 1, :] = jnp.sum(each, axis=0, keepdims=True)
            dq_ref[...] = jnp.zeros_like(dq_ref)

        def visit(masked):
            key, value = kv_ref[0, :, :HD], kv_ref[0, :, HD:]
            if masked:
                allowed = allowed_of(
                    kdoc_ref, qdoc_ref, (info_ref[0, step] - info_ref[0, 0]) * rows
                )
            d_key = jnp.zeros((rows, HD), f32)
            d_value = jnp.zeros((rows, HD), f32)
            for h in range(H):
                cols = slice(h * HD, (h + 1) * HD)
                q, d_o = q_ref[:, cols], do_ref[:, cols]
                prob = jnp.exp(contract(key, q, 1, 1) - lse_ref[h : h + 1, :])
                if masked:
                    prob = jnp.where(allowed, prob, 0.0)
                d_value = d_value + contract(prob.astype(bf16), d_o, 1, 0)
                d_prob = contract(value, d_o, 1, 1)
                d_score = (prob * (d_prob - delta_ref[h : h + 1, :])).astype(bf16)
                d_key = d_key + contract(d_score, q, 1, 0)
                dq_ref[:, cols] = dq_ref[:, cols] + contract(d_score, key, 0, 0)
            give(d_key, d_value)

        pl.when(info_ref[1, step] == WHOLE)(lambda: visit(False))
        pl.when(info_ref[1, step] == MASKED)(lambda: visit(True))

        @pl.when(info_ref[1, step] == DEAD)
        def _():
            give(jnp.zeros((rows, HD), f32), jnp.zeros((rows, HD), f32))

        @pl.when(step == blocks - 1)
        def _():
            dq_ref[...] = dq_ref[...] * SCORE_SCALE

    block = pl.BlockSpec((1, rows, 2 * HD), lambda i, info: (i, 0, 0))
    resident = pl.BlockSpec(memory_space=pltpu.VMEM)
    return pl.pallas_call(
        body,
        grid_spec=pltpu.PrefetchScalarGridSpec(
            num_scalar_prefetch=1,
            grid=(blocks,),
            in_specs=[
                resident,
                block,
                pl.BlockSpec((rows, 1), lambda i, info: (info[0, i], 0)),
                resident,
                resident,
                resident,
                *[resident] * (terms + 3),
                resident,
                resident,
                resident,
            ],
            out_specs=[
                resident,
                resident,
                resident,
                resident,
                resident,
                *[resident] * blocks,
            ],
            scratch_shapes=[pltpu.VMEM((rows, H * HD), bf16), pltpu.VMEM((8, rows), f32)],
        ),
        out_shape=(
            jax.ShapeDtypeStruct((rows, H * HD), f32),
            jax.ShapeDtypeStruct((rows, D), bf16),
            jax.ShapeDtypeStruct((rows, D), f32),
            jax.ShapeDtypeStruct((1, D), f32),
            jax.ShapeDtypeStruct((1, D), f32),
            *[jax.ShapeDtypeStruct((rows, 2 * HD), bf16)] * blocks,
        ),
        compiler_params=pltpu.CompilerParams(vmem_limit_bytes=48 * 1024 * 1024),
        cost_estimate=pl.CostEstimate(flops=0, bytes_accessed=0, transcendentals=0),
        name="attend_back",
    )(
        info, query, kv, key_docs, query_docs, heads, log_total, *d_in, middle, attn_out, cotangent,
        w_out, g_post, g_fpre,
    )


def gelu_parts(gate):
    scale = 0.7978845608028654
    square = gate * gate
    inner = jnp.tanh(scale * gate * (1.0 + 0.044715 * square))
    half_up = 0.5 * (1.0 + inner)
    slope = half_up + 0.5 * gate * (1.0 - inner * inner) * scale * (1.0 + 3 * 0.044715 * square)
    return gate * half_up, slope


def gather_rows(refs, held, sems):
    tok = refs[0].shape[0]
    return [
        pltpu.make_async_copy(ref, held.at[k * tok : (k + 1) * tok], sems.at[k])
        for k, ref in enumerate(refs)
    ]


def scatter_rows(held, refs, sems):
    tok = refs[0].shape[0]
    return [
        pltpu.make_async_copy(held.at[k * tok : (k + 1) * tok], ref, sems.at[k])
        for k, ref in enumerate(refs)
    ]


def by_chunk(step, chunks, copies, do):
    per = len(copies) // chunks
    for k in range(chunks):

        @pl.when(step == k)
        def _(k=k):
            for copy in copies[k * per : (k + 1) * per]:
                do(copy)


def ffn_call(name, body, rows, streams, weights, outs, order):
    count, (tok, wide) = len(rows), rows[0].shape
    chunks = -(-count * tok // 512)
    both = count * tok // chunks
    blocks = len(weights)
    starts = np.cumsum([0] + [w.shape[0] for w in weights]).tolist()
    per = starts[-1]

    def kernel(*refs):
        row_refs, refs = refs[:count], refs[count:]
        stream_refs, refs = refs[: len(streams)], refs[len(streams) :]
        w_refs, refs = refs[:blocks], refs[blocks:]
        out_refs, refs = refs[: len(outs)], refs[len(outs) :]
        sum_refs, (held, given, units, sems_in, sems_out, sems_w) = refs[:count], refs[count:]
        step = pl.program_id(0)
        coming = gather_rows(row_refs, held, sems_in)
        going = scatter_rows(given, sum_refs, sems_out)
        brought = {
            k: [
                pltpu.make_async_copy(
                    ref.at[:, k * D : (k + 1) * D],
                    units.at[k, starts[i] : starts[i + 1]],
                    sems_w.at[k * blocks + i],
                )
                for i, ref in enumerate(w_refs)
            ]
            for k in order
        }

        @pl.when(step == 0)
        def _():
            first = len(coming) // chunks
            bringing = [c for k in order for c in brought[k]]
            for copy in coming[:first] + bringing + coming[first:]:
                copy.start()

        by_chunk(step, chunks, coming, lambda copy: copy.wait())
        here = pl.ds(pl.multiple_of(step * both, both), both)

        def arrived(k):
            for copy in brought[k]:
                copy.wait()
            return units[k]

        @pl.when(step == 0)
        def _():
            given[here, :] = body(held[here, :], stream_refs, arrived, out_refs)

        @pl.when(step > 0)
        def _():
            given[here, :] = body(held[here, :], stream_refs, lambda k: units[k], out_refs)

        by_chunk(step, chunks, going, lambda copy: copy.start())

        @pl.when(step == chunks - 1)
        def _():
            for copy in going:
                copy.wait()

    def chunk(width):
        return pl.BlockSpec((both, width), lambda i: (i, 0))

    anywhere = pl.BlockSpec(memory_space=pl.ANY)
    return pl.pallas_call(
        kernel,
        grid=(chunks,),
        in_specs=[anywhere] * count
        + [chunk(s.shape[1]) for s in streams]
        + [anywhere] * blocks,
        out_specs=tuple([chunk(w) for w in outs] + [anywhere] * count),
        out_shape=tuple(
            [jax.ShapeDtypeStruct((count * tok, w), bf16) for w in outs]
            + [jax.ShapeDtypeStruct((tok, wide), bf16)] * count
        ),
        scratch_shapes=[
            pltpu.VMEM((count * tok, wide), bf16),
            pltpu.VMEM((count * tok, wide), bf16),
            pltpu.VMEM((3, per, D), bf16),
            pltpu.SemaphoreType.DMA((count,)),
            pltpu.SemaphoreType.DMA((count,)),
            pltpu.SemaphoreType.DMA((3 * blocks,)),
        ],
        compiler_params=pltpu.CompilerParams(vmem_limit_bytes={"ffn_forward": 46, "ffn_backward": 46}[name] * 1024 * 1024),
        cost_estimate=pl.CostEstimate(
            flops=6 * count * tok * per * D, bytes_accessed=0, transcendentals=0
        ),
        name=name,
    )(*rows, *streams, *weights)


def ffn_forward(rows, weights):
    def body(x, _, weight, out_refs):
        act_ref, gelu_ref, slope_ref = out_refs
        gate = contract(x, weight(0), 1, 1)
        up = contract(x, weight(1), 1, 1)
        gelu, slope = gelu_parts(gate)
        act = (gelu * up).astype(bf16)
        act_ref[...] = act
        gelu_ref[...] = gelu.astype(bf16)
        slope_ref[...] = (slope * up).astype(bf16)
        return contract(act, weight(2), 1, 0).astype(bf16)

    units = sum(w.shape[0] for w in weights)
    act, gelu, slope, *parts = ffn_call("ffn_forward", body, rows, [], weights, [units] * 3, (0, 1, 2))
    return act, gelu, slope, parts


def ffn_backward(rows, gelu, slope, weights):
    units = sum(w.shape[0] for w in weights)

    def body(x, stream_refs, weight, out_refs):
        gelu_ref, slope_ref = stream_refs
        d_act = contract(x, weight(2), 1, 1)
        d_gate = (d_act * slope_ref[...].astype(f32)).astype(bf16)
        d_up = (d_act * gelu_ref[...].astype(f32)).astype(bf16)
        out_refs[0][:, :units] = d_gate
        out_refs[0][:, units:] = d_up
        return (contract(d_gate, weight(0), 1, 0) + contract(d_up, weight(1), 1, 0)).astype(bf16)

    d_both, *parts = ffn_call(
        "ffn_backward", body, rows, [gelu, slope], weights, [2 * units], (2, 0, 1)
    )
    return d_both, parts


def unit_grads(units, part, blocks, per, rows):
    count = len(rows)
    tokens, both = units.shape[0], blocks * per

    def body(unit_ref, *refs):
        row_refs, out_refs, (held, sems) = refs[:count], refs[count : count + blocks], refs[-2:]
        copies = gather_rows(row_refs, held, sems)
        for copy in copies:
            copy.start()
        for copy in copies:
            copy.wait()
        total = contract(unit_ref[...], held[...], 0, 0).astype(bf16)
        for i, ref in enumerate(out_refs):
            ref[...] = total[i * per : (i + 1) * per]

    return pl.pallas_call(
        body,
        grid=(1,),
        in_specs=[pl.BlockSpec((tokens, both), lambda i: (0, part))]
        + [pl.BlockSpec(memory_space=pl.ANY)] * count,
        out_specs=[pl.BlockSpec((per, D), lambda i: (0, 0))] * blocks,
        out_shape=[jax.ShapeDtypeStruct((per, D), bf16)] * blocks,
        scratch_shapes=[pltpu.VMEM((tokens, D), bf16), pltpu.SemaphoreType.DMA((count,))],
        compiler_params=pltpu.CompilerParams(vmem_limit_bytes=40 * 1024 * 1024),
        cost_estimate=pl.CostEstimate(
            flops=2 * tokens * both * D, bytes_accessed=0, transcendentals=0
        ),
        name="unit_grads",
    )(units, *rows)


def after_ffn(out_parts, middle, cotangent, g_fpost):
    terms = len(out_parts)

    def body(*refs):
        mid_ref, cot_ref, g_ref, mixed_ref, d_ref, dg_ref = refs[terms:]
        total = refs[0][...].astype(f32)
        for ref in refs[1:terms]:
            total = total + ref[...].astype(f32)
        unit, scale = normed(total)
        mixed_ref[...] = (mid_ref[...] + unit * g_ref[...]).astype(bf16)
        upstream = cot_ref[...].astype(f32)
        dg_ref[...] = jnp.sum(upstream * unit, axis=0, keepdims=True)
        d_ref[...] = norm_back(unit, scale, upstream * g_ref[...]).astype(bf16)

    shape = out_parts[0].shape
    return run(
        "after_ffn",
        body,
        [*out_parts, middle, cotangent, g_fpost],
        "v" * (terms + 3),
        [(shape, bf16), (shape, bf16), ((1, D), f32)],
    )


def query_side(flat, d_query, raw, cosine, sine, g_q, a, w_qkv, heads, d_attn_out):
    tok = a.shape[0]
    wide = H * HD

    def body(
        dq_ref, raw_ref, cos_ref, sin_ref, g_ref, a_ref, w_ref, o_ref, dout_ref,
        lines, da_ref, dg_ref, low, grad, grad_o,
    ):
        cos, sin = cos_ref[...], sin_ref[...]
        dg = jnp.zeros((1, HD), f32)
        for h in range(H):
            cols = slice(h * HD, (h + 1) * HD)
            unit, scale = normed(raw_ref[:, cols])
            turned = rotate(dq_ref[:, cols], cos, -sin)
            dg = dg + jnp.sum(turned * unit, axis=0, keepdims=True)
            low[:, cols] = norm_back(unit, scale, turned * g_ref[...]).astype(bf16)
        dg_ref[...] = dg
        da_ref[...] = contract(low[...], w_ref[:, :wide], 1, 1)
        grad[...] = contract(a_ref[...], low[...], 0, 0)
        for j in range(wide // LANES):
            lines[pl.ds(j, D, stride=flat.q_across), :] = grad[:, j * LANES : (j + 1) * LANES]
        grad_o[...] = contract(o_ref[...], dout_ref[...], 0, 0)
        for j in range(flat.o_across):
            lines[pl.ds(flat.q_lines + j, wide, stride=flat.o_across), :] = grad_o[
                :, j * LANES : (j + 1) * LANES
            ]
        lines[flat.q_lines + flat.o_lines :, :] = jnp.zeros((16, LANES), f32)

    return run(
        "query_side",
        body,
        [d_query, raw, cosine, sine, g_q, a, w_qkv, heads, d_attn_out],
        "v" * 9,
        [((flat.q_lines + flat.o_lines + 16, LANES), f32), ((tok, D), f32), ((1, HD), f32)],
        [pltpu.VMEM((tok, wide), bf16), pltpu.VMEM((D, wide), f32), pltpu.VMEM((wide, D), f32)],
    )


def last_part(
    flat, order, groups, lines, kv_parts, raw, cosine, sine, g_k, a, w_qkv, tokens, g_pre, d_middle,
    da_query, gain_grads,
):
    tok = a.shape[0]
    terms = len(kv_parts)
    wide = H * HD
    each = flat.devices // groups

    straight = flat.lines % 16 == 0

    def body(order_ref, lines_ref, *refs):
        kv_refs = refs[:terms]
        (
            raw_ref, cos_ref, sin_ref, gk_ref, a_ref, w_ref, tok_ref, gpre_ref, dmid_ref, da_ref,
            dgq, dgpost, dgfpre, dgfpost, in_ref, *outs, held, grad, gains, blocks, windows, sems,
        ) = refs[terms:]
        q_copy = pltpu.make_async_copy(
            lines_ref.at[: flat.q_lines], held.at[: flat.q_lines], sems.at[0]
        )
        o_copy = pltpu.make_async_copy(
            lines_ref.at[flat.q_lines :], held.at[flat.q_lines :], sems.at[1]
        )
        q_copy.start()
        o_copy.start()
        d_kv = kv_refs[0][...].astype(f32)
        for ref in kv_refs[1:]:
            d_kv = d_kv + ref[...].astype(f32)
        unit, scale = normed(raw_ref[:, wide:])
        turned = rotate(d_kv[:, :HD], cos_ref[...], -sin_ref[...])
        dgk = jnp.sum(turned * unit, axis=0, keepdims=True)
        low = jnp.concatenate(
            [norm_back(unit, scale, turned * gk_ref[...]).astype(bf16), d_kv[:, HD:].astype(bf16)],
            axis=1,
        )
        grad[...] = contract(a_ref[...], low, 0, 0)
        d_a = da_ref[...] + contract(low, w_ref[:, wide:], 1, 1)
        unit, scale = normed(tok_ref[...].astype(f32))
        dgpre = jnp.sum(d_a * unit, axis=0, keepdims=True)
        in_ref[...] = (dmid_ref[...] + norm_back(unit, scale, d_a * gpre_ref[...])).astype(bf16)
        gains[...] = jnp.zeros_like(gains)
        at = 0
        for value in (dgpre, dgq[...], dgk, dgpost[...], dgfpre[...], dgfpost[...]):
            for i in range(value.shape[1] // LANES):
                gains[at : at + 1, :] = value[:, i * LANES : (i + 1) * LANES]
                at += 1
        q_copy.wait()
        for j in range(2 * HD // LANES):
            held[pl.ds(wide // LANES + j, D, stride=flat.q_across), :] = grad[
                :, j * LANES : (j + 1) * LANES
            ]
        o_copy.wait()
        for i in range(flat.devices):
            at = flat.gain_line(i)
            windows[i] = gains[at : at + 16, :].astype(bf16)
            if not straight:
                at = i * flat.lines
                blocks[i, : flat.gain_at, :] = held[at : at + flat.gain_at, :].astype(bf16)
        copies = []
        for k in range(flat.devices):
            device = order_ref[k]
            if straight:
                at = pl.multiple_of(device * flat.lines, 8)
                blocks[k, : flat.gain_at, :] = held[pl.ds(at, flat.gain_at), :].astype(bf16)
            source = blocks.at[k if straight else device]
            for part, low, high in ((source.at[: flat.gain_at], 0, flat.gain_at), (windows.at[device], flat.gain_at, flat.rows)):
                target = outs[k // each].at[k % each, low:high]
                copies.append(pltpu.make_async_copy(part, target, sems.at[2 + len(copies)]))
                copies[-1].start()
        for copy in copies:
            copy.wait()

    return run(
        "last_part",
        body,
        [order, lines, *kv_parts, raw, cosine, sine, g_k, a, w_qkv, tokens, g_pre, d_middle]
        + [da_query, *gain_grads],
        "sh" + "v" * (terms + 14),
        [((tok, D), bf16)] + [((each, flat.rows, LANES), bf16)] * groups,
        [
            pltpu.VMEM(lines.shape, f32),
            pltpu.VMEM((D, 2 * HD), f32),
            pltpu.VMEM((-(-(flat.gain_lines + 16) // 8) * 8, LANES), f32),
            pltpu.VMEM((flat.devices, flat.gain_at, LANES), bf16),
            pltpu.VMEM((flat.devices, 16, LANES), bf16),
            pltpu.SemaphoreType.DMA((2 + 2 * flat.devices,)),
        ],
        "v" + "h" * groups,
    )


class Ways:
    def __init__(self, sizes):
        self.sizes = sizes
        self.what = ""

    def size(self, axis):
        if isinstance(axis, str):
            return self.sizes[axis]
        n = 1
        for a in axis:
            n *= self.sizes[a]
        return n

    def fro(self, value, axis, offset):
        n = self.size(axis)
        if offset % n == 0:
            return value
        with jax.named_scope(self.what + "_" + "".join(axis) + str(offset)):
            return lax.ppermute(value, axis, [((i + offset) % n, i) for i in range(n)])

    def places(self):
        nx, ny = self.sizes["x"], self.sizes["y"]
        return [(ox, oy) for ox in range(nx) for oy in range(ny)]

    def outers(self):
        return [(ou, ov) for ou in range(self.sizes["u"]) for ov in range(self.sizes["v"])]

    def plane_gather(self, value, beside=(None, None)):
        early, late = beside
        nx, ny = self.sizes["x"], self.sizes["y"]
        half = halfway(value.shape[0])
        found = {(0, 0): value}
        for ox in range(1, nx):
            found[ox, 0] = self.fro(value, "x", ox)
        for oy in range(1, ny):
            found[0, oy] = self.fro(value, "y", oy)
        if early is not None:
            found, early = lax.optimization_barrier((found, early))
        halves = {}
        for ox in range(1, nx):
            for oy in range(1, ny):
                first = self.fro(found[ox, 0][:half], "y", oy)
                second = self.fro(found[0, oy][half:], "x", ox)
                halves[ox, oy] = [first, second]
        if late is not None:
            halves, late = lax.optimization_barrier((halves, late))
        found.update({at: jnp.concatenate(v, axis=0) for at, v in halves.items()})
        found = {at: [block, self.fro(block, "c", 1)] for at, block in found.items()}
        return found, (early, late)

    def plane_scatter(self, parts, first=None, second=None):
        nx, ny = self.sizes["x"], self.sizes["y"]
        low = {
            at: add_low(parts[at][0], self.fro(parts[at][1], "c", 1))
            for at in sorted(parts, reverse=True)
        }
        what = self.what
        if first is not None:
            last = max(low)
            low[last] = first(low[last])
            self.what = what
        half = halfway(low[0, 0].shape[0])
        along_x = {ox: [low[ox, 0][:half]] for ox in range(1, nx)}
        along_y = {oy: [low[0, oy][half:]] for oy in range(1, ny)}
        for ox in range(1, nx):
            for oy in range(1, ny):
                along_x[ox].append(self.fro(low[ox, oy][:half], "y", -oy))
                along_y[oy].append(self.fro(low[ox, oy][half:], "x", -ox))
        by_x = {
            ox: jnp.concatenate([add_low(*v), low[ox, 0][half:]], axis=0) for ox, v in along_x.items()
        }
        by_y = {
            oy: jnp.concatenate([low[0, oy][:half], add_low(*v)], axis=0) for oy, v in along_y.items()
        }
        if second is not None:
            by_x, by_y = second((by_x, by_y))
            self.what = what
        terms = [low[0, 0]]
        terms += [self.fro(v, "x", -ox) for ox, v in by_x.items()]
        terms += [self.fro(v, "y", -oy) for oy, v in by_y.items()]
        return terms

    def z_begin(self, value):
        n = self.sizes["z"]
        if n != 4:
            return ()
        return self.fro(value, "z", 1), self.fro(value, "z", -1)

    def z_end(self, value, begun, halves=None):
        n = self.sizes["z"]
        if n != 4:
            return [self.fro(value, "z", oz) for oz in range(n)]
        above, below = begun
        half = halfway(value.shape[0])
        first, second = self.fro(above[:half], "z", 1), self.fro(below[half:], "z", -1)
        return [value, above, jnp.concatenate([first, second], axis=0), below]

    def z_gather(self, value):
        return self.z_end(value, self.z_begin(value))

    def z_pair(self, one, other, begun_one, begun_other):
        if self.sizes["z"] != 4:
            return self.z_end(one, ()), self.z_end(other, ())
        far_one = self.fro(begun_one[0], "z", 1)
        far_other = self.fro(begun_other[1], "z", -1)
        return [one, begun_one[0], far_one, begun_one[1]], [
            other, begun_other[0], far_other, begun_other[1]
        ]

    def z_scatter_begin(self, far):
        if self.sizes["z"] != 4:
            return ()
        half = halfway(far.shape[0])
        return self.fro(far[:half], "z", -1), self.fro(far[half:], "z", 1)

    def z_scatter_go(self, parts, begun):
        n = self.sizes["z"]
        if n != 4:
            return [self.fro(parts[oz], "z", -oz) for oz in range(1, n)]
        half = halfway(parts[0].shape[0])
        above = jnp.concatenate([add_low(parts[1][:half], begun[0]), parts[1][half:]], axis=0)
        below = jnp.concatenate([parts[3][:half], add_low(parts[3][half:], begun[1])], axis=0)
        return [self.fro(above, "z", -1), self.fro(below, "z", 1)]

    def z_scatter(self, parts):
        return [parts[0], *self.z_scatter_go(parts, self.z_scatter_begin(parts[len(parts) // 2]))]


SEQ = ("u", "y", "c")
CTX = ("z", "v", "x")
ACROSS = ("v", "x")


def make_shards(sizes):
    ways = Ways(sizes)
    ns, nctx, nx = ways.size(SEQ), ways.size(CTX), ways.size(ACROSS)
    nz, nc = sizes["z"], sizes["c"]
    devices = ns * nctx
    places, outers = ways.places(), ways.outers()

    def from_outers(value):
        if len(outers) == 1:
            return value
        return jnp.concatenate(
            [ways.fro(ways.fro(value, "u", ou), "v", ov) for ou, ov in outers], axis=0
        )

    def to_outers(value):
        if len(outers) == 1:
            return value
        rows = value.shape[0] // len(outers)
        return add_low(
            *[
                ways.fro(ways.fro(value[i * rows : (i + 1) * rows], "u", -ou), "v", -ov)
                for i, (ou, ov) in enumerate(outers)
            ]
        )

    def plane_rows(value, *beside):
        found, beside = ways.plane_gather(value, beside or (None, None))
        return [block for p in places for block in found[p]], beside

    def by_device(parts):
        return {p: parts[i * nc : (i + 1) * nc] for i, p in enumerate(places)}

    def shards(
        tokens, cotangent, segments, positions, attn_w, attn_m, attn_v,
        mlp_w, mlp_m, mlp_v, gains, gain_m, gain_v,
    ):
        at = {a: lax.axis_index(a) for a in sizes}
        seq_place = lax.axis_index(SEQ)
        across_place = lax.axis_index(ACROSS)
        ctx_place = at["z"] * nx + across_place
        device = seq_place * nctx + ctx_place
        piece, gain_piece = attn_w.shape[0], gains.shape[0]
        flat = Flat(piece, gain_piece, devices)

        sides = [sizes[a] for a in ("x", "y", "c", "u", "v", "z")]
        here = [at[a] for a in ("x", "y", "c", "u", "v", "z")]
        ox, oy, oc, ou, ov, oz = (
            (jnp.asarray(o, jnp.int32) + h) % n
            for o, h, n in zip(np.unravel_index(np.arange(devices), sides), here, sides)
        )
        order = ((ou * sizes["y"] + oy) * sizes["c"] + oc) * nz + oz
        order = (order * sizes["v"] + ov) * sizes["x"] + ox

        ways.what = "attn_gather"
        gain_offset = gain_piece * device % LANES
        gain_window = lax.dynamic_update_slice(
            jnp.zeros((16 * LANES,), bf16), gains.astype(bf16), (gain_offset,)
        )
        low_piece = jnp.concatenate(
            [
                jnp.pad(
                    attn_w.astype(bf16).reshape(flat.lines, LANES),
                    ((0, flat.gain_at - flat.lines), (0, 0)),
                ),
                gain_window.reshape(16, LANES),
            ],
            axis=0,
        )
        ways.what = "unit_exchange"
        units, width = mlp_w.shape
        share = units // ns
        held = -(-share // 32) * 32

        def seq_send(by_place):
            return [ways.fro(v, SEQ, offset) for offset, v in enumerate(seq_parts(by_place))]

        def seq_parts(by_place):
            return [
                lax.dynamic_index_in_dim(by_place, (seq_place - offset) % ns, 0, keepdims=False)
                for offset in range(ns)
            ]

        def seq_place_all(heard):
            kept = jnp.zeros((ns,) + heard[0].shape, heard[0].dtype)
            for offset, value in enumerate(heard):
                kept = lax.dynamic_update_index_in_dim(kept, value, (seq_place + offset) % ns, 0)
            return kept

        sent = seq_parts(mlp_w.astype(bf16).reshape(ns, share, width))
        sent, low_piece = lax.optimization_barrier((sent, low_piece))
        heard = [ways.fro(v, SEQ, offset) for offset, v in enumerate(sent)]
        ways.what = "attn_gather"
        line_blocks = ways.z_gather(low_piece)
        line_blocks, heard = lax.optimization_barrier((line_blocks, heard))
        by_cols = seq_place_all(heard)
        rows_own = jnp.concatenate([by_cols[i] for i in range(ns)], axis=1)
        rows_own = jnp.pad(rows_own, ((0, held - share), (0, 0)))
        ways.what = "attn_gather"
        line_z, rows_own = lax.optimization_barrier(
            (from_outers(jnp.concatenate(line_blocks, axis=0)), rows_own)
        )
        def next_units(ring, *beside):
            if beside:
                ring[-1], *beside = lax.optimization_barrier((ring[-1],) + beside)
            what, ways.what = ways.what, "unit_gather"
            ring.append(ways.fro(ring[-1], "z", 1))
            ways.what = what
            return beside[0] if len(beside) == 1 else beside

        steps = nz == 4
        cut = halfway(held)
        whole = [rows_own]
        next_units(whole)
        gathered, _ = ways.plane_gather(line_z)
        line_parts = [part.reshape(-1, flat.rows, LANES) for p in places for part in gathered[p]]
        line_parts, whole[-1] = lax.optimization_barrier((line_parts, whole[-1]))
        rings = [[v[:cut] for v in whole], [v[cut:] for v in whole]]
        if steps:
            next_units(rings[0])
        else:
            for ring in rings:
                for _ in range(2, nz):
                    next_units(ring)

        tok_rows = tokens.shape[1]
        cosine, sine = angles(positions[0])
        (
            w_qkv, g_pre, g_q, g_k, g_post, g_fpre, g_fpost, normed_in, query, kv_local, raw,
        ) = first_part(flat, line_parts, order, tokens[0], cosine, sine)
        w_out = spread_out(flat, [after(part, kv_local) for part in line_parts], order)
        ways.what = "kv_gather"
        if steps:
            half = halfway(tok_rows)
            above, below = ways.z_begin(kv_local)
            above, below, rings[0][-1] = next_units(rings[1], above, below, rings[0][-1])
            far = ways.fro(above[:half], "z", 1), ways.fro(below[half:], "z", -1)
            far = next_units(rings[0], *far)
            kv_blocks = [kv_local, above, jnp.concatenate(far, axis=0), below]
        else:
            kv_blocks = ways.z_gather(kv_local)
        kv_all = jnp.stack([ways.fro(block, ACROSS, oa) for block in kv_blocks for oa in range(nx)])

        doc_all = segments[0]
        first_docs, last_docs = doc_all[::tok_rows], doc_all[tok_rows - 1 :: tok_rows]
        key_at = np.arange(nctx)
        key_place = (at["z"] + jnp.asarray(key_at // nx, jnp.int32)) % nz * nx
        key_place = key_place + (across_place + jnp.asarray(key_at % nx, jnp.int32)) % nx
        is_place = key_place[:, None] == jnp.arange(nctx, dtype=jnp.int32)[None, :]
        key_first = jnp.sum(jnp.where(is_place, first_docs[None, :], 0), axis=1)
        key_last = jnp.sum(jnp.where(is_place, last_docs[None, :], 0), axis=1)
        live = (key_place < ctx_place) & (key_last >= key_first[0])
        one_doc = key_first == key_last[0]
        task = jnp.where(live, jnp.where(one_doc, WHOLE, MASKED), DEAD)
        task = jnp.where(key_place == ctx_place, MASKED, task)
        info = jnp.stack([key_place, task]).astype(jnp.int32)
        key_docs = doc_all[:, None]
        query_docs = lax.dynamic_slice_in_dim(doc_all, ctx_place * tok_rows, tok_rows)[None]

        heads, log_total, attn_out, middle, ffn_in = attend(
            info, query, kv_all, key_docs, query_docs, w_out, tokens[0], g_post, g_fpre
        )

        ways.what = "ffn_in_gather"
        if steps:
            ffn_in = next_units(rings[1], ffn_in)
            ffn_rows, (rings[0][-1], rings[1][-1]) = plane_rows(ffn_in, rings[0][-1], rings[1][-1])
        else:
            ffn_rows, _ = plane_rows(ffn_in)
        units_here = [from_outers(block) for block in whole[:nz]]
        units_here += [from_outers(block) for pair in zip(rings[0][2:], rings[1][2:]) for block in pair]
        act, gelu, slope, parts = ffn_forward(ffn_rows, units_here)
        ways.what = "ffn_out_sum"
        out_parts = ways.plane_scatter(by_device(parts))
        mixed, d_mlp_out, d_gfpost = after_ffn(out_parts, middle, cotangent[0], g_fpost)

        ways.what = "d_out_gather"
        d_out_rows, _ = plane_rows(d_mlp_out)
        per = units_here[0].shape[0]

        def z_step(blocks, far, *earlier):
            value = blocks[far] if not earlier else add_low(blocks[far], *earlier)
            return ways.fro(value, "z", -1)

        class Ring:
            def __init__(self, name, blocks):
                self.name, self.blocks, self.at, self.heard = name, [to_outers(b) for b in blocks], nz, None

            def step(self, beside=None):
                if not steps:
                    return beside
                if self.heard is not None and beside is not None:
                    self.heard, beside = lax.optimization_barrier((self.heard, beside))
                self.at -= 1
                if self.at > 0:
                    value = self.blocks[self.at]
                    if self.heard is not None:
                        value = add_low(value, self.heard)
                    what, ways.what = ways.what, self.name
                    self.heard = ways.fro(value, "z", -1)
                    ways.what = what
                return beside

            def settle(self, beside):
                if steps:
                    self.heard, beside = lax.optimization_barrier((self.heard, beside))
                return beside

            def result(self):
                if steps:
                    return add_low(self.blocks[0], self.heard)
                return add_low(*[ways.fro(v, "z", -i) for i, v in enumerate(self.blocks)])

        down = Ring("down_grad_sum", unit_grads(act, 0, nz, per, d_out_rows))
        down.step()
        d_out_rows[0] = after(d_out_rows[0], down.blocks[0])
        d_both, parts = ffn_backward(d_out_rows, gelu, slope, units_here)
        parts[-1] = down.step(parts[-1])
        rings = {}

        def gate_then(low):
            low, both = lax.optimization_barrier((low, d_both))
            rings["gate"] = Ring("gate_grad_sum", unit_grads(both, 0, nz, per, ffn_rows))
            rings["gate"].step()
            return low

        def up_then(summed):
            summed = down.step(summed)
            summed, both = lax.optimization_barrier((summed, d_both))
            rings["up"] = Ring("up_grad_sum", unit_grads(both, 1, nz, per, ffn_rows))
            rings["up"].step()
            return summed

        ways.what = "d_in_sum"
        d_in_parts = ways.plane_scatter(by_device(parts), gate_then, up_then)
        d_in_parts = lax.optimization_barrier((d_in_parts, rings["up"].blocks[0]))[0]
        d_in_parts = rings["gate"].step(d_in_parts)

        d_query, d_attn_out, d_middle, d_gfpre, d_gpost, *d_kv = attend_back(
            info, query, kv_all, key_docs, query_docs, heads, log_total, d_in_parts, middle, attn_out,
            cotangent[0], w_out, g_post, g_fpre,
        )
        d_kv = down.step(rings["up"].settle(d_kv))
        ways.what = "kv_sum"

        def across(oz):
            return [ways.fro(d_kv[oz * nx + oa], ACROSS, -oa) for oa in range(nx)]

        far = nz // 2
        kv_parts = {far: add_low(*across(far))}
        near = {oz: across(oz) for oz in range(nz) if oz != far}
        begun = ways.z_scatter_begin(kv_parts[far])
        near, begun = lax.optimization_barrier((near, begun))
        kv_parts.update({oz: add_low(*terms) for oz, terms in near.items()})
        kv_parts = [kv_parts[0], *ways.z_scatter_go(kv_parts, begun)]
        lines, da_query, d_gq = query_side(
            flat, after(d_query, *near[0]), raw, cosine, sine, g_q, normed_in, w_qkv, heads, d_attn_out
        )
        da_query = rings["up"].step(rings["gate"].step(da_query))
        input_grad, *packed = last_part(
            flat, order, len(places) * nc, lines, kv_parts, raw, cosine, sine, g_k, normed_in, w_qkv, tokens[0],
            g_pre, d_middle, da_query, [d_gq, d_gpost, d_gfpre, d_gfpost],
        )

        ways.what = "attn_grad_sum"
        packed = [part.reshape(-1, LANES) for part in packed]
        terms = ways.plane_scatter(
            {p: packed[i * nc : (i + 1) * nc] for i, p in enumerate(places)}, rings["up"].step
        )
        owned = [rings["gate"].result(), rings["up"].result(), down.result()]
        own_rows = jnp.concatenate([v[:share] for v in owned], axis=1)
        by_cols = jnp.stack([own_rows[:, i * width : (i + 1) * width] for i in range(ns)])
        terms, by_cols = lax.optimization_barrier((terms, by_cols))
        plane_sum = to_outers(add_low(*terms))

        ways.what = "grad_exchange"
        mlp_red = seq_place_all(seq_send(by_cols)).astype(f32).reshape(units, width)
        mlp_m_new, mlp_v_new, mlp_new = adam_update(
            mlp_w, mlp_m, mlp_v, mlp_red, RATE_MATRIX, DECAY_MATRIX
        )

        ways.what = "attn_grad_sum"
        terms = ways.z_scatter([plane_sum[oz * flat.rows : (oz + 1) * flat.rows] for oz in range(nz)])
        terms, mlp_new = lax.optimization_barrier((terms, mlp_new))
        red = sum(part.astype(f32) for part in terms)
        attn_red = red[: flat.lines].reshape(-1)
        gain_red = lax.dynamic_slice(red[flat.gain_at :].reshape(-1), (gain_offset,), (gain_piece,))

        attn_m_new, attn_v_new, attn_new = adam_update(
            attn_w, attn_m, attn_v, attn_red, RATE_MATRIX, DECAY_MATRIX
        )
        gain_m_new, gain_v_new, gain_new = adam_update(
            gains, gain_m, gain_v, gain_red, RATE_GAIN, 0.0
        )
        return (
            mixed[None], input_grad[None],
            attn_red, attn_m_new, attn_v_new, attn_new,
            mlp_red, mlp_m_new, mlp_v_new, mlp_new,
            gain_red, gain_m_new, gain_v_new, gain_new,
        )

    return shards


def solution(mesh):
    seq, ctx = mesh.shape["seq"], mesh.shape["ctx"]
    nz = 4 if ctx % 4 == 0 else 1
    chips_y, chips_x = seq // 2, ctx // nz
    y, x = 2 - chips_y % 2, 2 - chips_x % 2
    sizes = {"u": chips_y // y, "y": y, "c": 2, "z": nz, "v": chips_x // x, "x": x}
    fine = Mesh(mesh.devices.reshape(*sizes.values()), tuple(sizes))
    s, x = SEQ, CTX
    both = s + x
    in_specs = (
        P(s, x, None), P(s, x, None), P(s, None), P(s, x),
        P(both), P(both), P(both),
        P(x, s), P(x, s), P(x, s),
        P(both), P(both), P(both),
    )
    out_specs = (
        P(s, x, None), P(s, x, None),
        P(both), P(both), P(both), P(both),
        P(x, s), P(x, s), P(x, s), P(x, s),
        P(both), P(both), P(both), P(both),
    )
    return jax.shard_map(
        make_shards(sizes), mesh=fine, in_specs=in_specs, out_specs=out_specs, check_vma=False
    )
```
